512 devices in a mesh: sec: 4 (over x), dom: 128 (over y, z, core).
Axes of the slice: x: 4, y: 4, z: 16, core: 2. Of those that a mesh axis runs over, the one named last changes fastest.
Arguments:
- state: float32 [4, 30, 4096, 128], P('sec', None, 'dom'), may hold values from -6 to 6
- surface_frac: float32 [4, 4096, 128], P('sec', 'dom'), may hold values from 0.2 to 1
- diffusivity: float32 [4, 30], P('sec'), may hold values from 0.05 to 0.24
- column_ops: float32 [4, 30, 30], P('sec'), may hold values from -1 to 1
- remap_weights: float32 [4, 1024, 128, 128], P('sec', 'dom'), may hold values from -0.5 to 0.5
- flux_owner: int32 [4, 4096, 1], P('sec', 'dom'), may hold values from 0 to 127; in each aligned block of 32 rows (0 to 31, 32 to 63, ..., all dimensions but the last counted through in order) at most 2 rows name the same one
- flux_row: int32 [4, 4096], P('sec', 'dom'), may hold values from 0 to 31
- flux_block: int32 [4, 4096], P('sec', 'dom'), may hold values from 0 to 7
- runoff_owner: int32 [4, 4096, 1], P('sec', 'dom'), may hold values from 0 to 127; in each aligned block of 32 rows (0 to 31, 32 to 63, ..., all dimensions but the last counted through in order) at most 2 rows name the same one
- runoff_row: int32 [4, 4096], P('sec', 'dom'), may hold values from 0 to 31
- runoff_block: int32 [4, 4096], P('sec', 'dom'), may hold values from 0 to 7
- river_store: float32 [4, 4096, 128], P('sec', 'dom'), may hold values from -6 to 6
Outputs:
- state_out: float32 [4, 30, 4096, 128], P('sec', None, 'dom')
- river_out: float32 [4, 4096, 128], P('sec', 'dom')
The draws below stay inside these ranges and needn't reach their ends.
Inputs may be any that keep to these rules, and one draw needn't show every extreme that they name: `flux_owner`: among the 32 rows of one device no owner is named by more than 2 rows, a bound that some block reaches. `runoff_owner`: among the 32 rows of one device no owner is named by more than 2 rows, a bound that some block reaches.
All inputs are finite; a program needn't handle non-finite values.
Results may differ from the reference program's by a relative error of at most 0.0003.
Values sent between devices are 32-bit elements; how exact they have to be, the bound alone decides.
A program may use at most 64 MiB of HBM per device.

```python
import math
import jax
import jax.numpy as jnp
import numpy as np
from jax import lax

LEV = 30
COLS = 128
ROWS = 32
FIELDS = 4
NW = 8
STEPS = 2
CAP = 2
GRID_ROWS = 4096
WEIGHT_ROWS = 1024
N_SEC = 4
N_DOM = 128


def draw_column_ops(key, part):
    key = jax.random.fold_in(key, 11)
    noise = jax.random.uniform(key, (N_SEC, LEV, LEV), jnp.float32, -1.0, 1.0)
    identity = jnp.eye(LEV, dtype=jnp.float32)[None]
    return 0.7 * identity + noise * (0.5 / math.sqrt(LEV))


def set_ends(array, stream_key, low, largest):
    longest = array.shape.index(max(array.shape))
    spots = []
    for shift in (0, 1):
        where = [jax.random.randint(jax.random.fold_in(stream_key, axis), (), 0, length) for axis, length in enumerate(array.shape)]
        where[longest] = (where[longest] + shift) % array.shape[longest]
        spots.append(tuple(where))
    return array.at[spots[0]].set(low).at[spots[1]].set(largest)


def shard_levels(rng, dims, cuts, least, top_value):
    gain, own = 1.0, jax.random.fold_in(rng, 6)
    for dim, parts in cuts:
        heights = jnp.exp(jax.random.uniform(jax.random.fold_in(own, dim), (parts,), jnp.float32, least / len(cuts), top_value / len(cuts)))
        gain = gain * jnp.repeat(heights, dims[dim] // parts).reshape([-1 if axis == dim else 1 for axis in range(len(dims))])
    return gain


def shared_out(own_key, own, number, rows, number_of, top, most, lean):
    order = jax.random.permutation(own_key, number_of)
    crowded, usual = load_shares(number_of, rows * top, most, lean, True), load_shares(number_of, rows * top, most, lean, False)
    places = jnp.arange(number_of)

    def named(sizes, turn):
        used = int((sizes > 0).sum())
        fixed = max(1, used // 4)
        moved = fixed + (places - fixed + turn * (used - fixed)) % max(1, number_of - fixed)
        return jnp.zeros((number_of,), jnp.int32).at[order[jnp.where(places < fixed, places, moved)]].set(jnp.asarray(sizes, jnp.int32))

    sizes = jnp.where(number % 4 == 0, named(crowded, number // 4), named(usual, number - number // 4 - 1))
    mixed = jax.random.permutation(jax.random.fold_in(own, 3), number_of)
    giver, receiver = mixed[0:number_of // 2 * 2:2], mixed[1:number_of // 2 * 2:2]
    margin = jnp.minimum(sizes[giver] - 1, most - sizes[receiver]) // 2
    margin = jnp.where((giver == order[0]) | (receiver == order[0]) | (sizes[receiver] == 0), 0, jnp.maximum(margin, 0))
    moved = jax.random.randint(jax.random.fold_in(own, 4), (number_of // 2,), 0, 1 << 20) % (margin + 1)
    sizes = sizes.at[giver].add(-moved).at[receiver].add(moved)
    items = jnp.searchsorted(jnp.cumsum(sizes), jnp.arange(rows * top), side="right").astype(jnp.int32)
    table = items.reshape(top, rows).T
    table = table[jax.random.permutation(jax.random.fold_in(own, 1), rows)]
    turn = jax.random.randint(jax.random.fold_in(own, 2), (rows, 1), 0, top)
    return jnp.take_along_axis(table, (jnp.arange(top)[None, :] + turn) % top, axis=1)


def load_shares(number_of, total, most, skew, full):
    weights = [(1 << 20) // math.isqrt(rank ** skew) + 1 for rank in range(1, number_of + 1)]
    largest = most if full else min(most, max(-(-total // number_of), total * weights[0] // sum(weights)))
    least = 1 if total - largest >= number_of - 1 else 0
    counts, surplus = [largest] + [least] * (number_of - 1), total - largest - least * (number_of - 1)
    while surplus > 0:
        free = [i for i in range(1, number_of) if counts[i] < largest] or [i for i in range(1, number_of) if counts[i] < most]
        whole, budget = sum([weights[i] for i in free]), surplus
        for i in free:
            extra = min(most - counts[i], max(1, budget * weights[i] // whole), surplus)
            counts[i] = counts[i] + extra
            surplus = surplus - extra
    return np.array(counts)


def scatter_about(stream_key, extent, spread, bound, cuts=(), held_as=jnp.bfloat16):
    loudness = shard_levels(stream_key, extent, cuts, -0.22, 0.18) if cuts else 1.0
    result = jax.random.normal(stream_key, extent, jnp.float32) * spread * loudness
    return jnp.minimum(jnp.maximum(result, -bound), bound).astype(held_as)


def setup_inputs(seed: int = 0) -> dict:
    key_of = jax.random.split(jax.random.key(seed), 13)
    state = scatter_about(key_of[0], (N_SEC, LEV, GRID_ROWS, COLS), 1.0, 6.0, ((0, 4), (2, 128)), jnp.float32)
    surface_frac = jnp.clip(0.2 + 0.8 * jax.random.uniform(key_of[1], (N_SEC, GRID_ROWS, COLS), jnp.float32) ** shard_levels(key_of[1], (N_SEC, GRID_ROWS, COLS), ((0, 4), (1, 128)), -0.2, 0.2), 0.2, 1.0)
    diffusivity = jnp.clip(0.05 + 0.19 * jax.random.uniform(key_of[2], (N_SEC, LEV), jnp.float32) ** shard_levels(key_of[2], (N_SEC, LEV), ((0, 4),), -0.2, 0.2), 0.05, 0.24)
    column_ops = draw_column_ops(jax.random.fold_in(key_of[12], 71), 0)
    remap_weights = scatter_about(key_of[4], (N_SEC, WEIGHT_ROWS, COLS, COLS), COLS ** -0.5, 0.5, ((0, 4), (1, 128)), jnp.float32)
    flux_owner_keys = jax.random.split(jax.random.fold_in(key_of[5], 1), N_SEC * GRID_ROWS // ROWS)
    flux_owner_turns = jax.random.permutation(jax.random.fold_in(key_of[5], 3), N_SEC * GRID_ROWS // ROWS)
    flux_owner = jax.vmap(lambda own, number: shared_out(jax.random.fold_in(key_of[5], 2), own, number, ROWS, N_DOM, 1, CAP, 1))(flux_owner_keys, flux_owner_turns).reshape((N_SEC, GRID_ROWS, 1))
    flux_row = set_ends(jax.random.randint(key_of[6], (N_SEC, GRID_ROWS), 0, ROWS), jax.random.fold_in(key_of[6], 1), 0, ROWS - 1).astype(jnp.int32)
    flux_block = set_ends(jax.random.randint(key_of[7], (N_SEC, GRID_ROWS), 0, NW), jax.random.fold_in(key_of[7], 1), 0, NW - 1).astype(jnp.int32)
    runoff_owner_keys = jax.random.split(jax.random.fold_in(key_of[8], 1), N_SEC * GRID_ROWS // ROWS)
    runoff_owner_turns = jax.random.permutation(jax.random.fold_in(key_of[8], 3), N_SEC * GRID_ROWS // ROWS)
    runoff_owner = jax.vmap(lambda own, number: shared_out(jax.random.fold_in(key_of[8], 2), own, number, ROWS, N_DOM, 1, CAP, 1))(runoff_owner_keys, runoff_owner_turns).reshape((N_SEC, GRID_ROWS, 1))
    runoff_row = set_ends(jax.random.randint(key_of[9], (N_SEC, GRID_ROWS), 0, ROWS), jax.random.fold_in(key_of[9], 1), 0, ROWS - 1).astype(jnp.int32)
    runoff_block = set_ends(jax.random.randint(key_of[10], (N_SEC, GRID_ROWS), 0, NW), jax.random.fold_in(key_of[10], 1), 0, NW - 1).astype(jnp.int32)
    river_store = scatter_about(key_of[11], (N_SEC, GRID_ROWS, COLS), 1.0, 6.0, ((0, 4), (1, 128)), jnp.float32)
    return dict(state=state, surface_frac=surface_frac, diffusivity=diffusivity, column_ops=column_ops, remap_weights=remap_weights, flux_owner=flux_owner, flux_row=flux_row, flux_block=flux_block, runoff_owner=runoff_owner, runoff_row=runoff_row, runoff_block=runoff_block, river_store=river_store)


HIGHEST_PRECISION = lax.Precision.HIGHEST


def advance(pieces):
    field, fraction, coefficients, operator, forcing = pieces
    for step_number in range(STEPS):
        padded = jnp.pad(field, ((0, 0), (1, 1), (0, 0)))
        laplacian = padded[:, 2:] + padded[:, :-2] + jnp.roll(field, 1, 2) + jnp.roll(field, -1, 2) - 4.0 * field
        updated = field + coefficients[:, None, None] * laplacian
        updated = updated.at[:FIELDS].add(fraction[None] * forcing)
        field = jnp.einsum("kl,lrc->krc", operator, updated, precision=HIGHEST_PRECISION)
    return field


def reference(state, surface_frac, diffusivity, column_ops, remap_weights, flux_owner, flux_row, flux_block, runoff_owner, runoff_row, runoff_block, river_store):
    sections = state.shape[0]
    total_rows = N_DOM * ROWS

    def device_terms(device_index):
        section = device_index // N_DOM
        owner_index = device_index % N_DOM
        row_start = owner_index * ROWS
        anchor = jnp.zeros((), jnp.int32)
        surface = lax.dynamic_slice(state, (section, anchor, row_start, anchor), (1, FIELDS, ROWS, COLS))[0]
        weight_table = lax.dynamic_slice(remap_weights, (section, owner_index * NW, anchor, anchor), (1, NW, COLS, COLS))[0]
        flux_index = lax.dynamic_slice(flux_block, (section, row_start), (1, ROWS))[0]
        runoff_index = lax.dynamic_slice(runoff_block, (section, row_start), (1, ROWS))[0]
        flux_terms = jnp.einsum("frc,rcd->rfd", surface, weight_table[flux_index], precision=HIGHEST_PRECISION)
        runoff_terms = jnp.einsum("rc,rcd->rd", surface[0], weight_table[runoff_index], precision=HIGHEST_PRECISION)
        return flux_terms, runoff_terms

    flux_terms, runoff_terms = lax.map(device_terms, jnp.arange(sections * N_DOM, dtype=jnp.int32))
    flux_terms = flux_terms.reshape(sections, total_rows, FIELDS, COLS)
    runoff_terms = runoff_terms.reshape(sections, total_rows, COLS)
    section_ids = jnp.arange(sections, dtype=jnp.int32)
    partner = jnp.broadcast_to(((section_ids + 2) % sections)[:, None], (sections, total_rows))
    own_section = jnp.broadcast_to(section_ids[:, None], (sections, total_rows))
    flux_target = flux_owner[..., 0] * ROWS + flux_row
    runoff_target = runoff_owner[..., 0] * ROWS + runoff_row
    imported = jnp.zeros((sections, total_rows, FIELDS, COLS), jnp.float32).at[partner, flux_target].add(flux_terms)
    imported = jnp.transpose(imported, (0, 2, 1, 3))
    river_in = jnp.zeros((sections, total_rows, COLS), jnp.float32).at[own_section, runoff_target].add(runoff_terms)
    state_out = lax.map(advance, (state, surface_frac, diffusivity, column_ops, imported))
    return state_out, river_store + river_in
```

```python
import jax
import jax.numpy as jnp
from jax import lax
from jax.experimental import pallas as pl
from jax.experimental.pallas import tpu as pltpu
from jax.sharding import PartitionSpec as P

MESH = pl.DeviceIdType.MESH
F32 = jnp.float32
BF16 = jnp.bfloat16

LEV = 30
PAD = 32
COLS = 128
ROWS = 32
FIELDS = 4
NW = 8
NY, NZ, NC = 4, 16, 2
N_DOM = NY * NZ * NC
GROUP = NY * NC
HALF = NZ // 2
SLOTS = NZ
GROUPS = ROWS // 8
MAIN = GROUP * ROWS
EDGE = GROUP * 2
LABELS = ROWS
FLUX = LABELS + 8
SLOT = FLUX + 2 * NC * ROWS
PARTS = [(0, FLUX)] + [(FLUX + i * ROWS, ROWS) for i in range(2 * NC)]
BLOCK = 2 * ROWS + 8


def tree(count, double):
    levels, reached, level = {}, 0, 1
    while reached < count:
        step = 2 if level in double and reached + 2 <= count else 1
        levels[level] = [(reached, reached + i) for i in range(step, 0, -1)]
        reached, level = reached + step, level + 1
    return levels


LONG, SHORT = tree(HALF, (1, 3, 5)), tree(HALF - 1, (2, 4))
LEVELS = len(LONG)


def split(x):
    high = x.astype(BF16)
    return high, (x - high.astype(F32)).astype(BF16)


def mm(a, b):
    return jnp.dot(a, b, preferred_element_type=F32)


def mm3(a, b):
    (ah, al), (bh, bl) = a, b
    return mm(ah, bh) + (mm(ah, bl) + mm(al, bh))


def iota(shape, dim):
    return lax.broadcasted_iota(jnp.int32, shape, dim)


def neighbours_in_columns(x):
    axis = x.ndim - 1
    return pltpu.roll(x, 1, axis) + pltpu.roll(x, COLS - 1, axis)


def laplacian(x, above, below):
    row, count = iota(x.shape, 1), x.shape[1]
    down = jnp.where(row == 0, above, pltpu.roll(x, 1, 1))
    up = jnp.where(row == count - 1, below, pltpu.roll(x, count - 1, 1))
    return down + up + neighbours_in_columns(x) - 4.0 * x


def kernel(
    state_h, frac_h, diff_h, ops_h, weight_h, fo_h, fr_h, fb_h, ro_h, rr_h, rb_h, store_h,
    base2, kab, forced, river,
    st, frac, diff, ops, weight, fo, fr, fb, ro, rr, rb, store,
    local_sem,
    hs_up, hs_dn, hr_up, hr_dn, halo_ssem, halo_rsem,
    terms, label_out, label_in, part_ssem, part_rsem,
    ring, ring_ssem, ring_rsem, row_of, ends_acc,
    flux_send, flux_recv, run_send, run_recv, rs_ssem, rs_rsem,
    dcol, kron_h, kron_l, base1,
):
    sec = lax.axis_index("sec")
    me = lax.axis_index("dom")
    core = me & (NC - 1)
    z = (me >> 1) & (NZ - 1)
    y = me >> 5

    def dom_of(yy, zz, cc):
        return (yy * NZ + zz) * NC + cc

    def along(distance):
        return (sec, dom_of(y, (z + NZ + distance) & (NZ - 1), core))

    partners = [(sec ^ 2, me), (sec ^ 2, me ^ 1)]
    after = (sec, (me + 1) & (N_DOM - 1))
    before = (sec, (me + N_DOM - 1) & (N_DOM - 1))

    def member(b):
        return (sec, dom_of((y + b // NC) & (NY - 1), z, core ^ (b % NC)))

    pairs = [(weight_h.at[0], weight)]
    pairs += [
        (state_h.at[0, :, pl.ds(8 * i, 8)], st.at[1 + i, pl.ds(0, LEV)]) for i in range(GROUPS)
    ]
    pairs += [
        (fb_h, fb), (rb_h, rb), (fo_h, fo), (fr_h, fr), (ro_h, ro), (rr_h, rr),
        (frac_h.at[0], frac), (ops_h, ops), (diff_h, diff), (store_h.at[0], store),
    ]
    loads = [pltpu.make_async_copy(a, b, local_sem.at[i]) for i, (a, b) in enumerate(pairs)]
    for copy in loads:
        copy.start()

    barrier = pltpu.get_barrier_semaphore()
    peers = [along(d) for d in (1, -1, 2, -2)] + [*partners, after, before] + [member(b) for b in range(1, GROUP)]
    for peer in peers:
        pl.semaphore_signal(barrier, inc=1, device_id=peer, device_id_type=MESH)

    for copy in loads[5:11]:
        copy.wait()

    def label_of(owner, row):
        eye = iota((ROWS, ROWS), 0) == iota((ROWS, ROWS), 1)
        target = (owner[...] * ROWS + row[...]).astype(F32)
        rows = jnp.broadcast_to(target, (ROWS, ROWS))
        column = jnp.sum(jnp.where(eye, rows, 0.0), axis=1, keepdims=True)
        wide = jnp.broadcast_to(column, (ROWS, COLS))
        place = iota((ROWS, COLS), 0) == (iota((ROWS, COLS), 1) & (ROWS - 1))
        return jnp.sum(jnp.where(place, wide, 0.0), axis=0, keepdims=True)

    label_out[...] = jnp.broadcast_to(label_of(fo, fr), (8, COLS))
    ring[0, LABELS:FLUX, :] = jnp.broadcast_to(label_of(ro, rr), (8, COLS))

    tall = FIELDS * ROWS + ROWS
    spot = (iota((tall, ROWS), 0) & (ROWS - 1)) == iota((tall, ROWS), 1)
    blocks = jnp.where(
        iota((tall, ROWS), 0) < FIELDS * ROWS,
        jnp.broadcast_to(fb[...].astype(F32), (tall, ROWS)),
        jnp.broadcast_to(rb[...].astype(F32), (tall, ROWS)),
    )
    block = jnp.sum(jnp.where(spot, blocks, 0.0), axis=1, keepdims=True)
    block = jnp.broadcast_to(jnp.concatenate([block, block], axis=0), (2 * tall, COLS))
    for copy in loads[1:5]:
        copy.wait()
    surface = jnp.concatenate(
        [st[1 + i, f] for f in (*range(FIELDS), 0) for i in range(GROUPS)], axis=0
    )
    high = surface.astype(BF16).astype(F32)
    both = jnp.concatenate([high, surface - high], axis=0)
    lhs = jnp.concatenate(
        [jnp.where(block == float(w), both, 0.0).astype(BF16) for w in range(NW)], axis=1
    )
    loads[0].wait()
    rhs = jnp.concatenate(split(weight[...].reshape(NW * COLS, COLS)), axis=1)
    total = mm(lhs, rhs)
    result = total[:tall, :COLS] + (total[:tall, COLS:] + total[tall:, :COLS])
    terms[...] = result[: FIELDS * ROWS].reshape(FIELDS, ROWS, COLS)
    ring[0, :LABELS, :] = result[FIELDS * ROWS :]

    pl.semaphore_wait(barrier, len(peers))

    def remote(src, dst, ssem, rsem, device):
        return pltpu.make_async_remote_copy(
            src_ref=src, dst_ref=dst, send_sem=ssem, recv_sem=rsem,
            device_id=device, device_id_type=MESH,
        )

    def slot_of(way, distance):
        return 0 if distance == 0 else min(2 * distance - (way > 0), SLOTS - 1)

    def hop(c, way, start, end):
        slot, rows = slot_of(way, end), pl.ds(*PARTS[c])
        return remote(
            ring.at[slot_of(way, start), rows], ring.at[slot, rows],
            ring_ssem.at[c, slot], ring_rsem.at[c, slot], along(way * (end - start)),
        )

    arrivals, departures = {}, {}
    for c in range(len(PARTS)):
        for way in (1, -1):
            levels = LONG if (c % 2 == 0) == (way > 0) else SHORT
            for level, edges in levels.items():
                copies = [hop(c, way, *edge) for edge in edges]
                departures[c, way, level] = (slot_of(way, edges[0][0]), copies)
                for copy, (_, end) in zip(copies, edges):
                    arrivals[c, slot_of(way, end)] = copy
    sends = list(arrivals.values())

    def arrive(c, slots):
        for slot in slots:
            if (c, slot) in arrivals:
                arrivals.pop((c, slot)).wait_recv()

    def depart(c, level):
        for way in (1, -1):
            if (c, way, level) in departures:
                slot, copies = departures.pop((c, way, level))
                arrive(c, [slot])
                for copy in copies:
                    copy.start()

    label_swap = [
        remote(label_out, label_in.at[i], part_ssem.at[i], part_rsem.at[i], to)
        for i, to in enumerate(partners)
    ]
    swap = []
    for c in range(1, len(PARTS)):
        i, f = (c - 1) // 2, (c - 1) % 2
        source = terms.at[2 * (core ^ i) + f]
        swap.append(
            remote(
                source, ring.at[0, pl.ds(*PARTS[c])],
                part_ssem.at[1 + c], part_rsem.at[1 + c], partners[i],
            )
        )
    for copy in (*label_swap, *swap):
        copy.start()

    loads[11].wait()
    hs_up[0:LEV] = st[1, 0:LEV, 0:2, :]
    hs_dn[0:LEV] = st[GROUPS, 0:LEV, 6:8, :]
    hs_up[LEV] = frac[0:2, :]
    hs_dn[LEV] = frac[ROWS - 2 : ROWS, :]
    hs_up[LEV + 1] = jnp.zeros((2, COLS), F32)
    hs_dn[LEV + 1] = jnp.zeros((2, COLS), F32)
    for i in range(GROUPS):
        st[1 + i, LEV:PAD] = jnp.zeros((PAD - LEV, 8, COLS), F32)
    halo = [
        remote(hs_dn, hr_up, halo_ssem.at[0], halo_rsem.at[0], after),
        remote(hs_up, hr_dn, halo_ssem.at[1], halo_rsem.at[1], before),
    ]
    for copy in halo:
        copy.start()

    tall8 = PAD * 8
    for copy in loads[12:14]:
        copy.wait()
    pick = ((iota((tall8, LEV), 0) >> 3) == iota((tall8, LEV), 1)).astype(F32)
    pick_t = ((iota((LEV, tall8), 1) >> 3) == iota((LEV, tall8), 0)).astype(BF16)
    column = jnp.sum(pick * jnp.broadcast_to(diff[...], (tall8, LEV)), axis=1, keepdims=True)
    dcol[...] = jnp.broadcast_to(column, (tall8, COLS))
    op = ops[:, 0, :]
    op_h, op_l = split(op)
    op_r = (op - op_h.astype(F32) - op_l.astype(F32)).astype(BF16)
    pick = pick.astype(BF16)
    spread = mm(mm(pick, op_h).astype(BF16), pick_t) + (
        mm(mm(pick, op_l).astype(BF16), pick_t) + mm(mm(pick, op_r).astype(BF16), pick_t)
    )
    same8 = (iota((tall8, tall8), 0) & 7) == (iota((tall8, tall8), 1) & 7)
    kh, kl = split(jnp.where(same8, spread, 0.0))
    kron_h[...] = kh
    kron_l[...] = kl

    def kab_work():
        k4 = kron_h[:, : 8 * FIELDS].astype(F32) + kron_l[:, : 8 * FIELDS].astype(F32)
        eye = (iota(k4.shape, 0) == iota(k4.shape, 1)).astype(F32)
        q = jnp.concatenate([k4 + eye, dcol[:, : 8 * FIELDS] * k4], axis=1)
        kh, kl = split(mm3((kron_h[...], kron_l[...]), split(q)))
        kab[...] = jnp.concatenate([kh, kh, kl], axis=1)

    def block_start(b):
        return dom_of((y + (b >> 1)) & (NY - 1), z, core ^ (b & 1)) * ROWS

    i = iota((MAIN, COLS), 0)
    row_of[:MAIN] = (block_start(i >> 5) + (i & (ROWS - 1))).astype(F32)
    i = iota((EDGE, COLS), 0)
    row_of[MAIN:] = (block_start(i >> 1) + jnp.where((i & 1) == 0, -1, ROWS)).astype(F32)
    flux_send[...] = jnp.zeros(flux_send.shape, F32)
    run_send[...] = jnp.zeros(run_send.shape, F32)

    first = me == 0
    last = me == N_DOM - 1

    def apply(*groups):
        u = jnp.concatenate([u.reshape(PAD * 8, COLS) for u in groups], axis=1)
        out = mm3((kron_h[...], kron_l[...]), split(u))
        return [
            out[:, COLS * i : COLS * (i + 1)].reshape(PAD, 8, COLS) for i in range(len(groups))
        ]

    def diffused(i, source):
        x = source[i]
        lap = laplacian(x, source[i - 1, :, 7:8], source[i + 1, :, 0:1])
        return x + dcol[...].reshape(PAD, 8, COLS) * lap

    def step_one(i, j):
        base1[i], base1[j] = apply(diffused(i, st), diffused(j, st))

    def step_two(i, j):
        base2[i - 1], base2[j - 1] = apply(diffused(i, base1), diffused(j, base1))

    def step_one_ends():
        d = dcol[...].reshape(PAD, 8, COLS)
        spot = iota((PAD, 8, COLS), 1)
        above, below = st[0], st[GROUPS + 1]
        x = jnp.where(spot == 7, above[:, 7:8], below[:, 0:1])
        outer = jnp.where(spot == 7, above[:, 6:7], below[:, 1:2])
        inner = jnp.where(spot == 7, st[1, :, 0:1], st[GROUPS, :, 7:8])
        u = x + d * (outer + inner + neighbours_in_columns(x) - 4.0 * x)
        gone = ((spot == 7) & first) | ((spot < 7) & last)
        (ends,) = apply(jnp.where(gone, 0.0, u))
        base1[0] = ends
        base1[GROUPS + 1] = ends

    for i, copy in enumerate(label_swap):
        copy.wait_recv()
        ring[0, LABELS + i : LABELS + i + 1, :] = label_in[i, 0:1, :]
    depart(0, 1)
    step_one(2, 3)
    for c in range(1, len(PARTS)):
        swap[c - 1].wait_recv()
        depart(c, 1)
    for copy in halo:
        copy.wait_recv()
    st[0, :, 6:8, :] = jnp.where(first, 0.0, hr_up[...])
    st[GROUPS + 1, :, 0:2, :] = jnp.where(last, 0.0, hr_dn[...])

    def joined(slot, picks):
        lane = iota((1, COLS), 1) >> 5
        names = None
        for i, (offset, row) in enumerate(picks):
            one = ring[slot + offset, LABELS + row : LABELS + row + 1, :]
            names = one if i == 0 else jnp.where(lane == i, one, names)
        return names

    def one_hot(rows, names):
        return (rows == jnp.broadcast_to(names, rows.shape)).astype(F32).astype(BF16)

    def place_flux(j):
        for c in range(len(PARTS)):
            arrive(c, (2 * j, 2 * j + 1))
        slot = 2 * j
        fields = [
            jnp.concatenate(
                [
                    ring[slot + s, FLUX + (2 * c + f) * ROWS : FLUX + (2 * c + f + 1) * ROWS, :]
                    for s in range(2)
                    for c in range(NC)
                ],
                axis=0,
            )
            for f in range(2)
        ]
        high, low = split(jnp.concatenate(fields, axis=1))
        sel = one_hot(row_of[...], joined(slot, [(0, 0), (0, 1), (1, 0), (1, 1)]))
        part = mm(jnp.concatenate([sel, sel], axis=1), jnp.concatenate([high, low], axis=0))
        for f in range(2):
            cells = slice(f * COLS, (f + 1) * COLS)
            rows = slice(f * ROWS, (f + 1) * ROWS)
            flux_send[:, rows, :] += part[:MAIN, cells].reshape(GROUP, ROWS, COLS)
        ends_acc[...] += part[MAIN:]

    def place_water(j):
        slot = 2 * j
        arrive(0, (slot, slot + 1))
        water = jnp.concatenate([ring[slot + s, :LABELS, :] for s in range(2)], axis=0)
        high, low = split(water)
        sel = one_hot(row_of[:MAIN], joined(slot, [(0, 2), (1, 2), (0, 2), (1, 2)]))
        part = mm(sel, jnp.concatenate([high, low], axis=0))
        run_send[...] += part.reshape(GROUP, ROWS, COLS)

    ends_acc[...] = jnp.zeros(ends_acc.shape, F32)

    work = {
        2: ([lambda: step_one(1, 4)], [lambda: place_water(0)]),
        3: ([lambda: place_flux(0)], [step_one_ends, lambda: place_water(1)]),
        4: (
            [lambda: place_flux(1)],
            [lambda: place_flux(2), lambda: place_water(2), lambda: place_water(3)],
        ),
        5: (
            [lambda: place_flux(3)],
            [lambda: place_flux(4), lambda: place_flux(5), lambda: place_water(4)],
        ),
    }
    for level in range(2, LEVELS + 1):
        for c in range(len(PARTS)):
            depart(c, level)
            if c == 2:
                for item in work[level][0]:
                    item()
        for item in work[level][1]:
            item()
    for j in (HALF - 3, HALF - 2, HALF - 1):
        place_water(j)

    order = [4, 5, 2, 3, 6, 7, 1]

    def scatter_copies(src, dst, c):
        return [
            remote(src.at[b], dst.at[b], rs_ssem.at[c, b], rs_rsem.at[c, b], member(b))
            for b in order
        ]

    flux_scatter = scatter_copies(flux_send, flux_recv, 1)
    water_scatter = scatter_copies(run_send, run_recv, 0)
    for copy in water_scatter:
        copy.start()
    place_flux(HALF - 2)
    place_flux(HALF - 1)
    for b in range(GROUP):
        for f in range(2):
            cells = slice(f * COLS, (f + 1) * COLS)
            ends = 2 * ROWS + 2 * f
            flux_send[b, ends : ends + 2, :] = ends_acc[2 * b : 2 * b + 2, cells]
    for copy in flux_scatter:
        copy.start()

    step_two(1, 2)
    step_two(3, 4)
    kab_work()
    for copy in (*label_swap, *swap, *halo, *sends):
        copy.wait_send()

    loads[14].wait()
    for copy in water_scatter:
        copy.wait_recv()
    water = run_send[0]
    for b in range(1, GROUP):
        water = water + run_recv[b]
    river[...] = store[...] + water

    for copy in flux_scatter:
        copy.wait_recv()

    same, other = flux_send[0], flux_recv[1]
    for b in range(2, GROUP, 2):
        same = same + flux_recv[b]
        other = other + flux_recv[b + 1]
    pair = [jnp.where(core == 0, same, other), jnp.where(core == 0, other, same)]

    g4 = jnp.stack(
        [frac[...] * pair[f // 2][(f % 2) * ROWS : (f % 2 + 1) * ROWS] for f in range(FIELDS)],
        axis=0,
    )
    ends = [pair[f // 2][2 * ROWS + 2 * (f % 2) : 2 * ROWS + 2 * (f % 2) + 2] for f in range(FIELDS)]
    frac_above = jnp.where(first, 0.0, hr_up[LEV, 1:2, :])
    frac_below = jnp.where(last, 0.0, hr_dn[LEV, 0:1, :])
    above = jnp.stack([frac_above * x[0:1] for x in ends], axis=0)
    below = jnp.stack([frac_below * x[1:2] for x in ends], axis=0)
    lap = laplacian(g4, above, below)
    for i in range(GROUPS):
        high, low = split(
            jnp.concatenate(
                [x[:, 8 * i : 8 * i + 8].reshape(8 * FIELDS, COLS) for x in (g4, lap)], axis=0
            )
        )
        forced[i] = jnp.concatenate([high, low, high], axis=0)

    for copy in (*flux_scatter, *water_scatter):
        copy.wait_send()


def finish(base2, kab, forced, river, out_h, river_h, out, sems):
    river_copy = pltpu.make_async_copy(river, river_h.at[0], sems.at[GROUPS])
    river_copy.start()
    copies = []
    for i in range(0, GROUPS, 2):
        delta = mm(kab[...], jnp.concatenate([forced[i], forced[i + 1]], axis=1))
        for j in range(2):
            part = delta[:, COLS * j : COLS * (j + 1)].reshape(PAD, 8, COLS)
            out[i + j] = base2[i + j] + part
            copies.append(
                pltpu.make_async_copy(
                    out.at[i + j, pl.ds(0, LEV)],
                    out_h.at[0, :, pl.ds(8 * (i + j), 8)],
                    sems.at[i + j],
                )
            )
            copies[-1].start()
    for copy in (*copies, river_copy):
        copy.wait()


def shards(
    state, frac, diff, ops, weight, fo, fr, fb, ro, rr, rb, store,
):
    ops = jnp.transpose(ops, (1, 0, 2))
    fo, ro = fo.reshape(1, ROWS), ro.reshape(1, ROWS)
    args = (state, frac, diff, ops, weight, fo, fr, fb, ro, rr, rb, store)
    args = [pltpu.with_memory_space_constraint(x, pltpu.HBM) for x in args]
    vmem = pltpu.VMEM
    far = pl.BlockSpec(memory_space=pltpu.HBM)
    near = pl.BlockSpec(memory_space=vmem)
    dma = pltpu.SemaphoreType.DMA
    i32 = jnp.int32
    inner = pl.pallas_call(
        kernel,
        out_shape=(
            vmem((GROUPS, PAD, 8, COLS), F32),
            vmem((PAD * 8, 3 * 16 * FIELDS), BF16),
            vmem((GROUPS, 3 * 16 * FIELDS, COLS), BF16),
            vmem((ROWS, COLS), F32),
        ),
        in_specs=[far] * 12,
        out_specs=(near,) * 4,
        scratch_shapes=[
            vmem((GROUPS + 2, PAD, 8, COLS), F32),
            vmem((ROWS, COLS), F32),
            vmem((1, LEV), F32),
            vmem((LEV, 1, LEV), F32),
            vmem((NW, COLS, COLS), F32),
            vmem((1, ROWS), i32),
            vmem((1, ROWS), i32),
            vmem((1, ROWS), i32),
            vmem((1, ROWS), i32),
            vmem((1, ROWS), i32),
            vmem((1, ROWS), i32),
            vmem((ROWS, COLS), F32),
            dma((15,)),
            vmem((PAD, 2, COLS), F32),
            vmem((PAD, 2, COLS), F32),
            vmem((PAD, 2, COLS), F32),
            vmem((PAD, 2, COLS), F32),
            dma((2,)),
            dma((2,)),
            vmem((FIELDS, ROWS, COLS), F32),
            vmem((8, COLS), F32),
            vmem((2, 8, COLS), F32),
            dma((len(PARTS) + 1,)),
            dma((len(PARTS) + 1,)),
            vmem((SLOTS, SLOT, COLS), F32),
            dma((len(PARTS), SLOTS)),
            dma((len(PARTS), SLOTS)),
            vmem((MAIN + EDGE, COLS), F32),
            vmem((EDGE, 2 * COLS), F32),
            vmem((GROUP, BLOCK, COLS), F32),
            vmem((GROUP, BLOCK, COLS), F32),
            vmem((GROUP, ROWS, COLS), F32),
            vmem((GROUP, ROWS, COLS), F32),
            dma((2, GROUP)),
            dma((2, GROUP)),
            vmem((PAD * 8, COLS), F32),
            vmem((PAD * 8, PAD * 8), BF16),
            vmem((PAD * 8, PAD * 8), BF16),
            vmem((GROUPS + 2, PAD, 8, COLS), F32),
        ],
        compiler_params=pltpu.CompilerParams(
            collective_id=0, has_side_effects=True, vmem_limit_bytes=32 * 1024 * 1024
        ),
        name="coupling",
    )(*args)
    inner = [pltpu.with_memory_space_constraint(x, vmem) for x in inner]
    return pl.pallas_call(
        finish,
        out_shape=(
            pltpu.HBM((1, LEV, ROWS, COLS), F32),
            pltpu.HBM((1, ROWS, COLS), F32),
        ),
        in_specs=[near] * 4,
        out_specs=(far, far),
        scratch_shapes=[vmem((GROUPS, PAD, 8, COLS), F32), dma((GROUPS + 1,))],
        compiler_params=pltpu.CompilerParams(vmem_limit_bytes=16 * 1024 * 1024),
        name="finish",
    )(*inner)


def solution(mesh):
    in_specs = (
        P("sec", None, "dom", None),
        P("sec", "dom", None),
        P("sec", None),
        P("sec", None, None),
        P("sec", "dom", None, None),
        P("sec", "dom", None),
        P("sec", "dom"),
        P("sec", "dom"),
        P("sec", "dom", None),
        P("sec", "dom"),
        P("sec", "dom"),
        P("sec", "dom", None),
    )
    out_specs = (P("sec", None, "dom", None), P("sec", "dom", None))
    return jax.shard_map(shards, mesh=mesh, in_specs=in_specs, out_specs=out_specs, check_vma=False)
```

```python
import jax
import jax.numpy as jnp
from jax import lax
from jax.experimental import pallas as pl
from jax.experimental.pallas import tpu as pltpu
from jax.sharding import PartitionSpec as P

MESH = pl.DeviceIdType.MESH
F32 = jnp.float32
BF16 = jnp.bfloat16

LEV = 30
PAD = 32
COLS = 128
ROWS = 32
FIELDS = 4
NW = 8
NY, NZ, NC = 4, 16, 2
N_DOM = NY * NZ * NC
GROUP = NY * NC
HALF = NZ // 2
SLOTS = NZ
GROUPS = ROWS // 8
MAIN = GROUP * ROWS
EDGE = GROUP * 2
FLUX = ROWS
SLOT = FLUX + 2 * NC * ROWS
PIECES = 1 + 2 * NC
FLUX_LABEL, WATER_LABEL = PIECES, PIECES + 1
BLOCK = 2 * ROWS + 8


def tree(jumps):
    levels, reached = {}, 0
    for level, jump in enumerate(jumps, 1):
        levels[level] = [(reached, reached + i) for i in range(jump, 0, -1)]
        reached += jump
    return levels


LONG, SHORT = tree((2, 1, 2, 1, 2)), tree((1, 2, 1, 2, 1))
LEVELS = len(LONG)


def split(x):
    high = x.astype(BF16)
    return high, (x - high.astype(F32)).astype(BF16)


def mm(a, b):
    return jnp.dot(a, b, preferred_element_type=F32)


def mm3(a, b):
    (ah, al), (bh, bl) = a, b
    return mm(ah, bh) + (mm(ah, bl) + mm(al, bh))


def iota(shape, dim):
    return lax.broadcasted_iota(jnp.int32, shape, dim)


def neighbours_in_columns(x):
    axis = x.ndim - 1
    return pltpu.roll(x, 1, axis) + pltpu.roll(x, COLS - 1, axis)


def laplacian(x, above, below):
    row, count = iota(x.shape, 1), x.shape[1]
    down = jnp.where(row == 0, above, pltpu.roll(x, 1, 1))
    up = jnp.where(row == count - 1, below, pltpu.roll(x, count - 1, 1))
    return down + up + neighbours_in_columns(x) - 4.0 * x


def kernel(
    state_h, frac_h, diff_h, ops_h, weight_h, fo_h, fr_h, fb_h, ro_h, rr_h, rb_h, store_h,
    base2, kab, forced, river,
    st, frac, diff, ops, weight, fo, fr, fb, ro, rr, rb, store,
    local_sem,
    hs_up, hs_dn, hr_up, hr_dn, halo_ssem, halo_rsem,
    terms, label_out, label_in, part_ssem, part_rsem,
    ring, lab_f, lab_w, ring_ssem, ring_rsem, row_of, ends_acc,
    flux_send, flux_recv, run_send, run_recv, rs_ssem, rs_rsem,
    dcol, kron_h, kron_l, base1,
):
    sec = lax.axis_index("sec")
    me = lax.axis_index("dom")
    core = me & (NC - 1)
    z = (me >> 1) & (NZ - 1)
    y = me >> 5

    def dom_of(yy, zz, cc):
        return (yy * NZ + zz) * NC + cc

    def along(distance):
        return (sec, dom_of(y, (z + NZ + distance) & (NZ - 1), core))

    partners = [(sec ^ 2, me), (sec ^ 2, me ^ 1)]
    after = (sec, (me + 1) & (N_DOM - 1))
    before = (sec, (me + N_DOM - 1) & (N_DOM - 1))

    def member(b):
        return (sec, dom_of((y + b // NC) & (NY - 1), z, core ^ (b % NC)))

    pairs = [(weight_h.at[0], weight)]
    pairs += [
        (state_h.at[0, :, pl.ds(8 * i, 8)], st.at[1 + i, pl.ds(0, LEV)]) for i in range(GROUPS)
    ]
    pairs += [
        (fb_h, fb), (rb_h, rb), (fo_h, fo), (fr_h, fr), (ro_h, ro), (rr_h, rr),
        (frac_h.at[0], frac), (ops_h, ops), (diff_h, diff), (store_h.at[0], store),
    ]
    loads = [pltpu.make_async_copy(a, b, local_sem.at[i]) for i, (a, b) in enumerate(pairs)]
    for copy in loads:
        copy.start()

    barrier = pltpu.get_barrier_semaphore()
    peers = [along(d) for d in (1, -1, 2, -2)] + [*partners, after, before] + [member(b) for b in range(1, GROUP)]
    for peer in peers:
        pl.semaphore_signal(barrier, inc=1, device_id=peer, device_id_type=MESH)

    for copy in loads[5:11]:
        copy.wait()

    def label_of(owner, row):
        eye = iota((ROWS, ROWS), 0) == iota((ROWS, ROWS), 1)
        target = (owner[...] * ROWS + row[...]).astype(F32)
        rows = jnp.broadcast_to(target, (ROWS, ROWS))
        column = jnp.sum(jnp.where(eye, rows, 0.0), axis=1, keepdims=True)
        wide = jnp.broadcast_to(column, (ROWS, COLS))
        place = iota((ROWS, COLS), 0) == (iota((ROWS, COLS), 1) & (ROWS - 1))
        return jnp.sum(jnp.where(place, wide, 0.0), axis=0, keepdims=True)

    label_out[...] = label_of(fo, fr)
    lab_w[0] = label_of(ro, rr)

    tall = FIELDS * ROWS + ROWS
    spot = (iota((tall, ROWS), 0) & (ROWS - 1)) == iota((tall, ROWS), 1)
    blocks = jnp.where(
        iota((tall, ROWS), 0) < FIELDS * ROWS,
        jnp.broadcast_to(fb[...].astype(F32), (tall, ROWS)),
        jnp.broadcast_to(rb[...].astype(F32), (tall, ROWS)),
    )
    block = jnp.sum(jnp.where(spot, blocks, 0.0), axis=1, keepdims=True)
    block = jnp.broadcast_to(jnp.concatenate([block, block], axis=0), (2 * tall, COLS))
    for copy in loads[1:5]:
        copy.wait()
    surface = jnp.concatenate(
        [st[1 + i, f] for f in (*range(FIELDS), 0) for i in range(GROUPS)], axis=0
    )
    high = surface.astype(BF16).astype(F32)
    both = jnp.concatenate([high, surface - high], axis=0)
    lhs = jnp.concatenate(
        [jnp.where(block == float(w), both, 0.0).astype(BF16) for w in range(NW)], axis=1
    )
    loads[0].wait()
    rhs = jnp.concatenate(split(weight[...].reshape(NW * COLS, COLS)), axis=1)
    total = mm(lhs, rhs)
    result = total[:tall, :COLS] + (total[:tall, COLS:] + total[tall:, :COLS])
    terms[...] = result[: FIELDS * ROWS].reshape(FIELDS, ROWS, COLS)
    ring[0, :FLUX, :] = result[FIELDS * ROWS :]

    pl.semaphore_wait(barrier, len(peers))

    def remote(src, dst, ssem, rsem, device):
        return pltpu.make_async_remote_copy(
            src_ref=src, dst_ref=dst, send_sem=ssem, recv_sem=rsem,
            device_id=device, device_id_type=MESH,
        )

    def slot_of(way, distance):
        return 0 if distance == 0 else min(2 * distance - (way > 0), SLOTS - 1)

    def piece(c, slot):
        if c < PIECES:
            return ring.at[slot, pl.ds(c * ROWS, ROWS)]
        return (lab_f if c == FLUX_LABEL else lab_w).at[slot]

    def hop(c, way, start, end):
        slot = slot_of(way, end)
        return remote(
            piece(c, slot_of(way, start)), piece(c, slot),
            ring_ssem.at[c, slot], ring_rsem.at[c, slot], along(way * (end - start)),
        )

    arrivals, departures = {}, {}
    for c in range(PIECES + 2):
        for way in (1, -1):
            levels = LONG if (c % 2 == 0) == (way > 0) else SHORT
            for level, edges in levels.items():
                copies = [hop(c, way, *edge) for edge in edges]
                departures[c, way, level] = (slot_of(way, edges[0][0]), copies)
                for copy, (_, end) in zip(copies, edges):
                    arrivals[c, slot_of(way, end)] = copy
    sends = list(arrivals.values())

    def arrive(c, slots):
        for slot in slots:
            if (c, slot) in arrivals:
                arrivals.pop((c, slot)).wait_recv()

    def depart(c, level):
        for way in (1, -1):
            if (c, way, level) in departures:
                slot, copies = departures.pop((c, way, level))
                arrive(c, [slot])
                for copy in copies:
                    copy.start()

    label_swap = [
        remote(label_out, label_in.at[i], part_ssem.at[i], part_rsem.at[i], to)
        for i, to in enumerate(partners)
    ]
    swap = []
    for c in range(1, PIECES):
        f, i = (c - 1) // NC, (c - 1) % NC
        swap.append(
            remote(
                terms.at[2 * (core ^ i) + f], piece(c, 0),
                part_ssem.at[1 + c], part_rsem.at[1 + c], partners[i],
            )
        )
    for copy in (*label_swap, *swap):
        copy.start()

    def depart_water(level):
        depart(WATER_LABEL, level)
        depart(0, level)

    depart_water(1)

    loads[11].wait()
    hs_up[0:LEV] = st[1, 0:LEV, 0:2, :]
    hs_dn[0:LEV] = st[GROUPS, 0:LEV, 6:8, :]
    hs_up[LEV] = frac[0:2, :]
    hs_dn[LEV] = frac[ROWS - 2 : ROWS, :]
    hs_up[LEV + 1] = jnp.zeros((2, COLS), F32)
    hs_dn[LEV + 1] = jnp.zeros((2, COLS), F32)
    for i in range(GROUPS):
        st[1 + i, LEV:PAD] = jnp.zeros((PAD - LEV, 8, COLS), F32)
    halo = [
        remote(hs_dn, hr_up, halo_ssem.at[0], halo_rsem.at[0], after),
        remote(hs_up, hr_dn, halo_ssem.at[1], halo_rsem.at[1], before),
    ]
    for copy in halo:
        copy.start()

    tall8 = PAD * 8
    for copy in loads[12:14]:
        copy.wait()
    pick = ((iota((tall8, LEV), 0) >> 3) == iota((tall8, LEV), 1)).astype(F32)
    pick_t = ((iota((LEV, tall8), 1) >> 3) == iota((LEV, tall8), 0)).astype(BF16)
    column = jnp.sum(pick * jnp.broadcast_to(diff[...], (tall8, LEV)), axis=1, keepdims=True)
    dcol[...] = jnp.broadcast_to(column, (tall8, COLS))
    op = ops[:, 0, :]
    op_h, op_l = split(op)
    op_r = (op - op_h.astype(F32) - op_l.astype(F32)).astype(BF16)
    pick = pick.astype(BF16)
    spread = mm(mm(pick, op_h).astype(BF16), pick_t) + (
        mm(mm(pick, op_l).astype(BF16), pick_t) + mm(mm(pick, op_r).astype(BF16), pick_t)
    )
    same8 = (iota((tall8, tall8), 0) & 7) == (iota((tall8, tall8), 1) & 7)
    kh, kl = split(jnp.where(same8, spread, 0.0))
    kron_h[...] = kh
    kron_l[...] = kl

    def kab_work():
        k4 = kron_h[:, : 8 * FIELDS].astype(F32) + kron_l[:, : 8 * FIELDS].astype(F32)
        eye = (iota(k4.shape, 0) == iota(k4.shape, 1)).astype(F32)
        q = jnp.concatenate([k4 + eye, dcol[:, : 8 * FIELDS] * k4], axis=1)
        kh, kl = split(mm3((kron_h[...], kron_l[...]), split(q)))
        kab[...] = jnp.concatenate([kh, kh, kl], axis=1)

    def block_start(b):
        return dom_of((y + (b >> 1)) & (NY - 1), z, core ^ (b & 1)) * ROWS

    i = iota((MAIN, COLS), 0)
    row_of[:MAIN] = (block_start(i >> 5) + (i & (ROWS - 1))).astype(F32)
    i = iota((EDGE, COLS), 0)
    row_of[MAIN:] = (block_start(i >> 1) + jnp.where((i & 1) == 0, -1, ROWS)).astype(F32)
    flux_send[:, 2 * ROWS + 4 :, :] = jnp.zeros((GROUP, 4, COLS), F32)

    first = me == 0
    last = me == N_DOM - 1

    def apply(*groups):
        u = jnp.concatenate([u.reshape(PAD * 8, COLS) for u in groups], axis=1)
        out = mm3((kron_h[...], kron_l[...]), split(u))
        return [
            out[:, COLS * i : COLS * (i + 1)].reshape(PAD, 8, COLS) for i in range(len(groups))
        ]

    def diffused(i, source):
        x = source[i]
        lap = laplacian(x, source[i - 1, :, 7:8], source[i + 1, :, 0:1])
        return x + dcol[...].reshape(PAD, 8, COLS) * lap

    def step_one(i, j):
        base1[i], base1[j] = apply(diffused(i, st), diffused(j, st))

    def step_two(i, j):
        base2[i - 1], base2[j - 1] = apply(diffused(i, base1), diffused(j, base1))

    def step_one_ends():
        d = dcol[...].reshape(PAD, 8, COLS)
        spot = iota((PAD, 8, COLS), 1)
        above, below = st[0], st[GROUPS + 1]
        x = jnp.where(spot == 7, above[:, 7:8], below[:, 0:1])
        outer = jnp.where(spot == 7, above[:, 6:7], below[:, 1:2])
        inner = jnp.where(spot == 7, st[1, :, 0:1], st[GROUPS, :, 7:8])
        u = x + d * (outer + inner + neighbours_in_columns(x) - 4.0 * x)
        gone = ((spot == 7) & first) | ((spot < 7) & last)
        (ends,) = apply(jnp.where(gone, 0.0, u))
        base1[0] = ends
        base1[GROUPS + 1] = ends

    depart_water(2)
    step_one(2, 3)
    for i, copy in enumerate(label_swap):
        copy.wait_recv()
        lab_f[0, i : i + 1, :] = label_in[i]
    depart(FLUX_LABEL, 1)
    for c in range(1, PIECES):
        swap[c - 1].wait_recv()
        depart(c, 1)
    depart_water(3)
    for copy in halo:
        copy.wait_recv()
    st[0, :, 6:8, :] = jnp.where(first, 0.0, hr_up[...])
    st[GROUPS + 1, :, 0:2, :] = jnp.where(last, 0.0, hr_dn[...])

    def joined(rows):
        lane = iota((1, COLS), 1) >> 5
        names = rows[0]
        for i in range(1, 4):
            names = jnp.where(lane == i, rows[i], names)
        return names

    def one_hot(rows, names):
        return (rows == jnp.broadcast_to(names, rows.shape)).astype(F32).astype(BF16)

    def select_flux(j):
        arrive(FLUX_LABEL, (2 * j, 2 * j + 1))
        rows = [lab_f[2 * j + i // 2, i % 2 : i % 2 + 1, :] for i in range(4)]
        return one_hot(row_of[...], joined(rows))

    def rows_of(f, slots):
        parts = []
        for slot in slots:
            for c in range(1 + NC * f, 1 + NC * (f + 1)):
                arrive(c, [slot])
                parts.append(ring[slot, c * ROWS : (c + 1) * ROWS, :])
        return jnp.concatenate(parts, axis=0)

    def place_flux(first_slot, last_slot, fields, fresh):
        sel = [select_flux(j) for j in range(first_slot // 2, last_slot // 2)]
        data = [rows_of(f, range(first_slot, last_slot)) for f in fields]
        high, low = split(jnp.concatenate(data, axis=1))
        part = mm(jnp.concatenate([*sel, *sel], axis=1), jnp.concatenate([high, low], axis=0))
        for i, f in enumerate(fields):
            one = part[:, i * COLS : (i + 1) * COLS]
            rows = slice(f * ROWS, (f + 1) * ROWS)
            main = one[:MAIN].reshape(GROUP, ROWS, COLS)
            flux_send[:, rows, :] = main if fresh else flux_send[:, rows, :] + main
            ends_acc[f] = one[MAIN:] if fresh else ends_acc[f] + one[MAIN:]

    def place_water():
        for c in (WATER_LABEL, 0):
            arrive(c, range(SLOTS))
        high, low = split(jnp.concatenate([ring[slot, :FLUX, :] for slot in range(SLOTS)], axis=0))
        sel = [
            one_hot(row_of[:MAIN], joined([lab_w[4 * g + i] for i in range(4)]))
            for g in range(SLOTS // 4)
        ]
        part = mm(jnp.concatenate([*sel, *sel], axis=1), jnp.concatenate([high, low], axis=0))
        run_send[...] = part.reshape(GROUP, ROWS, COLS)
        for copy in water_scatter:
            copy.start()

    order = [4, 5, 2, 3, 6, 7, 1]

    def scatter_copies(src, dst, c, rows):
        return [
            remote(
                src.at[b, rows], dst.at[b, rows], rs_ssem.at[c, b], rs_rsem.at[c, b], member(b)
            )
            for b in order
        ]

    water_scatter = scatter_copies(run_send, run_recv, 0, pl.ds(0, ROWS))
    flux_scatter = [
        scatter_copies(flux_send, flux_recv, 1, pl.ds(0, ROWS)),
        scatter_copies(flux_send, flux_recv, 2, pl.ds(ROWS, BLOCK - ROWS)),
    ]

    for level in range(2, LEVELS + 1):
        depart(FLUX_LABEL, level)
        for c in range(1, PIECES):
            depart(c, level)
        depart_water(level + 2)
        if level == LEVELS - 1:
            place_water()
    place_flux(0, 8, (0, 1), True)
    place_flux(8, 12, (0, 1), False)
    for f in range(2):
        place_flux(12, SLOTS, (f,), False)
        if f == 1:
            for b in range(GROUP):
                for e in range(2):
                    ends = 2 * ROWS + 2 * e
                    flux_send[b, ends : ends + 2, :] = ends_acc[e, 2 * b : 2 * b + 2]
        for copy in flux_scatter[f]:
            copy.start()

    step_one(1, 4)
    step_one_ends()
    step_two(1, 2)
    step_two(3, 4)
    kab_work()
    for copy in (*label_swap, *swap, *halo, *sends):
        copy.wait_send()

    loads[14].wait()
    for copy in water_scatter:
        copy.wait_recv()
    water = run_send[0]
    for b in range(1, GROUP):
        water = water + run_recv[b]
    river[...] = store[...] + water

    for copy in (*flux_scatter[0], *flux_scatter[1]):
        copy.wait_recv()

    same, other = flux_send[0], flux_recv[1]
    for b in range(2, GROUP, 2):
        same = same + flux_recv[b]
        other = other + flux_recv[b + 1]
    pair = [jnp.where(core == 0, same, other), jnp.where(core == 0, other, same)]

    g4 = jnp.stack(
        [frac[...] * pair[f // 2][(f % 2) * ROWS : (f % 2 + 1) * ROWS] for f in range(FIELDS)],
        axis=0,
    )
    ends = [pair[f // 2][2 * ROWS + 2 * (f % 2) : 2 * ROWS + 2 * (f % 2) + 2] for f in range(FIELDS)]
    frac_above = jnp.where(first, 0.0, hr_up[LEV, 1:2, :])
    frac_below = jnp.where(last, 0.0, hr_dn[LEV, 0:1, :])
    above = jnp.stack([frac_above * x[0:1] for x in ends], axis=0)
    below = jnp.stack([frac_below * x[1:2] for x in ends], axis=0)
    lap = laplacian(g4, above, below)
    for i in range(GROUPS):
        high, low = split(
            jnp.concatenate(
                [x[:, 8 * i : 8 * i + 8].reshape(8 * FIELDS, COLS) for x in (g4, lap)], axis=0
            )
        )
        forced[i] = jnp.concatenate([high, low, high], axis=0)

    for copy in (*flux_scatter[0], *flux_scatter[1], *water_scatter):
        copy.wait_send()


def finish(base2, kab, forced, river, out_h, river_h, out, sems):
    river_copy = pltpu.make_async_copy(river, river_h.at[0], sems.at[GROUPS])
    river_copy.start()
    copies = []
    for i in range(0, GROUPS, 2):
        delta = mm(kab[...], jnp.concatenate([forced[i], forced[i + 1]], axis=1))
        for j in range(2):
            part = delta[:, COLS * j : COLS * (j + 1)].reshape(PAD, 8, COLS)
            out[i + j] = base2[i + j] + part
            copies.append(
                pltpu.make_async_copy(
                    out.at[i + j, pl.ds(0, LEV)],
                    out_h.at[0, :, pl.ds(8 * (i + j), 8)],
                    sems.at[i + j],
                )
            )
            copies[-1].start()
    for copy in (*copies, river_copy):
        copy.wait()


def shards(
    state, frac, diff, ops, weight, fo, fr, fb, ro, rr, rb, store,
):
    ops = jnp.transpose(ops, (1, 0, 2))
    fo, ro = fo.reshape(1, ROWS), ro.reshape(1, ROWS)
    args = (state, frac, diff, ops, weight, fo, fr, fb, ro, rr, rb, store)
    args = [pltpu.with_memory_space_constraint(x, pltpu.HBM) for x in args]
    vmem = pltpu.VMEM
    far = pl.BlockSpec(memory_space=pltpu.HBM)
    near = pl.BlockSpec(memory_space=vmem)
    dma = pltpu.SemaphoreType.DMA
    i32 = jnp.int32
    inner = pl.pallas_call(
        kernel,
        out_shape=(
            vmem((GROUPS, PAD, 8, COLS), F32),
            vmem((PAD * 8, 3 * 16 * FIELDS), BF16),
            vmem((GROUPS, 3 * 16 * FIELDS, COLS), BF16),
            vmem((ROWS, COLS), F32),
        ),
        in_specs=[far] * 12,
        out_specs=(near,) * 4,
        scratch_shapes=[
            vmem((GROUPS + 2, PAD, 8, COLS), F32),
            vmem((ROWS, COLS), F32),
            vmem((1, LEV), F32),
            vmem((LEV, 1, LEV), F32),
            vmem((NW, COLS, COLS), F32),
            vmem((1, ROWS), i32),
            vmem((1, ROWS), i32),
            vmem((1, ROWS), i32),
            vmem((1, ROWS), i32),
            vmem((1, ROWS), i32),
            vmem((1, ROWS), i32),
            vmem((ROWS, COLS), F32),
            dma((15,)),
            vmem((PAD, 2, COLS), F32),
            vmem((PAD, 2, COLS), F32),
            vmem((PAD, 2, COLS), F32),
            vmem((PAD, 2, COLS), F32),
            dma((2,)),
            dma((2,)),
            vmem((FIELDS, ROWS, COLS), F32),
            vmem((1, COLS), F32),
            vmem((2, 1, COLS), F32),
            dma((PIECES + 1,)),
            dma((PIECES + 1,)),
            vmem((SLOTS, SLOT, COLS), F32),
            vmem((SLOTS, 2, COLS), F32),
            vmem((SLOTS, 1, COLS), F32),
            dma((PIECES + 2, SLOTS)),
            dma((PIECES + 2, SLOTS)),
            vmem((MAIN + EDGE, COLS), F32),
            vmem((2, EDGE, COLS), F32),
            vmem((GROUP, BLOCK, COLS), F32),
            vmem((GROUP, BLOCK, COLS), F32),
            vmem((GROUP, ROWS, COLS), F32),
            vmem((GROUP, ROWS, COLS), F32),
            dma((3, GROUP)),
            dma((3, GROUP)),
            vmem((PAD * 8, COLS), F32),
            vmem((PAD * 8, PAD * 8), BF16),
            vmem((PAD * 8, PAD * 8), BF16),
            vmem((GROUPS + 2, PAD, 8, COLS), F32),
        ],
        compiler_params=pltpu.CompilerParams(
            collective_id=0, has_side_effects=True, vmem_limit_bytes=32 * 1024 * 1024
        ),
        name="coupling",
    )(*args)
    inner = [pltpu.with_memory_space_constraint(x, vmem) for x in inner]
    return pl.pallas_call(
        finish,
        out_shape=(
            pltpu.HBM((1, LEV, ROWS, COLS), F32),
            pltpu.HBM((1, ROWS, COLS), F32),
        ),
        in_specs=[near] * 4,
        out_specs=(far, far),
        scratch_shapes=[vmem((GROUPS, PAD, 8, COLS), F32), dma((GROUPS + 1,))],
        compiler_params=pltpu.CompilerParams(vmem_limit_bytes=16 * 1024 * 1024),
        name="finish",
    )(*inner)


def solution(mesh):
    in_specs = (
        P("sec", None, "dom", None),
        P("sec", "dom", None),
        P("sec", None),
        P("sec", None, None),
        P("sec", "dom", None, None),
        P("sec", "dom", None),
        P("sec", "dom"),
        P("sec", "dom"),
        P("sec", "dom", None),
        P("sec", "dom"),
        P("sec", "dom"),
        P("sec", "dom", None),
    )
    out_specs = (P("sec", None, "dom", None), P("sec", "dom", None))
    return jax.shard_map(shards, mesh=mesh, in_specs=in_specs, out_specs=out_specs, check_vma=False)
```

```python
import jax
import jax.numpy as jnp
from jax import lax
from jax.experimental import pallas as pl
from jax.experimental.pallas import tpu as pltpu
from jax.sharding import PartitionSpec as P

MESH = pl.DeviceIdType.MESH
F32 = jnp.float32
BF16 = jnp.bfloat16

LEV = 30
PAD = 32
COLS = 128
ROWS = 32
FIELDS = 4
NW = 8
NY, NZ, NC = 4, 16, 2
N_DOM = NY * NZ * NC
GROUP = NY * NC
HALF = NZ // 2
SLOTS = NZ
GROUPS = ROWS // 8
MAIN = GROUP * ROWS
EDGE = GROUP * 2
WATER_LABEL = ROWS
FLUX_LABEL = WATER_LABEL + 8
FLUX = FLUX_LABEL + 8
SLOT = FLUX + 2 * NC * ROWS
WATER, FIELD_A, FIELD_B = range(3)
PIECES = (
    (0, FLUX_LABEL),
    (FLUX_LABEL, 8 + NC * ROWS),
    (FLUX + NC * ROWS, NC * ROWS),
)
BLOCK = 2 * ROWS + 8


def tree(jumps):
    levels, reached = {}, 0
    for level, jump in enumerate(jumps, 1):
        levels[level] = [(reached, reached + i) for i in range(jump, 0, -1)]
        reached += jump
    return levels


WATER_TREES = tree((2, 1, 2, 1, 2)), tree((1, 2, 1, 2, 1))
FLUX_TREES = tree((2, 2, 2, 2)), tree((1, 2, 2, 2))
LEVELS = len(FLUX_TREES[0])


def split(x):
    high = x.astype(BF16)
    return high, (x - high.astype(F32)).astype(BF16)


def mm(a, b):
    return jnp.dot(a, b, preferred_element_type=F32)


def mm3(a, b):
    (ah, al), (bh, bl) = a, b
    return mm(ah, bh) + (mm(ah, bl) + mm(al, bh))


def iota(shape, dim):
    return lax.broadcasted_iota(jnp.int32, shape, dim)


def neighbours_in_columns(x):
    axis = x.ndim - 1
    return pltpu.roll(x, 1, axis) + pltpu.roll(x, COLS - 1, axis)


def laplacian(x, above, below):
    row, count = iota(x.shape, 1), x.shape[1]
    down = jnp.where(row == 0, above, pltpu.roll(x, 1, 1))
    up = jnp.where(row == count - 1, below, pltpu.roll(x, count - 1, 1))
    return down + up + neighbours_in_columns(x) - 4.0 * x


def kernel(
    state_h, frac_h, diff_h, ops_h, weight_h, fo_h, fr_h, fb_h, ro_h, rr_h, rb_h, store_h,
    base2, kab, forced, river,
    st, frac, diff, ops, weight, fo, fr, fb, ro, rr, rb, store,
    local_sem,
    hs_up, hs_dn, hr_up, hr_dn, halo_ssem, halo_rsem,
    terms, label_out, label_in, part_ssem, part_rsem,
    ring, ring_ssem, ring_rsem, row_of, ends_acc,
    flux_send, flux_recv, run_send, run_recv, rs_ssem, rs_rsem,
    dcol, kron_h, kron_l, base1,
):
    sec = lax.axis_index("sec")
    me = lax.axis_index("dom")
    core = me & (NC - 1)
    z = (me >> 1) & (NZ - 1)
    y = me >> 5

    def dom_of(yy, zz, cc):
        return (yy * NZ + zz) * NC + cc

    def along(distance):
        return (sec, dom_of(y, (z + NZ + distance) & (NZ - 1), core))

    partners = [(sec ^ 2, me), (sec ^ 2, me ^ 1)]
    after = (sec, (me + 1) & (N_DOM - 1))
    before = (sec, (me + N_DOM - 1) & (N_DOM - 1))

    def member(b):
        return (sec, dom_of((y + b // NC) & (NY - 1), z, core ^ (b % NC)))

    barrier = pltpu.get_barrier_semaphore()
    peers = [*partners, *[along(d) for d in (1, -1, 2, -2)], after, before]
    peers += [member(b) for b in range(1, GROUP)]
    for peer in peers:
        pl.semaphore_signal(barrier, inc=1, device_id=peer, device_id_type=MESH)

    pairs = [(weight_h.at[0], weight)]
    pairs += [
        (state_h.at[0, :, pl.ds(8 * i, 8)], st.at[1 + i, pl.ds(0, LEV)]) for i in range(GROUPS)
    ]
    pairs += [
        (fb_h, fb), (rb_h, rb), (fo_h, fo), (fr_h, fr), (ro_h, ro), (rr_h, rr),
        (frac_h.at[0], frac), (ops_h, ops), (diff_h, diff), (store_h.at[0], store),
    ]
    loads = [pltpu.make_async_copy(a, b, local_sem.at[i]) for i, (a, b) in enumerate(pairs)]
    for copy in loads:
        copy.start()

    for copy in loads[5:11]:
        copy.wait()

    def label_of(owner, row):
        eye = iota((ROWS, ROWS), 0) == iota((ROWS, ROWS), 1)
        target = (owner[...] * ROWS + row[...]).astype(F32)
        rows = jnp.broadcast_to(target, (ROWS, ROWS))
        column = jnp.sum(jnp.where(eye, rows, 0.0), axis=1, keepdims=True)
        wide = jnp.broadcast_to(column, (ROWS, COLS))
        place = iota((ROWS, COLS), 0) == (iota((ROWS, COLS), 1) & (ROWS - 1))
        return jnp.sum(jnp.where(place, wide, 0.0), axis=0, keepdims=True)

    label_out[...] = label_of(fo, fr)
    ring[0, WATER_LABEL:FLUX_LABEL, :] = jnp.broadcast_to(label_of(ro, rr), (8, COLS))
    ring[0, FLUX_LABEL:FLUX, :] = jnp.zeros((8, COLS), F32)

    tall = FIELDS * ROWS + ROWS
    spot = (iota((tall, ROWS), 0) & (ROWS - 1)) == iota((tall, ROWS), 1)
    blocks = jnp.where(
        iota((tall, ROWS), 0) < FIELDS * ROWS,
        jnp.broadcast_to(fb[...].astype(F32), (tall, ROWS)),
        jnp.broadcast_to(rb[...].astype(F32), (tall, ROWS)),
    )
    block = jnp.sum(jnp.where(spot, blocks, 0.0), axis=1, keepdims=True)
    block = jnp.broadcast_to(jnp.concatenate([block, block], axis=0), (2 * tall, COLS))
    for copy in loads[1:5]:
        copy.wait()
    surface = jnp.concatenate(
        [st[1 + i, f] for f in (*range(FIELDS), 0) for i in range(GROUPS)], axis=0
    )
    high = surface.astype(BF16).astype(F32)
    both = jnp.concatenate([high, surface - high], axis=0)
    lhs = jnp.concatenate(
        [jnp.where(block == float(w), both, 0.0).astype(BF16) for w in range(NW)], axis=1
    )
    loads[0].wait()
    rhs = jnp.concatenate(split(weight[...].reshape(NW * COLS, COLS)), axis=1)
    total = mm(lhs, rhs)
    result = total[:tall, :COLS] + (total[:tall, COLS:] + total[tall:, :COLS])
    terms[...] = result[: FIELDS * ROWS].reshape(FIELDS, ROWS, COLS)
    ring[0, :WATER_LABEL, :] = result[FIELDS * ROWS :]

    loads[11].wait()
    hs_up[0:LEV] = st[1, 0:LEV, 0:2, :]
    hs_dn[0:LEV] = st[GROUPS, 0:LEV, 6:8, :]
    hs_up[LEV] = frac[0:2, :]
    hs_dn[LEV] = frac[ROWS - 2 : ROWS, :]
    hs_up[LEV + 1] = jnp.zeros((2, COLS), F32)
    hs_dn[LEV + 1] = jnp.zeros((2, COLS), F32)
    for i in range(GROUPS):
        st[1 + i, LEV:PAD] = jnp.zeros((PAD - LEV, 8, COLS), F32)
    tall8 = PAD * 8
    for copy in loads[12:14]:
        copy.wait()
    pick = ((iota((tall8, LEV), 0) >> 3) == iota((tall8, LEV), 1)).astype(F32)
    pick_t = ((iota((LEV, tall8), 1) >> 3) == iota((LEV, tall8), 0)).astype(BF16)
    column = jnp.sum(pick * jnp.broadcast_to(diff[...], (tall8, LEV)), axis=1, keepdims=True)
    dcol[...] = jnp.broadcast_to(column, (tall8, COLS))
    op = ops[:, 0, :]
    op_h, op_l = split(op)
    op_r = (op - op_h.astype(F32) - op_l.astype(F32)).astype(BF16)
    pick = pick.astype(BF16)
    spread = mm(mm(pick, op_h).astype(BF16), pick_t) + (
        mm(mm(pick, op_l).astype(BF16), pick_t) + mm(mm(pick, op_r).astype(BF16), pick_t)
    )
    same8 = (iota((tall8, tall8), 0) & 7) == (iota((tall8, tall8), 1) & 7)
    kh, kl = split(jnp.where(same8, spread, 0.0))
    kron_h[...] = kh
    kron_l[...] = kl

    def block_start(b):
        return dom_of((y + (b >> 1)) & (NY - 1), z, core ^ (b & 1)) * ROWS

    i = iota((MAIN, COLS), 0)
    row_of[:MAIN] = (block_start(i >> 5) + (i & (ROWS - 1))).astype(F32)
    i = iota((EDGE, COLS), 0)
    row_of[MAIN:] = (block_start(i >> 1) + jnp.where((i & 1) == 0, -1, ROWS)).astype(F32)
    flux_send[:, 2 * ROWS + 4 :, :] = jnp.zeros((GROUP, 4, COLS), F32)

    pl.semaphore_wait(barrier, len(peers))

    def remote(src, dst, ssem, rsem, device):
        return pltpu.make_async_remote_copy(
            src_ref=src, dst_ref=dst, send_sem=ssem, recv_sem=rsem,
            device_id=device, device_id_type=MESH,
        )

    def slot_of(way, distance):
        return 0 if distance == 0 else min(2 * distance - (way > 0), SLOTS - 1)

    def piece(c, slot):
        return ring.at[slot, pl.ds(*PIECES[c])]

    def hop(c, way, start, end):
        slot = slot_of(way, end)
        return remote(
            piece(c, slot_of(way, start)), piece(c, slot),
            ring_ssem, ring_rsem.at[c, slot], along(way * (end - start)),
        )

    arrivals, departures = {}, {}
    for c in range(len(PIECES)):
        for way in (1, -1):
            trees = WATER_TREES if c == WATER else FLUX_TREES
            levels = trees[(c % 2 == 0) != (way > 0)]
            for level, edges in levels.items():
                copies = [hop(c, way, *edge) for edge in edges]
                departures[c, way, level] = (slot_of(way, edges[0][0]), copies)
                for copy, (_, end) in zip(copies, edges):
                    arrivals[c, slot_of(way, end)] = copy

    def arrive(c, slots):
        for slot in slots:
            if (c, slot) in arrivals:
                arrivals.pop((c, slot)).wait_recv()

    def depart(c, level):
        for way in (1, -1):
            if (c, way, level) in departures:
                slot, copies = departures.pop((c, way, level))
                arrive(c, [slot])
                for copy in copies:
                    copy.start()

    label_swap = [
        remote(label_out, label_in.at[i], part_ssem.at[i], part_rsem.at[i], to)
        for i, to in enumerate(partners)
    ]
    swap = []
    for f in range(2):
        for i in range(NC):
            n = NC * f + i
            swap.append(
                remote(
                    terms.at[2 * (core ^ i) + f], ring.at[0, pl.ds(FLUX + n * ROWS, ROWS)],
                    part_ssem.at[2 + n], part_rsem.at[2 + n], partners[i],
                )
            )
    for copy in (*label_swap, *swap):
        copy.start()

    depart(WATER, 1)

    halo = [
        remote(hs_dn, hr_up, halo_ssem.at[0], halo_rsem.at[0], after),
        remote(hs_up, hr_dn, halo_ssem.at[1], halo_rsem.at[1], before),
    ]
    for copy in halo:
        copy.start()


    def kab_work():
        k4 = kron_h[:, : 8 * FIELDS].astype(F32) + kron_l[:, : 8 * FIELDS].astype(F32)
        eye = (iota(k4.shape, 0) == iota(k4.shape, 1)).astype(F32)
        q = jnp.concatenate([k4 + eye, dcol[:, : 8 * FIELDS] * k4], axis=1)
        kh, kl = split(mm3((kron_h[...], kron_l[...]), split(q)))
        kab[...] = jnp.concatenate([kh, kh, kl], axis=1)

    first = me == 0
    last = me == N_DOM - 1

    def apply(*groups):
        u = jnp.concatenate([u.reshape(PAD * 8, COLS) for u in groups], axis=1)
        out = mm3((kron_h[...], kron_l[...]), split(u))
        return [
            out[:, COLS * i : COLS * (i + 1)].reshape(PAD, 8, COLS) for i in range(len(groups))
        ]

    def diffused(i, source):
        x = source[i]
        lap = laplacian(x, source[i - 1, :, 7:8], source[i + 1, :, 0:1])
        return x + dcol[...].reshape(PAD, 8, COLS) * lap

    def step_one(i, j):
        base1[i], base1[j] = apply(diffused(i, st), diffused(j, st))

    def step_two(i, j):
        base2[i - 1], base2[j - 1] = apply(diffused(i, base1), diffused(j, base1))

    def step_one_ends():
        d = dcol[...].reshape(PAD, 8, COLS)
        spot = iota((PAD, 8, COLS), 1)
        above, below = st[0], st[GROUPS + 1]
        x = jnp.where(spot == 7, above[:, 7:8], below[:, 0:1])
        outer = jnp.where(spot == 7, above[:, 6:7], below[:, 1:2])
        inner = jnp.where(spot == 7, st[1, :, 0:1], st[GROUPS, :, 7:8])
        u = x + d * (outer + inner + neighbours_in_columns(x) - 4.0 * x)
        gone = ((spot == 7) & first) | ((spot < 7) & last)
        (ends,) = apply(jnp.where(gone, 0.0, u))
        base1[0] = ends
        base1[GROUPS + 1] = ends

    step_one(2, 3)
    depart(WATER, 2)
    for i, copy in enumerate(label_swap):
        copy.wait_recv()
        ring[0, FLUX_LABEL + i : FLUX_LABEL + i + 1, :] = label_in[i]
    for c in (FIELD_A, FIELD_B):
        for copy in swap[NC * (c - 1) : NC * c]:
            copy.wait_recv()
        depart(c, 1)
    depart(WATER, 3)

    def joined(rows):
        lane = iota((1, COLS), 1) >> 5
        names = rows[0]
        for i in range(1, 4):
            names = jnp.where(lane == i, rows[i], names)
        return names

    def one_hot(rows, names):
        return (rows == jnp.broadcast_to(names, rows.shape)).astype(F32).astype(BF16)

    selected = {}

    def select_flux(j):
        if j not in selected:
            selected[j] = make_selection(j)
        return selected[j]

    def make_selection(j):
        arrive(FIELD_A, (2 * j, 2 * j + 1))
        rows = []
        for i in range(4):
            row = FLUX_LABEL + i % 2
            rows.append(ring[2 * j + i // 2, row : row + 1, :])
        return one_hot(row_of[...], joined(rows))

    def rows_of(f, slots):
        start = FLUX + f * NC * ROWS
        arrive((FIELD_A, FIELD_B)[f], slots)
        return jnp.concatenate([ring[n, start : start + NC * ROWS, :] for n in slots], axis=0)

    def place_flux(first_slot, last_slot, fields, fresh):
        sel = [select_flux(j) for j in range(first_slot // 2, last_slot // 2)]
        data = [rows_of(f, range(first_slot, last_slot)) for f in fields]
        high, low = split(jnp.concatenate(data, axis=1))
        part = mm(jnp.concatenate([*sel, *sel], axis=1), jnp.concatenate([high, low], axis=0))
        for i, f in enumerate(fields):
            one = part[:, i * COLS : (i + 1) * COLS]
            rows = slice(f * ROWS, (f + 1) * ROWS)
            main = one[:MAIN].reshape(GROUP, ROWS, COLS)
            flux_send[:, rows, :] = main if fresh else flux_send[:, rows, :] + main
            ends_acc[f] = one[MAIN:] if fresh else ends_acc[f] + one[MAIN:]

    def place_water():
        arrive(WATER, range(SLOTS))
        rows = [ring[slot, :WATER_LABEL, :] for slot in range(SLOTS)]
        high, low = split(jnp.concatenate(rows, axis=0))
        labels = [ring[slot, WATER_LABEL : WATER_LABEL + 1, :] for slot in range(SLOTS)]
        sel = [
            one_hot(row_of[:MAIN], joined(labels[4 * g : 4 * g + 4])) for g in range(SLOTS // 4)
        ]
        part = mm(jnp.concatenate([*sel, *sel], axis=1), jnp.concatenate([high, low], axis=0))
        run_send[...] = part.reshape(GROUP, ROWS, COLS)
        for copy in water_scatter:
            copy.start()

    order = [4, 5, 2, 3, 6, 7, 1]

    def scatter_copies(src, dst, c, rows):
        return [
            remote(src.at[b, rows], dst.at[b, rows], rs_ssem.at[c], rs_rsem.at[c], member(b))
            for b in order
        ]

    def whole(src, dst, c, rows):
        others = pl.ds(1, GROUP - 1)
        return remote(
            src.at[others, rows], dst.at[others, rows], rs_ssem.at[c], rs_rsem.at[c], member(1)
        )

    kinds = [
        (run_send, run_recv, 0, pl.ds(0, ROWS)),
        (flux_send, flux_recv, 1, pl.ds(0, ROWS)),
        (flux_send, flux_recv, 2, pl.ds(ROWS, BLOCK - ROWS)),
    ]
    water_scatter, *flux_scatter = [scatter_copies(*kind) for kind in kinds]
    water_whole, *flux_whole = [whole(*kind) for kind in kinds]

    for level in range(2, LEVELS + 1):
        depart(FIELD_A, level)
        depart(FIELD_B, level)
        depart(WATER, level + 2)
        if level == LEVELS:
            place_water()
    place_flux(0, 10, (0, 1), True)
    for f in range(2):
        place_flux(10, SLOTS, (f,), False)
        if f == 1:
            for b in range(GROUP):
                for e in range(2):
                    ends = 2 * ROWS + 2 * e
                    flux_send[b, ends : ends + 2, :] = ends_acc[e, 2 * b : 2 * b + 2]
        for copy in flux_scatter[f]:
            copy.start()

    for copy in halo:
        copy.wait_recv()
    st[0, :, 6:8, :] = jnp.where(first, 0.0, hr_up[...])
    st[GROUPS + 1, :, 0:2, :] = jnp.where(last, 0.0, hr_dn[...])
    step_one(1, 4)
    step_one_ends()
    step_two(1, 2)
    step_two(3, 4)
    kab_work()
    for copy in (*label_swap, *swap, *halo):
        copy.wait_send()
    every = ring.at[pl.ds(1, SLOTS - 1)]
    remote(every, every, ring_ssem, ring_rsem.at[0, 0], along(1)).wait_send()

    loads[14].wait()
    water_whole.wait_recv()
    water = run_send[0]
    for b in range(1, GROUP):
        water = water + run_recv[b]
    river[...] = store[...] + water

    for copy in flux_whole:
        copy.wait_recv()

    same, other = flux_send[0], flux_recv[1]
    for b in range(2, GROUP, 2):
        same = same + flux_recv[b]
        other = other + flux_recv[b + 1]
    pair = [jnp.where(core == 0, same, other), jnp.where(core == 0, other, same)]

    g4 = jnp.stack(
        [frac[...] * pair[f // 2][(f % 2) * ROWS : (f % 2 + 1) * ROWS] for f in range(FIELDS)],
        axis=0,
    )
    ends = [pair[f // 2][2 * ROWS + 2 * (f % 2) : 2 * ROWS + 2 * (f % 2) + 2] for f in range(FIELDS)]
    frac_above = jnp.where(first, 0.0, hr_up[LEV, 1:2, :])
    frac_below = jnp.where(last, 0.0, hr_dn[LEV, 0:1, :])
    above = jnp.stack([frac_above * x[0:1] for x in ends], axis=0)
    below = jnp.stack([frac_below * x[1:2] for x in ends], axis=0)
    lap = laplacian(g4, above, below)
    for i in range(GROUPS):
        high, low = split(
            jnp.concatenate(
                [x[:, 8 * i : 8 * i + 8].reshape(8 * FIELDS, COLS) for x in (g4, lap)], axis=0
            )
        )
        forced[i] = jnp.concatenate([high, low, high], axis=0)

    for copy in (*flux_whole, water_whole):
        copy.wait_send()


def finish(base2, kab, forced, river, out_h, river_h, out, sems):
    river_copy = pltpu.make_async_copy(river, river_h.at[0], sems.at[GROUPS])
    river_copy.start()
    copies = []
    for i in range(0, GROUPS, 2):
        delta = mm(kab[...], jnp.concatenate([forced[i], forced[i + 1]], axis=1))
        for j in range(2):
            part = delta[:, COLS * j : COLS * (j + 1)].reshape(PAD, 8, COLS)
            out[i + j] = base2[i + j] + part
            copies.append(
                pltpu.make_async_copy(
                    out.at[i + j, pl.ds(0, LEV)],
                    out_h.at[0, :, pl.ds(8 * (i + j), 8)],
                    sems.at[i + j],
                )
            )
            copies[-1].start()
    for copy in (*copies, river_copy):
        copy.wait()


def shards(
    state, frac, diff, ops, weight, fo, fr, fb, ro, rr, rb, store,
):
    ops = jnp.transpose(ops, (1, 0, 2))
    fo, ro = fo.reshape(1, ROWS), ro.reshape(1, ROWS)
    args = (state, frac, diff, ops, weight, fo, fr, fb, ro, rr, rb, store)
    args = [pltpu.with_memory_space_constraint(x, pltpu.HBM) for x in args]
    vmem = pltpu.VMEM
    far = pl.BlockSpec(memory_space=pltpu.HBM)
    near = pl.BlockSpec(memory_space=vmem)
    dma = pltpu.SemaphoreType.DMA
    i32 = jnp.int32
    inner = pl.pallas_call(
        kernel,
        out_shape=(
            vmem((GROUPS, PAD, 8, COLS), F32),
            vmem((PAD * 8, 3 * 16 * FIELDS), BF16),
            vmem((GROUPS, 3 * 16 * FIELDS, COLS), BF16),
            vmem((ROWS, COLS), F32),
        ),
        in_specs=[far] * 12,
        out_specs=(near,) * 4,
        scratch_shapes=[
            vmem((GROUPS + 2, PAD, 8, COLS), F32),
            vmem((ROWS, COLS), F32),
            vmem((1, LEV), F32),
            vmem((LEV, 1, LEV), F32),
            vmem((NW, COLS, COLS), F32),
            vmem((1, ROWS), i32),
            vmem((1, ROWS), i32),
            vmem((1, ROWS), i32),
            vmem((1, ROWS), i32),
            vmem((1, ROWS), i32),
            vmem((1, ROWS), i32),
            vmem((ROWS, COLS), F32),
            dma((15,)),
            vmem((PAD, 2, COLS), F32),
            vmem((PAD, 2, COLS), F32),
            vmem((PAD, 2, COLS), F32),
            vmem((PAD, 2, COLS), F32),
            dma((2,)),
            dma((2,)),
            vmem((FIELDS, ROWS, COLS), F32),
            vmem((1, COLS), F32),
            vmem((2, 1, COLS), F32),
            dma((2 + 2 * NC,)),
            dma((2 + 2 * NC,)),
            vmem((SLOTS, SLOT, COLS), F32),
            dma(()),
            dma((len(PIECES), SLOTS)),
            vmem((MAIN + EDGE, COLS), F32),
            vmem((2, EDGE, COLS), F32),
            vmem((GROUP, BLOCK, COLS), F32),
            vmem((GROUP, BLOCK, COLS), F32),
            vmem((GROUP, ROWS, COLS), F32),
            vmem((GROUP, ROWS, COLS), F32),
            dma((3,)),
            dma((3,)),
            vmem((PAD * 8, COLS), F32),
            vmem((PAD * 8, PAD * 8), BF16),
            vmem((PAD * 8, PAD * 8), BF16),
            vmem((GROUPS + 2, PAD, 8, COLS), F32),
        ],
        compiler_params=pltpu.CompilerParams(
            collective_id=0, has_side_effects=True, vmem_limit_bytes=32 * 1024 * 1024
        ),
        name="coupling",
    )(*args)
    inner = [pltpu.with_memory_space_constraint(x, vmem) for x in inner]
    return pl.pallas_call(
        finish,
        out_shape=(
            pltpu.HBM((1, LEV, ROWS, COLS), F32),
            pltpu.HBM((1, ROWS, COLS), F32),
        ),
        in_specs=[near] * 4,
        out_specs=(far, far),
        scratch_shapes=[vmem((GROUPS, PAD, 8, COLS), F32), dma((GROUPS + 1,))],
        compiler_params=pltpu.CompilerParams(vmem_limit_bytes=16 * 1024 * 1024),
        name="finish",
    )(*inner)


def solution(mesh):
    in_specs = (
        P("sec", None, "dom", None),
        P("sec", "dom", None),
        P("sec", None),
        P("sec", None, None),
        P("sec", "dom", None, None),
        P("sec", "dom", None),
        P("sec", "dom"),
        P("sec", "dom"),
        P("sec", "dom", None),
        P("sec", "dom"),
        P("sec", "dom"),
        P("sec", "dom", None),
    )
    out_specs = (P("sec", None, "dom", None), P("sec", "dom", None))
    return jax.shard_map(shards, mesh=mesh, in_specs=in_specs, out_specs=out_specs, check_vma=False)
```

```python
import jax
import jax.numpy as jnp
from jax import lax
from jax.experimental import pallas as pl
from jax.experimental.pallas import tpu as pltpu
from jax.sharding import PartitionSpec as P

MESH = pl.DeviceIdType.MESH
F32 = jnp.float32
BF16 = jnp.bfloat16

LEV = 30
PAD = 32
COLS = 128
ROWS = 32
FIELDS = 4
NW = 8
NY, NZ, NC = 4, 16, 2
N_DOM = NY * NZ * NC
GROUP = NY * NC
HALF = NZ // 2
SLOTS = NZ
GROUPS = ROWS // 8
MAIN = GROUP * ROWS
EDGE = GROUP * 2
WATER_LABEL = ROWS
FLUX_LABEL = WATER_LABEL + 8
FLUX = FLUX_LABEL + 8
SLOT = FLUX + 2 * NC * ROWS
WATER, FLUX_PIECES = 0, (1, 2, 3, 4)
PIECES = (
    (0, FLUX_LABEL),
    (FLUX_LABEL, 8 + ROWS),
    *[(FLUX + n * ROWS, ROWS) for n in range(1, 2 * NC)],
)
BLOCK = 2 * ROWS + 8


def tree(jumps):
    levels, reached = {}, 0
    for level, jump in enumerate(jumps, 1):
        levels[level] = [(reached, reached + i) for i in range(jump, 0, -1)]
        reached += jump
    return levels


WATER_TREES = tree((2, 1, 2, 1, 2)), tree((1, 2, 1, 2, 1))
FLUX_TREES = tree((2, 2, 2, 2)), tree((1, 2, 2, 2))
LEVELS = len(FLUX_TREES[0])


def split(x):
    high = x.astype(BF16)
    return high, (x - high.astype(F32)).astype(BF16)


def mm(a, b):
    return jnp.dot(a, b, preferred_element_type=F32)


def mm3(a, b):
    (ah, al), (bh, bl) = a, b
    return mm(ah, bh) + (mm(ah, bl) + mm(al, bh))


def iota(shape, dim):
    return lax.broadcasted_iota(jnp.int32, shape, dim)


def neighbours_in_columns(x):
    axis = x.ndim - 1
    return pltpu.roll(x, 1, axis) + pltpu.roll(x, COLS - 1, axis)


def laplacian(x, above, below):
    row, count = iota(x.shape, 1), x.shape[1]
    down = jnp.where(row == 0, above, pltpu.roll(x, 1, 1))
    up = jnp.where(row == count - 1, below, pltpu.roll(x, count - 1, 1))
    return down + up + neighbours_in_columns(x) - 4.0 * x


def kernel(
    state_h, frac_h, diff_h, ops_h, weight_h, fo_h, fr_h, fb_h, ro_h, rr_h, rb_h, store_h,
    base2, kab, forced, river,
    st, frac, diff, ops, weight, fo, fr, fb, ro, rr, rb, store,
    local_sem,
    hs_up, hs_dn, hr_up, hr_dn, halo_ssem, halo_rsem,
    terms, label_out, label_in, part_ssem, part_rsem,
    ring, ring_ssem, ring_rsem, row_of, ends_acc,
    flux_send, flux_recv, run_send, run_recv, rs_ssem, rs_rsem,
    dcol, kron_h, kron_l, base1,
):
    sec = lax.axis_index("sec")
    me = lax.axis_index("dom")
    core = me & (NC - 1)
    z = (me >> 1) & (NZ - 1)
    y = me >> 5

    def dom_of(yy, zz, cc):
        return (yy * NZ + zz) * NC + cc

    def along(distance):
        return (sec, dom_of(y, (z + NZ + distance) & (NZ - 1), core))

    partners = [(sec ^ 2, me), (sec ^ 2, me ^ 1)]
    after = (sec, (me + 1) & (N_DOM - 1))
    before = (sec, (me + N_DOM - 1) & (N_DOM - 1))

    def member(b):
        return (sec, dom_of((y + b // NC) & (NY - 1), z, core ^ (b % NC)))

    barrier = pltpu.get_barrier_semaphore()
    peers = [*partners, *[along(d) for d in (1, -1, 2, -2)], after, before]
    peers += [member(b) for b in range(1, GROUP)]
    for peer in peers:
        pl.semaphore_signal(barrier, inc=1, device_id=peer, device_id_type=MESH)

    pairs = [(weight_h.at[0], weight)]
    pairs += [
        (state_h.at[0, :, pl.ds(8 * i, 8)], st.at[1 + i, pl.ds(0, LEV)]) for i in range(GROUPS)
    ]
    pairs += [
        (fb_h, fb), (rb_h, rb), (fo_h, fo), (fr_h, fr), (ro_h, ro), (rr_h, rr),
        (frac_h.at[0], frac), (ops_h, ops), (diff_h, diff), (store_h.at[0], store),
    ]
    loads = [pltpu.make_async_copy(a, b, local_sem.at[i]) for i, (a, b) in enumerate(pairs)]
    for copy in loads:
        copy.start()

    for copy in loads[5:11]:
        copy.wait()

    def label_of(owner, row):
        eye = iota((ROWS, ROWS), 0) == iota((ROWS, ROWS), 1)
        target = (owner[...] * ROWS + row[...]).astype(F32)
        rows = jnp.broadcast_to(target, (ROWS, ROWS))
        column = jnp.sum(jnp.where(eye, rows, 0.0), axis=1, keepdims=True)
        wide = jnp.broadcast_to(column, (ROWS, COLS))
        place = iota((ROWS, COLS), 0) == (iota((ROWS, COLS), 1) & (ROWS - 1))
        return jnp.sum(jnp.where(place, wide, 0.0), axis=0, keepdims=True)

    label_out[...] = label_of(fo, fr)
    ring[0, WATER_LABEL:FLUX_LABEL, :] = jnp.broadcast_to(label_of(ro, rr), (8, COLS))
    ring[0, FLUX_LABEL:FLUX, :] = jnp.zeros((8, COLS), F32)

    tall = FIELDS * ROWS + ROWS
    spot = (iota((tall, ROWS), 0) & (ROWS - 1)) == iota((tall, ROWS), 1)
    blocks = jnp.where(
        iota((tall, ROWS), 0) < FIELDS * ROWS,
        jnp.broadcast_to(fb[...].astype(F32), (tall, ROWS)),
        jnp.broadcast_to(rb[...].astype(F32), (tall, ROWS)),
    )
    block = jnp.sum(jnp.where(spot, blocks, 0.0), axis=1, keepdims=True)
    block = jnp.broadcast_to(jnp.concatenate([block, block], axis=0), (2 * tall, COLS))
    for copy in loads[1:5]:
        copy.wait()
    surface = jnp.concatenate(
        [st[1 + i, f] for f in (*range(FIELDS), 0) for i in range(GROUPS)], axis=0
    )
    high = surface.astype(BF16).astype(F32)
    both = jnp.concatenate([high, surface - high], axis=0)
    lhs = jnp.concatenate(
        [jnp.where(block == float(w), both, 0.0).astype(BF16) for w in range(NW)], axis=1
    )
    loads[0].wait()
    rhs = jnp.concatenate(split(weight[...].reshape(NW * COLS, COLS)), axis=1)
    total = mm(lhs, rhs)
    result = total[:tall, :COLS] + (total[:tall, COLS:] + total[tall:, :COLS])
    terms[...] = result[: FIELDS * ROWS].reshape(FIELDS, ROWS, COLS)
    ring[0, :WATER_LABEL, :] = result[FIELDS * ROWS :]

    pl.semaphore_wait(barrier, len(peers))

    def remote(src, dst, ssem, rsem, device):
        return pltpu.make_async_remote_copy(
            src_ref=src, dst_ref=dst, send_sem=ssem, recv_sem=rsem,
            device_id=device, device_id_type=MESH,
        )

    def slot_of(way, distance):
        return 0 if distance == 0 else min(2 * distance - (way > 0), SLOTS - 1)

    def piece(c, slot):
        return ring.at[slot, pl.ds(*PIECES[c])]

    def hop(c, way, start, end):
        slot = slot_of(way, end)
        return remote(
            piece(c, slot_of(way, start)), piece(c, slot),
            ring_ssem, ring_rsem.at[c, slot], along(way * (end - start)),
        )

    arrivals, departures = {}, {}
    for c in range(len(PIECES)):
        for way in (1, -1):
            trees = WATER_TREES if c == WATER else FLUX_TREES
            levels = trees[(c % 2 == 0) != (way > 0)]
            for level, edges in levels.items():
                copies = [hop(c, way, *edge) for edge in edges]
                departures[c, way, level] = (slot_of(way, edges[0][0]), copies)
                for copy, (_, end) in zip(copies, edges):
                    arrivals[c, slot_of(way, end)] = copy

    def arrive(c, slots):
        for slot in slots:
            if (c, slot) in arrivals:
                arrivals.pop((c, slot)).wait_recv()

    def depart(c, level):
        for way in (1, -1):
            if (c, way, level) in departures:
                slot, copies = departures.pop((c, way, level))
                arrive(c, [slot])
                for copy in copies:
                    copy.start()

    label_swap = [
        remote(label_out, label_in.at[i], part_ssem.at[i], part_rsem.at[i], to)
        for i, to in enumerate(partners)
    ]
    swap = []
    for f in range(2):
        for i in range(NC):
            n = NC * f + i
            swap.append(
                remote(
                    terms.at[2 * (core ^ i) + f], ring.at[0, pl.ds(FLUX + n * ROWS, ROWS)],
                    part_ssem.at[2 + n], part_rsem.at[2 + n], partners[i],
                )
            )
    for copy in (*label_swap, *swap):
        copy.start()

    depart(WATER, 1)

    loads[11].wait()
    hs_up[0:LEV] = st[1, 0:LEV, 0:2, :]
    hs_dn[0:LEV] = st[GROUPS, 0:LEV, 6:8, :]
    hs_up[LEV] = frac[0:2, :]
    hs_dn[LEV] = frac[ROWS - 2 : ROWS, :]
    hs_up[LEV + 1] = jnp.zeros((2, COLS), F32)
    hs_dn[LEV + 1] = jnp.zeros((2, COLS), F32)
    for i in range(GROUPS):
        st[1 + i, LEV:PAD] = jnp.zeros((PAD - LEV, 8, COLS), F32)
    halo = [
        remote(hs_dn, hr_up, halo_ssem.at[0], halo_rsem.at[0], after),
        remote(hs_up, hr_dn, halo_ssem.at[1], halo_rsem.at[1], before),
    ]
    for copy in halo:
        copy.start()


    tall8 = PAD * 8
    for copy in loads[12:14]:
        copy.wait()
    pick = ((iota((tall8, LEV), 0) >> 3) == iota((tall8, LEV), 1)).astype(F32)
    pick_t = ((iota((LEV, tall8), 1) >> 3) == iota((LEV, tall8), 0)).astype(BF16)
    column = jnp.sum(pick * jnp.broadcast_to(diff[...], (tall8, LEV)), axis=1, keepdims=True)
    dcol[...] = jnp.broadcast_to(column, (tall8, COLS))
    op = ops[:, 0, :]
    op_h, op_l = split(op)
    op_r = (op - op_h.astype(F32) - op_l.astype(F32)).astype(BF16)
    pick = pick.astype(BF16)
    spread = mm(mm(pick, op_h).astype(BF16), pick_t) + (
        mm(mm(pick, op_l).astype(BF16), pick_t) + mm(mm(pick, op_r).astype(BF16), pick_t)
    )
    same8 = (iota((tall8, tall8), 0) & 7) == (iota((tall8, tall8), 1) & 7)
    kh, kl = split(jnp.where(same8, spread, 0.0))
    kron_h[...] = kh
    kron_l[...] = kl

    def block_start(b):
        return dom_of((y + (b >> 1)) & (NY - 1), z, core ^ (b & 1)) * ROWS

    i = iota((MAIN, COLS), 0)
    row_of[:MAIN] = (block_start(i >> 5) + (i & (ROWS - 1))).astype(F32)
    i = iota((EDGE, COLS), 0)
    row_of[MAIN:] = (block_start(i >> 1) + jnp.where((i & 1) == 0, -1, ROWS)).astype(F32)
    flux_send[:, 2 * ROWS + 4 :, :] = jnp.zeros((GROUP, 4, COLS), F32)

    def kab_work():
        k4 = kron_h[:, : 8 * FIELDS].astype(F32) + kron_l[:, : 8 * FIELDS].astype(F32)
        eye = (iota(k4.shape, 0) == iota(k4.shape, 1)).astype(F32)
        q = jnp.concatenate([k4 + eye, dcol[:, : 8 * FIELDS] * k4], axis=1)
        kh, kl = split(mm3((kron_h[...], kron_l[...]), split(q)))
        kab[...] = jnp.concatenate([kh, kh, kl], axis=1)

    first = me == 0
    last = me == N_DOM - 1

    def apply(*groups):
        u = jnp.concatenate([u.reshape(PAD * 8, COLS) for u in groups], axis=1)
        out = mm3((kron_h[...], kron_l[...]), split(u))
        return [
            out[:, COLS * i : COLS * (i + 1)].reshape(PAD, 8, COLS) for i in range(len(groups))
        ]

    def diffused(i, source):
        x = source[i]
        lap = laplacian(x, source[i - 1, :, 7:8], source[i + 1, :, 0:1])
        return x + dcol[...].reshape(PAD, 8, COLS) * lap

    def step_one(i, j):
        base1[i], base1[j] = apply(diffused(i, st), diffused(j, st))

    def step_two(i, j):
        base2[i - 1], base2[j - 1] = apply(diffused(i, base1), diffused(j, base1))

    def step_one_ends():
        d = dcol[...].reshape(PAD, 8, COLS)
        spot = iota((PAD, 8, COLS), 1)
        above, below = st[0], st[GROUPS + 1]
        x = jnp.where(spot == 7, above[:, 7:8], below[:, 0:1])
        outer = jnp.where(spot == 7, above[:, 6:7], below[:, 1:2])
        inner = jnp.where(spot == 7, st[1, :, 0:1], st[GROUPS, :, 7:8])
        u = x + d * (outer + inner + neighbours_in_columns(x) - 4.0 * x)
        gone = ((spot == 7) & first) | ((spot < 7) & last)
        (ends,) = apply(jnp.where(gone, 0.0, u))
        base1[0] = ends
        base1[GROUPS + 1] = ends

    step_one(2, 3)
    depart(WATER, 2)
    for i, copy in enumerate(label_swap):
        copy.wait_recv()
        ring[0, FLUX_LABEL + i : FLUX_LABEL + i + 1, :] = label_in[i]
    for c in FLUX_PIECES:
        swap[c - 1].wait_recv()
        depart(c, 1)
    depart(WATER, 3)

    def joined(rows):
        lane = iota((1, COLS), 1) >> 5
        names = rows[0]
        for i in range(1, 4):
            names = jnp.where(lane == i, rows[i], names)
        return names

    def one_hot(rows, names):
        return (rows == jnp.broadcast_to(names, rows.shape)).astype(F32).astype(BF16)

    selected = {}

    def select_flux(j):
        if j not in selected:
            selected[j] = make_selection(j)
        return selected[j]

    def make_selection(j):
        arrive(FLUX_PIECES[0], (2 * j, 2 * j + 1))
        rows = []
        for i in range(4):
            row = FLUX_LABEL + i % 2
            rows.append(ring[2 * j + i // 2, row : row + 1, :])
        return one_hot(row_of[...], joined(rows))

    def rows_of(f, slots):
        start = FLUX + f * NC * ROWS
        for c in FLUX_PIECES[NC * f : NC * (f + 1)]:
            arrive(c, slots)
        return jnp.concatenate([ring[n, start : start + NC * ROWS, :] for n in slots], axis=0)

    def place_flux(first_slot, last_slot, fields, fresh):
        sel = [select_flux(j) for j in range(first_slot // 2, last_slot // 2)]
        data = [rows_of(f, range(first_slot, last_slot)) for f in fields]
        high, low = split(jnp.concatenate(data, axis=1))
        part = mm(jnp.concatenate([*sel, *sel], axis=1), jnp.concatenate([high, low], axis=0))
        for i, f in enumerate(fields):
            one = part[:, i * COLS : (i + 1) * COLS]
            rows = slice(f * ROWS, (f + 1) * ROWS)
            main = one[:MAIN].reshape(GROUP, ROWS, COLS)
            flux_send[:, rows, :] = main if fresh else flux_send[:, rows, :] + main
            ends_acc[f] = one[MAIN:] if fresh else ends_acc[f] + one[MAIN:]

    def place_water():
        arrive(WATER, range(SLOTS))
        rows = [ring[slot, :WATER_LABEL, :] for slot in range(SLOTS)]
        high, low = split(jnp.concatenate(rows, axis=0))
        labels = [ring[slot, WATER_LABEL : WATER_LABEL + 1, :] for slot in range(SLOTS)]
        sel = [
            one_hot(row_of[:MAIN], joined(labels[4 * g : 4 * g + 4])) for g in range(SLOTS // 4)
        ]
        part = mm(jnp.concatenate([*sel, *sel], axis=1), jnp.concatenate([high, low], axis=0))
        run_send[...] = part.reshape(GROUP, ROWS, COLS)
        for copy in water_scatter:
            copy.start()

    order = [4, 5, 2, 3, 6, 7, 1]

    def scatter_copies(src, dst, c, rows):
        return [
            remote(src.at[b, rows], dst.at[b, rows], rs_ssem.at[c], rs_rsem.at[c], member(b))
            for b in order
        ]

    def whole(src, dst, c, rows):
        others = pl.ds(1, GROUP - 1)
        return remote(
            src.at[others, rows], dst.at[others, rows], rs_ssem.at[c], rs_rsem.at[c], member(1)
        )

    kinds = [
        (run_send, run_recv, 0, pl.ds(0, ROWS)),
        (flux_send, flux_recv, 1, pl.ds(0, ROWS)),
        (flux_send, flux_recv, 2, pl.ds(ROWS, BLOCK - ROWS)),
    ]
    water_scatter, *flux_scatter = [scatter_copies(*kind) for kind in kinds]
    water_whole, *flux_whole = [whole(*kind) for kind in kinds]

    for level in range(2, LEVELS + 1):
        for c in FLUX_PIECES:
            depart(c, level)
        depart(WATER, level + 2)
        if level == LEVELS:
            place_water()
    place_flux(0, 10, (0, 1), True)
    for f in range(2):
        place_flux(10, SLOTS, (f,), False)
        if f == 1:
            for b in range(GROUP):
                for e in range(2):
                    ends = 2 * ROWS + 2 * e
                    flux_send[b, ends : ends + 2, :] = ends_acc[e, 2 * b : 2 * b + 2]
        for copy in flux_scatter[f]:
            copy.start()

    for copy in halo:
        copy.wait_recv()
    st[0, :, 6:8, :] = jnp.where(first, 0.0, hr_up[...])
    st[GROUPS + 1, :, 0:2, :] = jnp.where(last, 0.0, hr_dn[...])
    step_one(1, 4)
    step_one_ends()
    step_two(1, 2)
    step_two(3, 4)
    kab_work()
    for copy in (*label_swap, *swap, *halo):
        copy.wait_send()
    every = ring.at[pl.ds(1, SLOTS - 1)]
    remote(every, every, ring_ssem, ring_rsem.at[0, 0], along(1)).wait_send()

    loads[14].wait()
    water_whole.wait_recv()
    water = run_send[0]
    for b in range(1, GROUP):
        water = water + run_recv[b]
    river[...] = store[...] + water

    for copy in flux_whole:
        copy.wait_recv()

    same, other = flux_send[0], flux_recv[1]
    for b in range(2, GROUP, 2):
        same = same + flux_recv[b]
        other = other + flux_recv[b + 1]
    pair = [jnp.where(core == 0, same, other), jnp.where(core == 0, other, same)]

    g4 = jnp.stack(
        [frac[...] * pair[f // 2][(f % 2) * ROWS : (f % 2 + 1) * ROWS] for f in range(FIELDS)],
        axis=0,
    )
    ends = [pair[f // 2][2 * ROWS + 2 * (f % 2) : 2 * ROWS + 2 * (f % 2) + 2] for f in range(FIELDS)]
    frac_above = jnp.where(first, 0.0, hr_up[LEV, 1:2, :])
    frac_below = jnp.where(last, 0.0, hr_dn[LEV, 0:1, :])
    above = jnp.stack([frac_above * x[0:1] for x in ends], axis=0)
    below = jnp.stack([frac_below * x[1:2] for x in ends], axis=0)
    lap = laplacian(g4, above, below)
    for i in range(GROUPS):
        high, low = split(
            jnp.concatenate(
                [x[:, 8 * i : 8 * i + 8].reshape(8 * FIELDS, COLS) for x in (g4, lap)], axis=0
            )
        )
        forced[i] = jnp.concatenate([high, low, high], axis=0)

    for copy in (*flux_whole, water_whole):
        copy.wait_send()


def finish(base2, kab, forced, river, out_h, river_h, out, sems):
    river_copy = pltpu.make_async_copy(river, river_h.at[0], sems.at[GROUPS])
    river_copy.start()
    copies = []
    for i in range(0, GROUPS, 2):
        delta = mm(kab[...], jnp.concatenate([forced[i], forced[i + 1]], axis=1))
        for j in range(2):
            part = delta[:, COLS * j : COLS * (j + 1)].reshape(PAD, 8, COLS)
            out[i + j] = base2[i + j] + part
            copies.append(
                pltpu.make_async_copy(
                    out.at[i + j, pl.ds(0, LEV)],
                    out_h.at[0, :, pl.ds(8 * (i + j), 8)],
                    sems.at[i + j],
                )
            )
            copies[-1].start()
    for copy in (*copies, river_copy):
        copy.wait()


def shards(
    state, frac, diff, ops, weight, fo, fr, fb, ro, rr, rb, store,
):
    ops = jnp.transpose(ops, (1, 0, 2))
    fo, ro = fo.reshape(1, ROWS), ro.reshape(1, ROWS)
    args = (state, frac, diff, ops, weight, fo, fr, fb, ro, rr, rb, store)
    args = [pltpu.with_memory_space_constraint(x, pltpu.HBM) for x in args]
    vmem = pltpu.VMEM
    far = pl.BlockSpec(memory_space=pltpu.HBM)
    near = pl.BlockSpec(memory_space=vmem)
    dma = pltpu.SemaphoreType.DMA
    i32 = jnp.int32
    inner = pl.pallas_call(
        kernel,
        out_shape=(
            vmem((GROUPS, PAD, 8, COLS), F32),
            vmem((PAD * 8, 3 * 16 * FIELDS), BF16),
            vmem((GROUPS, 3 * 16 * FIELDS, COLS), BF16),
            vmem((ROWS, COLS), F32),
        ),
        in_specs=[far] * 12,
        out_specs=(near,) * 4,
        scratch_shapes=[
            vmem((GROUPS + 2, PAD, 8, COLS), F32),
            vmem((ROWS, COLS), F32),
            vmem((1, LEV), F32),
            vmem((LEV, 1, LEV), F32),
            vmem((NW, COLS, COLS), F32),
            vmem((1, ROWS), i32),
            vmem((1, ROWS), i32),
            vmem((1, ROWS), i32),
            vmem((1, ROWS), i32),
            vmem((1, ROWS), i32),
            vmem((1, ROWS), i32),
            vmem((ROWS, COLS), F32),
            dma((15,)),
            vmem((PAD, 2, COLS), F32),
            vmem((PAD, 2, COLS), F32),
            vmem((PAD, 2, COLS), F32),
            vmem((PAD, 2, COLS), F32),
            dma((2,)),
            dma((2,)),
            vmem((FIELDS, ROWS, COLS), F32),
            vmem((1, COLS), F32),
            vmem((2, 1, COLS), F32),
            dma((2 + 2 * NC,)),
            dma((2 + 2 * NC,)),
            vmem((SLOTS, SLOT, COLS), F32),
            dma(()),
            dma((len(PIECES), SLOTS)),
            vmem((MAIN + EDGE, COLS), F32),
            vmem((2, EDGE, COLS), F32),
            vmem((GROUP, BLOCK, COLS), F32),
            vmem((GROUP, BLOCK, COLS), F32),
            vmem((GROUP, ROWS, COLS), F32),
            vmem((GROUP, ROWS, COLS), F32),
            dma((3,)),
            dma((3,)),
            vmem((PAD * 8, COLS), F32),
            vmem((PAD * 8, PAD * 8), BF16),
            vmem((PAD * 8, PAD * 8), BF16),
            vmem((GROUPS + 2, PAD, 8, COLS), F32),
        ],
        compiler_params=pltpu.CompilerParams(
            collective_id=0, has_side_effects=True, vmem_limit_bytes=32 * 1024 * 1024
        ),
        name="coupling",
    )(*args)
    inner = [pltpu.with_memory_space_constraint(x, vmem) for x in inner]
    return pl.pallas_call(
        finish,
        out_shape=(
            pltpu.HBM((1, LEV, ROWS, COLS), F32),
            pltpu.HBM((1, ROWS, COLS), F32),
        ),
        in_specs=[near] * 4,
        out_specs=(far, far),
        scratch_shapes=[vmem((GROUPS, PAD, 8, COLS), F32), dma((GROUPS + 1,))],
        compiler_params=pltpu.CompilerParams(vmem_limit_bytes=16 * 1024 * 1024),
        name="finish",
    )(*inner)


def solution(mesh):
    in_specs = (
        P("sec", None, "dom", None),
        P("sec", "dom", None),
        P("sec", None),
        P("sec", None, None),
        P("sec", "dom", None, None),
        P("sec", "dom", None),
        P("sec", "dom"),
        P("sec", "dom"),
        P("sec", "dom", None),
        P("sec", "dom"),
        P("sec", "dom"),
        P("sec", "dom", None),
    )
    out_specs = (P("sec", None, "dom", None), P("sec", "dom", None))
    return jax.shard_map(shards, mesh=mesh, in_specs=in_specs, out_specs=out_specs, check_vma=False)
```

```python
import jax
import jax.numpy as jnp
from jax import lax
from jax.experimental import pallas as pl
from jax.experimental.pallas import tpu as pltpu
from jax.sharding import PartitionSpec as P

MESH = pl.DeviceIdType.MESH
F32 = jnp.float32
BF16 = jnp.bfloat16

LEV = 30
PAD = 32
COLS = 128
ROWS = 32
FIELDS = 4
NW = 8
NY, NZ, NC = 4, 16, 2
N_DOM = NY * NZ * NC
GROUP = NY * NC
HALF = NZ // 2
SLOTS = NZ
GROUPS = ROWS // 8
MAIN = GROUP * ROWS
EDGE = GROUP * 2
WATER_LABEL = ROWS
FLUX_LABEL = WATER_LABEL + 8
FLUX = FLUX_LABEL + 8
SLOT = FLUX + 2 * NC * ROWS
WATER, FLUX_PIECES = 0, (1, 2, 3, 4)
PIECES = (
    (0, FLUX_LABEL),
    (FLUX_LABEL, 8 + ROWS),
    *[(FLUX + n * ROWS, ROWS) for n in range(1, 2 * NC)],
)
BLOCK = 2 * ROWS + 8


def tree(jumps):
    levels, reached = {}, 0
    for level, jump in enumerate(jumps, 1):
        levels[level] = [(reached, reached + i) for i in range(jump, 0, -1)]
        reached += jump
    return levels


WATER_TREES = tree((2, 1, 2, 1, 2)), tree((1, 2, 1, 2, 1))
FLUX_TREES = tree((2, 2, 2, 2)), tree((1, 2, 2, 2))
LEVELS = len(FLUX_TREES[0])


def split(x):
    high = x.astype(BF16)
    return high, (x - high.astype(F32)).astype(BF16)


def mm(a, b):
    return jnp.dot(a, b, preferred_element_type=F32)


def mm3(a, b):
    (ah, al), (bh, bl) = a, b
    return mm(ah, bh) + (mm(ah, bl) + mm(al, bh))


def iota(shape, dim):
    return lax.broadcasted_iota(jnp.int32, shape, dim)


def neighbours_in_columns(x):
    axis = x.ndim - 1
    return pltpu.roll(x, 1, axis) + pltpu.roll(x, COLS - 1, axis)


def laplacian(x, above, below):
    row, count = iota(x.shape, 1), x.shape[1]
    down = jnp.where(row == 0, above, pltpu.roll(x, 1, 1))
    up = jnp.where(row == count - 1, below, pltpu.roll(x, count - 1, 1))
    return down + up + neighbours_in_columns(x) - 4.0 * x


def kernel(
    state_h, frac_h, diff_h, ops_h, weight_h, fo_h, fr_h, fb_h, ro_h, rr_h, rb_h, store_h,
    base2, kab, forced, river,
    st, frac, diff, ops, weight, fo, fr, fb, ro, rr, rb, store,
    local_sem,
    hs_up, hs_dn, hr_up, hr_dn, halo_ssem, halo_rsem,
    terms, label_out, label_in, part_ssem, part_rsem,
    ring, ring_ssem, ring_rsem, row_of, ends_acc,
    flux_send, flux_recv, run_send, run_recv, rs_ssem, rs_rsem,
    dcol, kron_h, kron_l, base1,
):
    sec = lax.axis_index("sec")
    me = lax.axis_index("dom")
    core = me & (NC - 1)
    z = (me >> 1) & (NZ - 1)
    y = me >> 5

    def dom_of(yy, zz, cc):
        return (yy * NZ + zz) * NC + cc

    def along(distance):
        return (sec, dom_of(y, (z + NZ + distance) & (NZ - 1), core))

    partners = [(sec ^ 2, me), (sec ^ 2, me ^ 1)]
    after = (sec, (me + 1) & (N_DOM - 1))
    before = (sec, (me + N_DOM - 1) & (N_DOM - 1))

    def member(b):
        return (sec, dom_of((y + b // NC) & (NY - 1), z, core ^ (b % NC)))

    barrier = pltpu.get_barrier_semaphore()
    peers = [*partners, *[along(d) for d in (1, -1, 2, -2)], after, before]
    peers += [member(b) for b in range(1, GROUP)]
    for peer in peers:
        pl.semaphore_signal(barrier, inc=1, device_id=peer, device_id_type=MESH)

    pairs = [(weight_h.at[0], weight)]
    pairs += [
        (state_h.at[0, :, pl.ds(8 * i, 8)], st.at[1 + i, pl.ds(0, LEV)]) for i in range(GROUPS)
    ]
    pairs += [
        (fb_h, fb), (rb_h, rb), (fo_h, fo), (fr_h, fr), (ro_h, ro), (rr_h, rr),
        (frac_h.at[0], frac), (ops_h, ops), (diff_h, diff), (store_h.at[0], store),
    ]
    loads = [pltpu.make_async_copy(a, b, local_sem.at[i]) for i, (a, b) in enumerate(pairs)]
    for copy in loads:
        copy.start()

    for copy in loads[5:11]:
        copy.wait()

    def label_of(owner, row):
        eye = iota((ROWS, ROWS), 0) == iota((ROWS, ROWS), 1)
        target = (owner[...] * ROWS + row[...]).astype(F32)
        rows = jnp.broadcast_to(target, (ROWS, ROWS))
        column = jnp.sum(jnp.where(eye, rows, 0.0), axis=1, keepdims=True)
        wide = jnp.broadcast_to(column, (ROWS, COLS))
        place = iota((ROWS, COLS), 0) == (iota((ROWS, COLS), 1) & (ROWS - 1))
        return jnp.sum(jnp.where(place, wide, 0.0), axis=0, keepdims=True)

    label_out[...] = label_of(fo, fr)
    ring[0, WATER_LABEL:FLUX_LABEL, :] = jnp.broadcast_to(label_of(ro, rr), (8, COLS))
    ring[0, FLUX_LABEL:FLUX, :] = jnp.zeros((8, COLS), F32)

    tall = FIELDS * ROWS + ROWS
    spot = (iota((tall, ROWS), 0) & (ROWS - 1)) == iota((tall, ROWS), 1)
    blocks = jnp.where(
        iota((tall, ROWS), 0) < FIELDS * ROWS,
        jnp.broadcast_to(fb[...].astype(F32), (tall, ROWS)),
        jnp.broadcast_to(rb[...].astype(F32), (tall, ROWS)),
    )
    block = jnp.sum(jnp.where(spot, blocks, 0.0), axis=1, keepdims=True)
    block = jnp.broadcast_to(jnp.concatenate([block, block], axis=0), (2 * tall, COLS))
    for copy in loads[1:5]:
        copy.wait()
    surface = jnp.concatenate(
        [st[1 + i, f] for f in (*range(FIELDS), 0) for i in range(GROUPS)], axis=0
    )
    high = surface.astype(BF16).astype(F32)
    both = jnp.concatenate([high, surface - high], axis=0)
    lhs = jnp.concatenate(
        [jnp.where(block == float(w), both, 0.0).astype(BF16) for w in range(NW)], axis=1
    )
    loads[0].wait()
    rhs = jnp.concatenate(split(weight[...].reshape(NW * COLS, COLS)), axis=1)
    total = mm(lhs, rhs)
    result = total[:tall, :COLS] + (total[:tall, COLS:] + total[tall:, :COLS])
    terms[...] = result[: FIELDS * ROWS].reshape(FIELDS, ROWS, COLS)
    ring[0, :WATER_LABEL, :] = result[FIELDS * ROWS :]

    pl.semaphore_wait(barrier, len(peers))

    def remote(src, dst, ssem, rsem, device):
        return pltpu.make_async_remote_copy(
            src_ref=src, dst_ref=dst, send_sem=ssem, recv_sem=rsem,
            device_id=device, device_id_type=MESH,
        )

    def slot_of(way, distance):
        return 0 if distance == 0 else min(2 * distance - (way > 0), SLOTS - 1)

    def piece(c, slot):
        return ring.at[slot, pl.ds(*PIECES[c])]

    def hop(c, way, start, end):
        slot = slot_of(way, end)
        return remote(
            piece(c, slot_of(way, start)), piece(c, slot),
            ring_ssem, ring_rsem.at[c, slot], along(way * (end - start)),
        )

    arrivals, departures = {}, {}
    for c in range(len(PIECES)):
        for way in (1, -1):
            trees = WATER_TREES if c == WATER else FLUX_TREES
            levels = trees[(c % 2 == 0) != (way > 0)]
            for level, edges in levels.items():
                copies = [hop(c, way, *edge) for edge in edges]
                departures[c, way, level] = (slot_of(way, edges[0][0]), copies)
                for copy, (_, end) in zip(copies, edges):
                    arrivals[c, slot_of(way, end)] = copy

    def arrive(c, slots):
        for slot in slots:
            if (c, slot) in arrivals:
                arrivals.pop((c, slot)).wait_recv()

    later = []

    def depart(c, level):
        for way in (1, -1):
            if (c, way, level) in departures:
                slot, copies = departures.pop((c, way, level))
                arrive(c, [slot])
                copies[0].start()
                later.extend(copies[1:])

    def flush(count=None):
        for copy in later[:count]:
            copy.start()
        del later[:count]

    label_swap = [
        remote(label_out, label_in.at[i], part_ssem.at[i], part_rsem.at[i], to)
        for i, to in enumerate(partners)
    ]
    swap = []
    for f in range(2):
        for i in range(NC):
            n = NC * f + i
            swap.append(
                remote(
                    terms.at[2 * (core ^ i) + f], ring.at[0, pl.ds(FLUX + n * ROWS, ROWS)],
                    part_ssem.at[2 + n], part_rsem.at[2 + n], partners[i],
                )
            )
    for copy in (*label_swap, *swap):
        copy.start()

    depart(WATER, 1)
    flush()

    loads[11].wait()
    hs_up[0:LEV] = st[1, 0:LEV, 0:2, :]
    hs_dn[0:LEV] = st[GROUPS, 0:LEV, 6:8, :]
    hs_up[LEV] = frac[0:2, :]
    hs_dn[LEV] = frac[ROWS - 2 : ROWS, :]
    hs_up[LEV + 1] = jnp.zeros((2, COLS), F32)
    hs_dn[LEV + 1] = jnp.zeros((2, COLS), F32)
    for i in range(GROUPS):
        st[1 + i, LEV:PAD] = jnp.zeros((PAD - LEV, 8, COLS), F32)
    halo = [
        remote(hs_dn, hr_up, halo_ssem.at[0], halo_rsem.at[0], after),
        remote(hs_up, hr_dn, halo_ssem.at[1], halo_rsem.at[1], before),
    ]
    for copy in halo:
        copy.start()


    tall8 = PAD * 8
    for copy in loads[12:14]:
        copy.wait()
    pick = ((iota((tall8, LEV), 0) >> 3) == iota((tall8, LEV), 1)).astype(F32)
    pick_t = ((iota((LEV, tall8), 1) >> 3) == iota((LEV, tall8), 0)).astype(BF16)
    column = jnp.sum(pick * jnp.broadcast_to(diff[...], (tall8, LEV)), axis=1, keepdims=True)
    dcol[...] = jnp.broadcast_to(column, (tall8, COLS))
    op = ops[:, 0, :]
    op_h, op_l = split(op)
    op_r = (op - op_h.astype(F32) - op_l.astype(F32)).astype(BF16)
    pick = pick.astype(BF16)
    spread = mm(mm(pick, op_h).astype(BF16), pick_t) + (
        mm(mm(pick, op_l).astype(BF16), pick_t) + mm(mm(pick, op_r).astype(BF16), pick_t)
    )
    same8 = (iota((tall8, tall8), 0) & 7) == (iota((tall8, tall8), 1) & 7)
    kh, kl = split(jnp.where(same8, spread, 0.0))
    kron_h[...] = kh
    kron_l[...] = kl

    def block_start(b):
        return dom_of((y + (b >> 1)) & (NY - 1), z, core ^ (b & 1)) * ROWS

    i = iota((MAIN, COLS), 0)
    row_of[:MAIN] = (block_start(i >> 5) + (i & (ROWS - 1))).astype(F32)
    i = iota((EDGE, COLS), 0)
    row_of[MAIN:] = (block_start(i >> 1) + jnp.where((i & 1) == 0, -1, ROWS)).astype(F32)
    flux_send[:, 2 * ROWS + 4 :, :] = jnp.zeros((GROUP, 4, COLS), F32)

    def kab_work():
        k4 = kron_h[:, : 8 * FIELDS].astype(F32) + kron_l[:, : 8 * FIELDS].astype(F32)
        eye = (iota(k4.shape, 0) == iota(k4.shape, 1)).astype(F32)
        q = jnp.concatenate([k4 + eye, dcol[:, : 8 * FIELDS] * k4], axis=1)
        kh, kl = split(mm3((kron_h[...], kron_l[...]), split(q)))
        kab[...] = jnp.concatenate([kh, kh, kl], axis=1)

    first = me == 0
    last = me == N_DOM - 1

    def apply(*groups):
        u = jnp.concatenate([u.reshape(PAD * 8, COLS) for u in groups], axis=1)
        out = mm3((kron_h[...], kron_l[...]), split(u))
        return [
            out[:, COLS * i : COLS * (i + 1)].reshape(PAD, 8, COLS) for i in range(len(groups))
        ]

    def diffused(i, source):
        x = source[i]
        lap = laplacian(x, source[i - 1, :, 7:8], source[i + 1, :, 0:1])
        return x + dcol[...].reshape(PAD, 8, COLS) * lap

    def step_one(i, j):
        base1[i], base1[j] = apply(diffused(i, st), diffused(j, st))

    def step_two(i, j):
        base2[i - 1], base2[j - 1] = apply(diffused(i, base1), diffused(j, base1))

    def step_one_ends():
        d = dcol[...].reshape(PAD, 8, COLS)
        spot = iota((PAD, 8, COLS), 1)
        above, below = st[0], st[GROUPS + 1]
        x = jnp.where(spot == 7, above[:, 7:8], below[:, 0:1])
        outer = jnp.where(spot == 7, above[:, 6:7], below[:, 1:2])
        inner = jnp.where(spot == 7, st[1, :, 0:1], st[GROUPS, :, 7:8])
        u = x + d * (outer + inner + neighbours_in_columns(x) - 4.0 * x)
        gone = ((spot == 7) & first) | ((spot < 7) & last)
        (ends,) = apply(jnp.where(gone, 0.0, u))
        base1[0] = ends
        base1[GROUPS + 1] = ends

    step_one(2, 3)
    depart(WATER, 2)
    flush()
    for i, copy in enumerate(label_swap):
        copy.wait_recv()
        ring[0, FLUX_LABEL + i : FLUX_LABEL + i + 1, :] = label_in[i]
    for c in FLUX_PIECES:
        swap[c - 1].wait_recv()
        before_this = len(later)
        depart(c, 1)
        flush(before_this)
    depart(WATER, 3)
    flush()

    def joined(rows):
        lane = iota((1, COLS), 1) >> 5
        names = rows[0]
        for i in range(1, 4):
            names = jnp.where(lane == i, rows[i], names)
        return names

    def one_hot(rows, names):
        return (rows == jnp.broadcast_to(names, rows.shape)).astype(F32).astype(BF16)

    selected = {}

    def select_flux(j):
        if j not in selected:
            selected[j] = make_selection(j)
        return selected[j]

    def make_selection(j):
        arrive(FLUX_PIECES[0], (2 * j, 2 * j + 1))
        rows = []
        for i in range(4):
            row = FLUX_LABEL + i % 2
            rows.append(ring[2 * j + i // 2, row : row + 1, :])
        return one_hot(row_of[...], joined(rows))

    def rows_of(f, slots):
        start = FLUX + f * NC * ROWS
        for c in FLUX_PIECES[NC * f : NC * (f + 1)]:
            arrive(c, slots)
        return jnp.concatenate([ring[n, start : start + NC * ROWS, :] for n in slots], axis=0)

    def place_flux(first_slot, last_slot, fields, fresh):
        sel = [select_flux(j) for j in range(first_slot // 2, last_slot // 2)]
        data = [rows_of(f, range(first_slot, last_slot)) for f in fields]
        high, low = split(jnp.concatenate(data, axis=1))
        part = mm(jnp.concatenate([*sel, *sel], axis=1), jnp.concatenate([high, low], axis=0))
        for i, f in enumerate(fields):
            one = part[:, i * COLS : (i + 1) * COLS]
            rows = slice(f * ROWS, (f + 1) * ROWS)
            main = one[:MAIN].reshape(GROUP, ROWS, COLS)
            flux_send[:, rows, :] = main if fresh else flux_send[:, rows, :] + main
            ends_acc[f] = one[MAIN:] if fresh else ends_acc[f] + one[MAIN:]

    def place_water():
        arrive(WATER, range(SLOTS))
        rows = [ring[slot, :WATER_LABEL, :] for slot in range(SLOTS)]
        high, low = split(jnp.concatenate(rows, axis=0))
        labels = [ring[slot, WATER_LABEL : WATER_LABEL + 1, :] for slot in range(SLOTS)]
        sel = [
            one_hot(row_of[:MAIN], joined(labels[4 * g : 4 * g + 4])) for g in range(SLOTS // 4)
        ]
        part = mm(jnp.concatenate([*sel, *sel], axis=1), jnp.concatenate([high, low], axis=0))
        run_send[...] = part.reshape(GROUP, ROWS, COLS)
        for copy in water_scatter:
            copy.start()

    order = [4, 5, 2, 3, 6, 7, 1]

    def scatter_copies(src, dst, c, rows):
        return [
            remote(src.at[b, rows], dst.at[b, rows], rs_ssem.at[c], rs_rsem.at[c], member(b))
            for b in order
        ]

    def whole(src, dst, c, rows):
        others = pl.ds(1, GROUP - 1)
        return remote(
            src.at[others, rows], dst.at[others, rows], rs_ssem.at[c], rs_rsem.at[c], member(1)
        )

    kinds = [
        (run_send, run_recv, 0, pl.ds(0, ROWS)),
        (flux_send, flux_recv, 1, pl.ds(0, ROWS)),
        (flux_send, flux_recv, 2, pl.ds(ROWS, BLOCK - ROWS)),
    ]
    water_scatter, *flux_scatter = [scatter_copies(*kind) for kind in kinds]
    water_whole, *flux_whole = [whole(*kind) for kind in kinds]

    for level in range(2, LEVELS + 1):
        for c in FLUX_PIECES:
            depart(c, level)
        flush()
        depart(WATER, level + 2)
        flush()
        if level == LEVELS:
            place_water()
    place_flux(0, 10, (0, 1), True)
    for f in range(2):
        place_flux(10, SLOTS, (f,), False)
        if f == 1:
            for b in range(GROUP):
                for e in range(2):
                    ends = 2 * ROWS + 2 * e
                    flux_send[b, ends : ends + 2, :] = ends_acc[e, 2 * b : 2 * b + 2]
        for copy in flux_scatter[f]:
            copy.start()

    for copy in halo:
        copy.wait_recv()
    st[0, :, 6:8, :] = jnp.where(first, 0.0, hr_up[...])
    st[GROUPS + 1, :, 0:2, :] = jnp.where(last, 0.0, hr_dn[...])
    step_one(1, 4)
    step_one_ends()
    step_two(1, 2)
    step_two(3, 4)
    kab_work()
    for copy in (*label_swap, *swap, *halo):
        copy.wait_send()
    every = ring.at[pl.ds(1, SLOTS - 1)]
    remote(every, every, ring_ssem, ring_rsem.at[0, 0], along(1)).wait_send()

    loads[14].wait()
    water_whole.wait_recv()
    water = run_send[0]
    for b in range(1, GROUP):
        water = water + run_recv[b]
    river[...] = store[...] + water

    for copy in flux_whole:
        copy.wait_recv()

    same, other = flux_send[0], flux_recv[1]
    for b in range(2, GROUP, 2):
        same = same + flux_recv[b]
        other = other + flux_recv[b + 1]
    pair = [jnp.where(core == 0, same, other), jnp.where(core == 0, other, same)]

    g4 = jnp.stack(
        [frac[...] * pair[f // 2][(f % 2) * ROWS : (f % 2 + 1) * ROWS] for f in range(FIELDS)],
        axis=0,
    )
    ends = [pair[f // 2][2 * ROWS + 2 * (f % 2) : 2 * ROWS + 2 * (f % 2) + 2] for f in range(FIELDS)]
    frac_above = jnp.where(first, 0.0, hr_up[LEV, 1:2, :])
    frac_below = jnp.where(last, 0.0, hr_dn[LEV, 0:1, :])
    above = jnp.stack([frac_above * x[0:1] for x in ends], axis=0)
    below = jnp.stack([frac_below * x[1:2] for x in ends], axis=0)
    lap = laplacian(g4, above, below)
    for i in range(GROUPS):
        high, low = split(
            jnp.concatenate(
                [x[:, 8 * i : 8 * i + 8].reshape(8 * FIELDS, COLS) for x in (g4, lap)], axis=0
            )
        )
        forced[i] = jnp.concatenate([high, low, high], axis=0)

    for copy in (*flux_whole, water_whole):
        copy.wait_send()


def finish(base2, kab, forced, river, out_h, river_h, out, sems):
    river_copy = pltpu.make_async_copy(river, river_h.at[0], sems.at[GROUPS])
    river_copy.start()
    copies = []
    for i in range(0, GROUPS, 2):
        delta = mm(kab[...], jnp.concatenate([forced[i], forced[i + 1]], axis=1))
        for j in range(2):
            part = delta[:, COLS * j : COLS * (j + 1)].reshape(PAD, 8, COLS)
            out[i + j] = base2[i + j] + part
            copies.append(
                pltpu.make_async_copy(
                    out.at[i + j, pl.ds(0, LEV)],
                    out_h.at[0, :, pl.ds(8 * (i + j), 8)],
                    sems.at[i + j],
                )
            )
            copies[-1].start()
    for copy in (*copies, river_copy):
        copy.wait()


def shards(
    state, frac, diff, ops, weight, fo, fr, fb, ro, rr, rb, store,
):
    ops = jnp.transpose(ops, (1, 0, 2))
    fo, ro = fo.reshape(1, ROWS), ro.reshape(1, ROWS)
    args = (state, frac, diff, ops, weight, fo, fr, fb, ro, rr, rb, store)
    args = [pltpu.with_memory_space_constraint(x, pltpu.HBM) for x in args]
    vmem = pltpu.VMEM
    far = pl.BlockSpec(memory_space=pltpu.HBM)
    near = pl.BlockSpec(memory_space=vmem)
    dma = pltpu.SemaphoreType.DMA
    i32 = jnp.int32
    inner = pl.pallas_call(
        kernel,
        out_shape=(
            vmem((GROUPS, PAD, 8, COLS), F32),
            vmem((PAD * 8, 3 * 16 * FIELDS), BF16),
            vmem((GROUPS, 3 * 16 * FIELDS, COLS), BF16),
            vmem((ROWS, COLS), F32),
        ),
        in_specs=[far] * 12,
        out_specs=(near,) * 4,
        scratch_shapes=[
            vmem((GROUPS + 2, PAD, 8, COLS), F32),
            vmem((ROWS, COLS), F32),
            vmem((1, LEV), F32),
            vmem((LEV, 1, LEV), F32),
            vmem((NW, COLS, COLS), F32),
            vmem((1, ROWS), i32),
            vmem((1, ROWS), i32),
            vmem((1, ROWS), i32),
            vmem((1, ROWS), i32),
            vmem((1, ROWS), i32),
            vmem((1, ROWS), i32),
            vmem((ROWS, COLS), F32),
            dma((15,)),
            vmem((PAD, 2, COLS), F32),
            vmem((PAD, 2, COLS), F32),
            vmem((PAD, 2, COLS), F32),
            vmem((PAD, 2, COLS), F32),
            dma((2,)),
            dma((2,)),
            vmem((FIELDS, ROWS, COLS), F32),
            vmem((1, COLS), F32),
            vmem((2, 1, COLS), F32),
            dma((2 + 2 * NC,)),
            dma((2 + 2 * NC,)),
            vmem((SLOTS, SLOT, COLS), F32),
            dma(()),
            dma((len(PIECES), SLOTS)),
            vmem((MAIN + EDGE, COLS), F32),
            vmem((2, EDGE, COLS), F32),
            vmem((GROUP, BLOCK, COLS), F32),
            vmem((GROUP, BLOCK, COLS), F32),
            vmem((GROUP, ROWS, COLS), F32),
            vmem((GROUP, ROWS, COLS), F32),
            dma((3,)),
            dma((3,)),
            vmem((PAD * 8, COLS), F32),
            vmem((PAD * 8, PAD * 8), BF16),
            vmem((PAD * 8, PAD * 8), BF16),
            vmem((GROUPS + 2, PAD, 8, COLS), F32),
        ],
        compiler_params=pltpu.CompilerParams(
            collective_id=0, has_side_effects=True, vmem_limit_bytes=32 * 1024 * 1024
        ),
        name="coupling",
    )(*args)
    inner = [pltpu.with_memory_space_constraint(x, vmem) for x in inner]
    return pl.pallas_call(
        finish,
        out_shape=(
            pltpu.HBM((1, LEV, ROWS, COLS), F32),
            pltpu.HBM((1, ROWS, COLS), F32),
        ),
        in_specs=[near] * 4,
        out_specs=(far, far),
        scratch_shapes=[vmem((GROUPS, PAD, 8, COLS), F32), dma((GROUPS + 1,))],
        compiler_params=pltpu.CompilerParams(vmem_limit_bytes=16 * 1024 * 1024),
        name="finish",
    )(*inner)


def solution(mesh):
    in_specs = (
        P("sec", None, "dom", None),
        P("sec", "dom", None),
        P("sec", None),
        P("sec", None, None),
        P("sec", "dom", None, None),
        P("sec", "dom", None),
        P("sec", "dom"),
        P("sec", "dom"),
        P("sec", "dom", None),
        P("sec", "dom"),
        P("sec", "dom"),
        P("sec", "dom", None),
    )
    out_specs = (P("sec", None, "dom", None), P("sec", "dom", None))
    return jax.shard_map(shards, mesh=mesh, in_specs=in_specs, out_specs=out_specs, check_vma=False)
```

```python
import jax
import jax.numpy as jnp
from jax import lax
from jax.experimental import pallas as pl
from jax.experimental.pallas import tpu as pltpu
from jax.sharding import PartitionSpec as P

MESH = pl.DeviceIdType.MESH
F32 = jnp.float32
BF16 = jnp.bfloat16

LEV = 30
PAD = 32
COLS = 128
ROWS = 32
FIELDS = 4
NW = 8
NY, NZ, NC = 4, 16, 2
N_DOM = NY * NZ * NC
GROUP = NY * NC
HALF = NZ // 2
SLOTS = NZ
GROUPS = ROWS // 8
MAIN = GROUP * ROWS
EDGE = GROUP * 2
WATER_LABEL = ROWS
FLUX_LABEL = WATER_LABEL + 8
FLUX = FLUX_LABEL + 8
SLOT = FLUX + 2 * NC * ROWS
WATER, FLUX_PIECES = 0, (1, 2, 3, 4)
PIECES = (
    (0, FLUX_LABEL),
    (FLUX_LABEL, 8 + ROWS),
    *[(FLUX + n * ROWS, ROWS) for n in range(1, 2 * NC)],
)
BLOCK = 2 * ROWS + 8


def tree(jumps):
    levels, reached = {}, 0
    for level, jump in enumerate(jumps, 1):
        levels[level] = [(reached, reached + i) for i in range(jump, 0, -1)]
        reached += jump
    return levels


WATER_TREES = tree((2, 1, 2, 1, 2)), tree((1, 2, 1, 2, 1))
FLUX_TREES = WATER_TREES
LEVELS = len(FLUX_TREES[0])


def split(x):
    high = x.astype(BF16)
    return high, (x - high.astype(F32)).astype(BF16)


def mm(a, b):
    return jnp.dot(a, b, preferred_element_type=F32)


def mm3(a, b):
    (ah, al), (bh, bl) = a, b
    return mm(ah, bh) + (mm(ah, bl) + mm(al, bh))


def iota(shape, dim):
    return lax.broadcasted_iota(jnp.int32, shape, dim)


def neighbours_in_columns(x):
    axis = x.ndim - 1
    return pltpu.roll(x, 1, axis) + pltpu.roll(x, COLS - 1, axis)


def laplacian(x, above, below):
    row, count = iota(x.shape, 1), x.shape[1]
    down = jnp.where(row == 0, above, pltpu.roll(x, 1, 1))
    up = jnp.where(row == count - 1, below, pltpu.roll(x, count - 1, 1))
    return down + up + neighbours_in_columns(x) - 4.0 * x


def kernel(
    state_h, frac_h, diff_h, ops_h, weight_h, fo_h, fr_h, fb_h, ro_h, rr_h, rb_h, store_h,
    base2, kab, forced, river,
    st, frac, diff, ops, weight, fo, fr, fb, ro, rr, rb, store,
    local_sem,
    hs_up, hs_dn, hr_up, hr_dn, halo_ssem, halo_rsem,
    terms, label_out, label_in, part_ssem, part_rsem,
    ring, ring_ssem, ring_rsem, row_of, ends_acc,
    flux_send, flux_recv, run_send, run_recv, rs_ssem, rs_rsem,
    dcol, kron_h, kron_l, base1,
):
    sec = lax.axis_index("sec")
    me = lax.axis_index("dom")
    core = me & (NC - 1)
    z = (me >> 1) & (NZ - 1)
    y = me >> 5

    def dom_of(yy, zz, cc):
        return (yy * NZ + zz) * NC + cc

    def along(distance):
        return (sec, dom_of(y, (z + NZ + distance) & (NZ - 1), core))

    partners = [(sec ^ 2, me), (sec ^ 2, me ^ 1)]
    after = (sec, (me + 1) & (N_DOM - 1))
    before = (sec, (me + N_DOM - 1) & (N_DOM - 1))

    def member(b):
        return (sec, dom_of((y + b // NC) & (NY - 1), z, core ^ (b % NC)))

    barrier = pltpu.get_barrier_semaphore()
    peers = [*partners, *[along(d) for d in (1, -1, 2, -2)], after, before]
    peers += [member(b) for b in range(1, GROUP)]
    for peer in peers:
        pl.semaphore_signal(barrier, inc=1, device_id=peer, device_id_type=MESH)

    pairs = [(weight_h.at[0], weight)]
    pairs += [
        (state_h.at[0, :, pl.ds(8 * i, 8)], st.at[1 + i, pl.ds(0, LEV)]) for i in range(GROUPS)
    ]
    pairs += [
        (fb_h, fb), (rb_h, rb), (fo_h, fo), (fr_h, fr), (ro_h, ro), (rr_h, rr),
        (frac_h.at[0], frac), (ops_h, ops), (diff_h, diff), (store_h.at[0], store),
    ]
    loads = [pltpu.make_async_copy(a, b, local_sem.at[i]) for i, (a, b) in enumerate(pairs)]
    for copy in loads:
        copy.start()

    for copy in loads[5:11]:
        copy.wait()

    def label_of(owner, row):
        eye = iota((ROWS, ROWS), 0) == iota((ROWS, ROWS), 1)
        target = (owner[...] * ROWS + row[...]).astype(F32)
        rows = jnp.broadcast_to(target, (ROWS, ROWS))
        column = jnp.sum(jnp.where(eye, rows, 0.0), axis=1, keepdims=True)
        wide = jnp.broadcast_to(column, (ROWS, COLS))
        place = iota((ROWS, COLS), 0) == (iota((ROWS, COLS), 1) & (ROWS - 1))
        return jnp.sum(jnp.where(place, wide, 0.0), axis=0, keepdims=True)

    label_out[...] = label_of(fo, fr)
    ring[0, WATER_LABEL:FLUX_LABEL, :] = jnp.broadcast_to(label_of(ro, rr), (8, COLS))
    ring[0, FLUX_LABEL:FLUX, :] = jnp.zeros((8, COLS), F32)

    tall = FIELDS * ROWS + ROWS
    spot = (iota((tall, ROWS), 0) & (ROWS - 1)) == iota((tall, ROWS), 1)
    blocks = jnp.where(
        iota((tall, ROWS), 0) < FIELDS * ROWS,
        jnp.broadcast_to(fb[...].astype(F32), (tall, ROWS)),
        jnp.broadcast_to(rb[...].astype(F32), (tall, ROWS)),
    )
    block = jnp.sum(jnp.where(spot, blocks, 0.0), axis=1, keepdims=True)
    block = jnp.broadcast_to(jnp.concatenate([block, block], axis=0), (2 * tall, COLS))
    for copy in loads[1:5]:
        copy.wait()
    surface = jnp.concatenate(
        [st[1 + i, f] for f in (*range(FIELDS), 0) for i in range(GROUPS)], axis=0
    )
    high = surface.astype(BF16).astype(F32)
    both = jnp.concatenate([high, surface - high], axis=0)
    lhs = jnp.concatenate(
        [jnp.where(block == float(w), both, 0.0).astype(BF16) for w in range(NW)], axis=1
    )
    loads[0].wait()
    rhs = jnp.concatenate(split(weight[...].reshape(NW * COLS, COLS)), axis=1)
    total = mm(lhs, rhs)
    result = total[:tall, :COLS] + (total[:tall, COLS:] + total[tall:, :COLS])
    terms[...] = result[: FIELDS * ROWS].reshape(FIELDS, ROWS, COLS)
    ring[0, :WATER_LABEL, :] = result[FIELDS * ROWS :]

    pl.semaphore_wait(barrier, len(peers))

    def remote(src, dst, ssem, rsem, device):
        return pltpu.make_async_remote_copy(
            src_ref=src, dst_ref=dst, send_sem=ssem, recv_sem=rsem,
            device_id=device, device_id_type=MESH,
        )

    def slot_of(way, distance):
        return 0 if distance == 0 else min(2 * distance - (way > 0), SLOTS - 1)

    def piece(c, slot):
        return ring.at[slot, pl.ds(*PIECES[c])]

    def hop(c, way, start, end):
        slot = slot_of(way, end)
        return remote(
            piece(c, slot_of(way, start)), piece(c, slot),
            ring_ssem, ring_rsem.at[c, slot], along(way * (end - start)),
        )

    arrivals, departures = {}, {}
    for c in range(len(PIECES)):
        for way in (1, -1):
            trees = WATER_TREES if c == WATER else FLUX_TREES
            levels = trees[(c % 2 == 0) != (way > 0)]
            for level, edges in levels.items():
                copies = [hop(c, way, *edge) for edge in edges]
                departures[c, way, level] = (slot_of(way, edges[0][0]), copies)
                for copy, (_, end) in zip(copies, edges):
                    arrivals[c, slot_of(way, end)] = copy

    def arrive(c, slots):
        for slot in slots:
            if (c, slot) in arrivals:
                arrivals.pop((c, slot)).wait_recv()

    def depart(c, level):
        for way in (1, -1):
            if (c, way, level) in departures:
                slot, copies = departures.pop((c, way, level))
                arrive(c, [slot])
                for copy in copies:
                    copy.start()

    label_swap = [
        remote(label_out, label_in.at[i], part_ssem.at[i], part_rsem.at[i], to)
        for i, to in enumerate(partners)
    ]
    swap = []
    for f in range(2):
        for i in range(NC):
            n = NC * f + i
            swap.append(
                remote(
                    terms.at[2 * (core ^ i) + f], ring.at[0, pl.ds(FLUX + n * ROWS, ROWS)],
                    part_ssem.at[2 + n], part_rsem.at[2 + n], partners[i],
                )
            )
    for copy in (*label_swap, *swap):
        copy.start()

    depart(WATER, 1)

    loads[11].wait()
    hs_up[0:LEV] = st[1, 0:LEV, 0:2, :]
    hs_dn[0:LEV] = st[GROUPS, 0:LEV, 6:8, :]
    hs_up[LEV] = frac[0:2, :]
    hs_dn[LEV] = frac[ROWS - 2 : ROWS, :]
    hs_up[LEV + 1] = jnp.zeros((2, COLS), F32)
    hs_dn[LEV + 1] = jnp.zeros((2, COLS), F32)
    for i in range(GROUPS):
        st[1 + i, LEV:PAD] = jnp.zeros((PAD - LEV, 8, COLS), F32)
    halo = [
        remote(hs_dn, hr_up, halo_ssem.at[0], halo_rsem.at[0], after),
        remote(hs_up, hr_dn, halo_ssem.at[1], halo_rsem.at[1], before),
    ]
    for copy in halo:
        copy.start()


    tall8 = PAD * 8
    for copy in loads[12:14]:
        copy.wait()
    pick = ((iota((tall8, LEV), 0) >> 3) == iota((tall8, LEV), 1)).astype(F32)
    pick_t = ((iota((LEV, tall8), 1) >> 3) == iota((LEV, tall8), 0)).astype(BF16)
    column = jnp.sum(pick * jnp.broadcast_to(diff[...], (tall8, LEV)), axis=1, keepdims=True)
    dcol[...] = jnp.broadcast_to(column, (tall8, COLS))
    op = ops[:, 0, :]
    op_h, op_l = split(op)
    op_r = (op - op_h.astype(F32) - op_l.astype(F32)).astype(BF16)
    pick = pick.astype(BF16)
    spread = mm(mm(pick, op_h).astype(BF16), pick_t) + (
        mm(mm(pick, op_l).astype(BF16), pick_t) + mm(mm(pick, op_r).astype(BF16), pick_t)
    )
    same8 = (iota((tall8, tall8), 0) & 7) == (iota((tall8, tall8), 1) & 7)
    kh, kl = split(jnp.where(same8, spread, 0.0))
    kron_h[...] = kh
    kron_l[...] = kl

    def block_start(b):
        return dom_of((y + (b >> 1)) & (NY - 1), z, core ^ (b & 1)) * ROWS

    i = iota((MAIN, COLS), 0)
    row_of[:MAIN] = (block_start(i >> 5) + (i & (ROWS - 1))).astype(F32)
    i = iota((EDGE, COLS), 0)
    row_of[MAIN:] = (block_start(i >> 1) + jnp.where((i & 1) == 0, -1, ROWS)).astype(F32)
    flux_send[:, 2 * ROWS + 4 :, :] = jnp.zeros((GROUP, 4, COLS), F32)

    def kab_work():
        k4 = kron_h[:, : 8 * FIELDS].astype(F32) + kron_l[:, : 8 * FIELDS].astype(F32)
        eye = (iota(k4.shape, 0) == iota(k4.shape, 1)).astype(F32)
        q = jnp.concatenate([k4 + eye, dcol[:, : 8 * FIELDS] * k4], axis=1)
        kh, kl = split(mm3((kron_h[...], kron_l[...]), split(q)))
        kab[...] = jnp.concatenate([kh, kh, kl], axis=1)

    first = me == 0
    last = me == N_DOM - 1

    def apply(*groups):
        u = jnp.concatenate([u.reshape(PAD * 8, COLS) for u in groups], axis=1)
        out = mm3((kron_h[...], kron_l[...]), split(u))
        return [
            out[:, COLS * i : COLS * (i + 1)].reshape(PAD, 8, COLS) for i in range(len(groups))
        ]

    def diffused(i, source):
        x = source[i]
        lap = laplacian(x, source[i - 1, :, 7:8], source[i + 1, :, 0:1])
        return x + dcol[...].reshape(PAD, 8, COLS) * lap

    def step_one(i, j):
        base1[i], base1[j] = apply(diffused(i, st), diffused(j, st))

    def step_two(i, j):
        base2[i - 1], base2[j - 1] = apply(diffused(i, base1), diffused(j, base1))

    def step_one_ends():
        d = dcol[...].reshape(PAD, 8, COLS)
        spot = iota((PAD, 8, COLS), 1)
        above, below = st[0], st[GROUPS + 1]
        x = jnp.where(spot == 7, above[:, 7:8], below[:, 0:1])
        outer = jnp.where(spot == 7, above[:, 6:7], below[:, 1:2])
        inner = jnp.where(spot == 7, st[1, :, 0:1], st[GROUPS, :, 7:8])
        u = x + d * (outer + inner + neighbours_in_columns(x) - 4.0 * x)
        gone = ((spot == 7) & first) | ((spot < 7) & last)
        (ends,) = apply(jnp.where(gone, 0.0, u))
        base1[0] = ends
        base1[GROUPS + 1] = ends

    step_one(2, 3)
    depart(WATER, 2)
    for i, copy in enumerate(label_swap):
        copy.wait_recv()
        ring[0, FLUX_LABEL + i : FLUX_LABEL + i + 1, :] = label_in[i]
    for c in FLUX_PIECES:
        swap[c - 1].wait_recv()
        depart(c, 1)
    depart(WATER, 3)

    def joined(rows):
        lane = iota((1, COLS), 1) >> 5
        names = rows[0]
        for i in range(1, 4):
            names = jnp.where(lane == i, rows[i], names)
        return names

    def one_hot(rows, names):
        return (rows == jnp.broadcast_to(names, rows.shape)).astype(F32).astype(BF16)

    selected = {}

    def select_flux(j):
        if j not in selected:
            selected[j] = make_selection(j)
        return selected[j]

    def make_selection(j):
        arrive(FLUX_PIECES[0], (2 * j, 2 * j + 1))
        rows = []
        for i in range(4):
            row = FLUX_LABEL + i % 2
            rows.append(ring[2 * j + i // 2, row : row + 1, :])
        return one_hot(row_of[...], joined(rows))

    def rows_of(f, slots):
        start = FLUX + f * NC * ROWS
        for c in FLUX_PIECES[NC * f : NC * (f + 1)]:
            arrive(c, slots)
        return jnp.concatenate([ring[n, start : start + NC * ROWS, :] for n in slots], axis=0)

    def place_flux(first_slot, last_slot, fields, fresh):
        sel = [select_flux(j) for j in range(first_slot // 2, last_slot // 2)]
        data = [rows_of(f, range(first_slot, last_slot)) for f in fields]
        high, low = split(jnp.concatenate(data, axis=1))
        part = mm(jnp.concatenate([*sel, *sel], axis=1), jnp.concatenate([high, low], axis=0))
        for i, f in enumerate(fields):
            one = part[:, i * COLS : (i + 1) * COLS]
            rows = slice(f * ROWS, (f + 1) * ROWS)
            main = one[:MAIN].reshape(GROUP, ROWS, COLS)
            flux_send[:, rows, :] = main if fresh else flux_send[:, rows, :] + main
            ends_acc[f] = one[MAIN:] if fresh else ends_acc[f] + one[MAIN:]

    def place_water():
        arrive(WATER, range(SLOTS))
        rows = [ring[slot, :WATER_LABEL, :] for slot in range(SLOTS)]
        high, low = split(jnp.concatenate(rows, axis=0))
        labels = [ring[slot, WATER_LABEL : WATER_LABEL + 1, :] for slot in range(SLOTS)]
        sel = [
            one_hot(row_of[:MAIN], joined(labels[4 * g : 4 * g + 4])) for g in range(SLOTS // 4)
        ]
        part = mm(jnp.concatenate([*sel, *sel], axis=1), jnp.concatenate([high, low], axis=0))
        run_send[...] = part.reshape(GROUP, ROWS, COLS)
        for copy in water_scatter:
            copy.start()

    order = [4, 5, 2, 3, 6, 7, 1]

    def scatter_copies(src, dst, c, rows):
        return [
            remote(src.at[b, rows], dst.at[b, rows], rs_ssem.at[c], rs_rsem.at[c], member(b))
            for b in order
        ]

    def whole(src, dst, c, rows):
        others = pl.ds(1, GROUP - 1)
        return remote(
            src.at[others, rows], dst.at[others, rows], rs_ssem.at[c], rs_rsem.at[c], member(1)
        )

    kinds = [
        (run_send, run_recv, 0, pl.ds(0, ROWS)),
        (flux_send, flux_recv, 1, pl.ds(0, ROWS)),
        (flux_send, flux_recv, 2, pl.ds(ROWS, BLOCK - ROWS)),
    ]
    water_scatter, *flux_scatter = [scatter_copies(*kind) for kind in kinds]
    water_whole, *flux_whole = [whole(*kind) for kind in kinds]

    for level in range(2, LEVELS + 1):
        for c in FLUX_PIECES:
            depart(c, level)
        depart(WATER, level + 2)
        if level == LEVELS - 1:
            place_water()
    place_flux(0, 12, (0, 1), True)
    for f in range(2):
        place_flux(12, SLOTS, (f,), False)
        if f == 1:
            for b in range(GROUP):
                for e in range(2):
                    ends = 2 * ROWS + 2 * e
                    flux_send[b, ends : ends + 2, :] = ends_acc[e, 2 * b : 2 * b + 2]
        for copy in flux_scatter[f]:
            copy.start()

    for copy in halo:
        copy.wait_recv()
    st[0, :, 6:8, :] = jnp.where(first, 0.0, hr_up[...])
    st[GROUPS + 1, :, 0:2, :] = jnp.where(last, 0.0, hr_dn[...])
    step_one(1, 4)
    step_one_ends()
    step_two(1, 2)
    step_two(3, 4)
    kab_work()
    for copy in (*label_swap, *swap, *halo):
        copy.wait_send()
    every = ring.at[pl.ds(1, SLOTS - 1)]
    remote(every, every, ring_ssem, ring_rsem.at[0, 0], along(1)).wait_send()

    loads[14].wait()
    water_whole.wait_recv()
    water = run_send[0]
    for b in range(1, GROUP):
        water = water + run_recv[b]
    river[...] = store[...] + water

    for copy in flux_whole:
        copy.wait_recv()

    same, other = flux_send[0], flux_recv[1]
    for b in range(2, GROUP, 2):
        same = same + flux_recv[b]
        other = other + flux_recv[b + 1]
    pair = [jnp.where(core == 0, same, other), jnp.where(core == 0, other, same)]

    g4 = jnp.stack(
        [frac[...] * pair[f // 2][(f % 2) * ROWS : (f % 2 + 1) * ROWS] for f in range(FIELDS)],
        axis=0,
    )
    ends = [pair[f // 2][2 * ROWS + 2 * (f % 2) : 2 * ROWS + 2 * (f % 2) + 2] for f in range(FIELDS)]
    frac_above = jnp.where(first, 0.0, hr_up[LEV, 1:2, :])
    frac_below = jnp.where(last, 0.0, hr_dn[LEV, 0:1, :])
    above = jnp.stack([frac_above * x[0:1] for x in ends], axis=0)
    below = jnp.stack([frac_below * x[1:2] for x in ends], axis=0)
    lap = laplacian(g4, above, below)
    for i in range(GROUPS):
        high, low = split(
            jnp.concatenate(
                [x[:, 8 * i : 8 * i + 8].reshape(8 * FIELDS, COLS) for x in (g4, lap)], axis=0
            )
        )
        forced[i] = jnp.concatenate([high, low, high], axis=0)

    for copy in (*flux_whole, water_whole):
        copy.wait_send()


def finish(base2, kab, forced, river, out_h, river_h, out, sems):
    river_copy = pltpu.make_async_copy(river, river_h.at[0], sems.at[GROUPS])
    river_copy.start()
    copies = []
    for i in range(0, GROUPS, 2):
        delta = mm(kab[...], jnp.concatenate([forced[i], forced[i + 1]], axis=1))
        for j in range(2):
            part = delta[:, COLS * j : COLS * (j + 1)].reshape(PAD, 8, COLS)
            out[i + j] = base2[i + j] + part
            copies.append(
                pltpu.make_async_copy(
                    out.at[i + j, pl.ds(0, LEV)],
                    out_h.at[0, :, pl.ds(8 * (i + j), 8)],
                    sems.at[i + j],
                )
            )
            copies[-1].start()
    for copy in (*copies, river_copy):
        copy.wait()


def shards(
    state, frac, diff, ops, weight, fo, fr, fb, ro, rr, rb, store,
):
    ops = jnp.transpose(ops, (1, 0, 2))
    fo, ro = fo.reshape(1, ROWS), ro.reshape(1, ROWS)
    args = (state, frac, diff, ops, weight, fo, fr, fb, ro, rr, rb, store)
    args = [pltpu.with_memory_space_constraint(x, pltpu.HBM) for x in args]
    vmem = pltpu.VMEM
    far = pl.BlockSpec(memory_space=pltpu.HBM)
    near = pl.BlockSpec(memory_space=vmem)
    dma = pltpu.SemaphoreType.DMA
    i32 = jnp.int32
    inner = pl.pallas_call(
        kernel,
        out_shape=(
            vmem((GROUPS, PAD, 8, COLS), F32),
            vmem((PAD * 8, 3 * 16 * FIELDS), BF16),
            vmem((GROUPS, 3 * 16 * FIELDS, COLS), BF16),
            vmem((ROWS, COLS), F32),
        ),
        in_specs=[far] * 12,
        out_specs=(near,) * 4,
        scratch_shapes=[
            vmem((GROUPS + 2, PAD, 8, COLS), F32),
            vmem((ROWS, COLS), F32),
            vmem((1, LEV), F32),
            vmem((LEV, 1, LEV), F32),
            vmem((NW, COLS, COLS), F32),
            vmem((1, ROWS), i32),
            vmem((1, ROWS), i32),
            vmem((1, ROWS), i32),
            vmem((1, ROWS), i32),
            vmem((1, ROWS), i32),
            vmem((1, ROWS), i32),
            vmem((ROWS, COLS), F32),
            dma((15,)),
            vmem((PAD, 2, COLS), F32),
            vmem((PAD, 2, COLS), F32),
            vmem((PAD, 2, COLS), F32),
            vmem((PAD, 2, COLS), F32),
            dma((2,)),
            dma((2,)),
            vmem((FIELDS, ROWS, COLS), F32),
            vmem((1, COLS), F32),
            vmem((2, 1, COLS), F32),
            dma((2 + 2 * NC,)),
            dma((2 + 2 * NC,)),
            vmem((SLOTS, SLOT, COLS), F32),
            dma(()),
            dma((len(PIECES), SLOTS)),
            vmem((MAIN + EDGE, COLS), F32),
            vmem((2, EDGE, COLS), F32),
            vmem((GROUP, BLOCK, COLS), F32),
            vmem((GROUP, BLOCK, COLS), F32),
            vmem((GROUP, ROWS, COLS), F32),
            vmem((GROUP, ROWS, COLS), F32),
            dma((3,)),
            dma((3,)),
            vmem((PAD * 8, COLS), F32),
            vmem((PAD * 8, PAD * 8), BF16),
            vmem((PAD * 8, PAD * 8), BF16),
            vmem((GROUPS + 2, PAD, 8, COLS), F32),
        ],
        compiler_params=pltpu.CompilerParams(
            collective_id=0, has_side_effects=True, vmem_limit_bytes=32 * 1024 * 1024
        ),
        name="coupling",
    )(*args)
    inner = [pltpu.with_memory_space_constraint(x, vmem) for x in inner]
    return pl.pallas_call(
        finish,
        out_shape=(
            pltpu.HBM((1, LEV, ROWS, COLS), F32),
            pltpu.HBM((1, ROWS, COLS), F32),
        ),
        in_specs=[near] * 4,
        out_specs=(far, far),
        scratch_shapes=[vmem((GROUPS, PAD, 8, COLS), F32), dma((GROUPS + 1,))],
        compiler_params=pltpu.CompilerParams(vmem_limit_bytes=16 * 1024 * 1024),
        name="finish",
    )(*inner)


def solution(mesh):
    in_specs = (
        P("sec", None, "dom", None),
        P("sec", "dom", None),
        P("sec", None),
        P("sec", None, None),
        P("sec", "dom", None, None),
        P("sec", "dom", None),
        P("sec", "dom"),
        P("sec", "dom"),
        P("sec", "dom", None),
        P("sec", "dom"),
        P("sec", "dom"),
        P("sec", "dom", None),
    )
    out_specs = (P("sec", None, "dom", None), P("sec", "dom", None))
    return jax.shard_map(shards, mesh=mesh, in_specs=in_specs, out_specs=out_specs, check_vma=False)
```

```python
import jax
import jax.numpy as jnp
from jax import lax
from jax.experimental import pallas as pl
from jax.experimental.pallas import tpu as pltpu
from jax.sharding import PartitionSpec as P

MESH = pl.DeviceIdType.MESH
F32 = jnp.float32
BF16 = jnp.bfloat16

LEV = 30
PAD = 32
COLS = 128
ROWS = 32
FIELDS = 4
NW = 8
NY, NZ, NC = 4, 16, 2
N_DOM = NY * NZ * NC
GROUP = NY * NC
HALF = NZ // 2
SLOTS = NZ
GROUPS = ROWS // 8
MAIN = GROUP * ROWS
EDGE = GROUP * 2
WATER_LABEL = ROWS
FLUX = WATER_LABEL + 8
SLOT = FLUX + 2 * NC * ROWS
WATER, FLUX_PIECES = 0, (1, 2, 3, 4)
PIECES = (
    (0, FLUX),
    *[(FLUX + n * ROWS, ROWS) for n in range(2 * NC)],
)
FLUX_LABEL = len(PIECES)
BLOCK = 2 * ROWS + 8


def tree(jumps):
    levels, reached = {}, 0
    for level, jump in enumerate(jumps, 1):
        levels[level] = [(reached, reached + i) for i in range(jump, 0, -1)]
        reached += jump
    return levels


WATER_TREES = tree((2, 1, 2, 1, 2)), tree((1, 2, 1, 2, 1))
FLUX_TREES = tree((2, 2, 2, 2)), tree((1, 2, 2, 2))
LEVELS = len(FLUX_TREES[0])


def split(x):
    high = x.astype(BF16)
    return high, (x - high.astype(F32)).astype(BF16)


def mm(a, b):
    return jnp.dot(a, b, preferred_element_type=F32)


def mm3(a, b):
    (ah, al), (bh, bl) = a, b
    return mm(ah, bh) + (mm(ah, bl) + mm(al, bh))


def iota(shape, dim):
    return lax.broadcasted_iota(jnp.int32, shape, dim)


def neighbours_in_columns(x):
    axis = x.ndim - 1
    return pltpu.roll(x, 1, axis) + pltpu.roll(x, COLS - 1, axis)


def laplacian(x, above, below):
    row, count = iota(x.shape, 1), x.shape[1]
    down = jnp.where(row == 0, above, pltpu.roll(x, 1, 1))
    up = jnp.where(row == count - 1, below, pltpu.roll(x, count - 1, 1))
    return down + up + neighbours_in_columns(x) - 4.0 * x


def kernel(
    state_h, frac_h, diff_h, ops_h, weight_h, fo_h, fr_h, fb_h, ro_h, rr_h, rb_h, store_h,
    base2, kab, forced, river,
    st, frac, diff, ops, weight, fo, fr, fb, ro, rr, rb, store,
    local_sem,
    hs_up, hs_dn, hr_up, hr_dn, halo_ssem, halo_rsem,
    terms, label_out, label_in, part_ssem, part_rsem,
    ring, names_in, ring_ssem, names_ssem, ring_rsem, row_of, ends_acc,
    flux_send, flux_recv, run_send, run_recv, rs_ssem, rs_rsem,
    dcol, kron_h, kron_l, base1,
):
    sec = lax.axis_index("sec")
    me = lax.axis_index("dom")
    core = me & (NC - 1)
    z = (me >> 1) & (NZ - 1)
    y = me >> 5

    def dom_of(yy, zz, cc):
        return (yy * NZ + zz) * NC + cc

    def along(distance):
        return (sec, dom_of(y, (z + NZ + distance) & (NZ - 1), core))

    partners = [(sec ^ 2, me), (sec ^ 2, me ^ 1)]
    after = (sec, (me + 1) & (N_DOM - 1))
    before = (sec, (me + N_DOM - 1) & (N_DOM - 1))

    def member(b):
        return (sec, dom_of((y + b // NC) & (NY - 1), z, core ^ (b % NC)))

    barrier = pltpu.get_barrier_semaphore()
    peers = [*partners, *[along(d) for d in (1, -1, 2, -2)], after, before]
    peers += [member(b) for b in range(1, GROUP)]
    for peer in peers:
        pl.semaphore_signal(barrier, inc=1, device_id=peer, device_id_type=MESH)

    pairs = [(weight_h.at[0], weight)]
    pairs += [
        (state_h.at[0, :, pl.ds(8 * i, 8)], st.at[1 + i, pl.ds(0, LEV)]) for i in range(GROUPS)
    ]
    pairs += [
        (fb_h, fb), (rb_h, rb), (fo_h, fo), (fr_h, fr), (ro_h, ro), (rr_h, rr),
        (frac_h.at[0], frac), (ops_h, ops), (diff_h, diff), (store_h.at[0], store),
    ]
    loads = [pltpu.make_async_copy(a, b, local_sem.at[i]) for i, (a, b) in enumerate(pairs)]
    for copy in loads:
        copy.start()

    for copy in loads[5:11]:
        copy.wait()

    def label_of(owner, row):
        eye = iota((ROWS, ROWS), 0) == iota((ROWS, ROWS), 1)
        target = (owner[...] * ROWS + row[...]).astype(F32)
        rows = jnp.broadcast_to(target, (ROWS, ROWS))
        column = jnp.sum(jnp.where(eye, rows, 0.0), axis=1, keepdims=True)
        wide = jnp.broadcast_to(column, (ROWS, COLS))
        place = iota((ROWS, COLS), 0) == (iota((ROWS, COLS), 1) & (ROWS - 1))
        return jnp.sum(jnp.where(place, wide, 0.0), axis=0, keepdims=True)

    label_out[...] = label_of(fo, fr)
    ring[0, WATER_LABEL:FLUX, :] = jnp.broadcast_to(label_of(ro, rr), (8, COLS))

    tall = FIELDS * ROWS + ROWS
    spot = (iota((tall, ROWS), 0) & (ROWS - 1)) == iota((tall, ROWS), 1)
    blocks = jnp.where(
        iota((tall, ROWS), 0) < FIELDS * ROWS,
        jnp.broadcast_to(fb[...].astype(F32), (tall, ROWS)),
        jnp.broadcast_to(rb[...].astype(F32), (tall, ROWS)),
    )
    block = jnp.sum(jnp.where(spot, blocks, 0.0), axis=1, keepdims=True)
    block = jnp.broadcast_to(jnp.concatenate([block, block], axis=0), (2 * tall, COLS))
    for copy in loads[1:5]:
        copy.wait()
    surface = jnp.concatenate(
        [st[1 + i, f] for f in (*range(FIELDS), 0) for i in range(GROUPS)], axis=0
    )
    high = surface.astype(BF16).astype(F32)
    both = jnp.concatenate([high, surface - high], axis=0)
    lhs = jnp.concatenate(
        [jnp.where(block == float(w), both, 0.0).astype(BF16) for w in range(NW)], axis=1
    )
    loads[0].wait()
    rhs = jnp.concatenate(split(weight[...].reshape(NW * COLS, COLS)), axis=1)
    total = mm(lhs, rhs)
    result = total[:tall, :COLS] + (total[:tall, COLS:] + total[tall:, :COLS])
    terms[...] = result[: FIELDS * ROWS].reshape(FIELDS, ROWS, COLS)
    ring[0, :WATER_LABEL, :] = result[FIELDS * ROWS :]

    pl.semaphore_wait(barrier, len(peers))

    def remote(src, dst, ssem, rsem, device):
        return pltpu.make_async_remote_copy(
            src_ref=src, dst_ref=dst, send_sem=ssem, recv_sem=rsem,
            device_id=device, device_id_type=MESH,
        )

    def slot_of(way, distance):
        return 0 if distance == 0 else min(2 * distance - (way > 0), SLOTS - 1)

    def piece(c, slot):
        return names_in.at[slot] if c == FLUX_LABEL else ring.at[slot, pl.ds(*PIECES[c])]

    def hop(c, way, start, end):
        slot = slot_of(way, end)
        return remote(
            piece(c, slot_of(way, start)), piece(c, slot),
            names_ssem if c == FLUX_LABEL else ring_ssem, ring_rsem.at[c, slot],
            along(way * (end - start)),
        )

    arrivals, departures = {}, {}
    for c in range(len(PIECES) + 1):
        for way in (1, -1):
            trees = WATER_TREES if c == WATER else FLUX_TREES
            levels = trees[(c % 2 == 0) != (way > 0)]
            for level, edges in levels.items():
                copies = [hop(c, way, *edge) for edge in edges]
                departures[c, way, level] = (slot_of(way, edges[0][0]), copies)
                for copy, (_, end) in zip(copies, edges):
                    arrivals[c, slot_of(way, end)] = copy

    def arrive(c, slots):
        for slot in slots:
            if (c, slot) in arrivals:
                arrivals.pop((c, slot)).wait_recv()

    def depart(c, level):
        for way in (1, -1):
            if (c, way, level) in departures:
                slot, copies = departures.pop((c, way, level))
                arrive(c, [slot])
                for copy in copies:
                    copy.start()

    label_swap = [
        remote(label_out, label_in.at[i], part_ssem.at[i], part_rsem.at[i], to)
        for i, to in enumerate(partners)
    ]
    swap = []
    for f in range(2):
        for i in range(NC):
            n = NC * f + i
            swap.append(
                remote(
                    terms.at[2 * (core ^ i) + f], ring.at[0, pl.ds(FLUX + n * ROWS, ROWS)],
                    part_ssem.at[2 + n], part_rsem.at[2 + n], partners[i],
                )
            )
    for copy in (*label_swap, *swap):
        copy.start()

    depart(WATER, 1)

    loads[11].wait()
    hs_up[0:LEV] = st[1, 0:LEV, 0:2, :]
    hs_dn[0:LEV] = st[GROUPS, 0:LEV, 6:8, :]
    hs_up[LEV] = frac[0:2, :]
    hs_dn[LEV] = frac[ROWS - 2 : ROWS, :]
    hs_up[LEV + 1] = jnp.zeros((2, COLS), F32)
    hs_dn[LEV + 1] = jnp.zeros((2, COLS), F32)
    for i in range(GROUPS):
        st[1 + i, LEV:PAD] = jnp.zeros((PAD - LEV, 8, COLS), F32)
    halo = [
        remote(hs_dn, hr_up, halo_ssem.at[0], halo_rsem.at[0], after),
        remote(hs_up, hr_dn, halo_ssem.at[1], halo_rsem.at[1], before),
    ]
    for copy in halo:
        copy.start()


    tall8 = PAD * 8
    for copy in loads[12:14]:
        copy.wait()
    pick = ((iota((tall8, LEV), 0) >> 3) == iota((tall8, LEV), 1)).astype(F32)
    pick_t = ((iota((LEV, tall8), 1) >> 3) == iota((LEV, tall8), 0)).astype(BF16)
    column = jnp.sum(pick * jnp.broadcast_to(diff[...], (tall8, LEV)), axis=1, keepdims=True)
    dcol[...] = jnp.broadcast_to(column, (tall8, COLS))
    op = ops[:, 0, :]
    op_h, op_l = split(op)
    op_r = (op - op_h.astype(F32) - op_l.astype(F32)).astype(BF16)
    pick = pick.astype(BF16)
    spread = mm(mm(pick, op_h).astype(BF16), pick_t) + (
        mm(mm(pick, op_l).astype(BF16), pick_t) + mm(mm(pick, op_r).astype(BF16), pick_t)
    )
    same8 = (iota((tall8, tall8), 0) & 7) == (iota((tall8, tall8), 1) & 7)
    kh, kl = split(jnp.where(same8, spread, 0.0))
    kron_h[...] = kh
    kron_l[...] = kl

    def block_start(b):
        return dom_of((y + (b >> 1)) & (NY - 1), z, core ^ (b & 1)) * ROWS

    i = iota((MAIN, COLS), 0)
    row_of[:MAIN] = (block_start(i >> 5) + (i & (ROWS - 1))).astype(F32)
    i = iota((EDGE, COLS), 0)
    row_of[MAIN:] = (block_start(i >> 1) + jnp.where((i & 1) == 0, -1, ROWS)).astype(F32)
    flux_send[:, 2 * ROWS + 4 :, :] = jnp.zeros((GROUP, 4, COLS), F32)

    def kab_work():
        k4 = kron_h[:, : 8 * FIELDS].astype(F32) + kron_l[:, : 8 * FIELDS].astype(F32)
        eye = (iota(k4.shape, 0) == iota(k4.shape, 1)).astype(F32)
        q = jnp.concatenate([k4 + eye, dcol[:, : 8 * FIELDS] * k4], axis=1)
        kh, kl = split(mm3((kron_h[...], kron_l[...]), split(q)))
        kab[...] = jnp.concatenate([kh, kh, kl], axis=1)

    first = me == 0
    last = me == N_DOM - 1

    def apply(*groups):
        u = jnp.concatenate([u.reshape(PAD * 8, COLS) for u in groups], axis=1)
        out = mm3((kron_h[...], kron_l[...]), split(u))
        return [
            out[:, COLS * i : COLS * (i + 1)].reshape(PAD, 8, COLS) for i in range(len(groups))
        ]

    def diffused(i, source):
        x = source[i]
        lap = laplacian(x, source[i - 1, :, 7:8], source[i + 1, :, 0:1])
        return x + dcol[...].reshape(PAD, 8, COLS) * lap

    def step_one(i, j):
        base1[i], base1[j] = apply(diffused(i, st), diffused(j, st))

    def step_two(i, j):
        base2[i - 1], base2[j - 1] = apply(diffused(i, base1), diffused(j, base1))

    def step_one_ends():
        d = dcol[...].reshape(PAD, 8, COLS)
        spot = iota((PAD, 8, COLS), 1)
        above, below = st[0], st[GROUPS + 1]
        x = jnp.where(spot == 7, above[:, 7:8], below[:, 0:1])
        outer = jnp.where(spot == 7, above[:, 6:7], below[:, 1:2])
        inner = jnp.where(spot == 7, st[1, :, 0:1], st[GROUPS, :, 7:8])
        u = x + d * (outer + inner + neighbours_in_columns(x) - 4.0 * x)
        gone = ((spot == 7) & first) | ((spot < 7) & last)
        (ends,) = apply(jnp.where(gone, 0.0, u))
        base1[0] = ends
        base1[GROUPS + 1] = ends

    step_one(2, 3)
    depart(WATER, 2)
    for i, copy in enumerate(label_swap):
        copy.wait_recv()
        names_in[0, i : i + 1, :] = label_in[i]
    depart(FLUX_LABEL, 1)
    for c in FLUX_PIECES:
        swap[c - 1].wait_recv()
        depart(c, 1)
    depart(WATER, 3)

    def joined(rows):
        lane = iota((1, COLS), 1) >> 5
        names = rows[0]
        for i in range(1, 4):
            names = jnp.where(lane == i, rows[i], names)
        return names

    def one_hot(rows, names):
        return (rows == jnp.broadcast_to(names, rows.shape)).astype(F32).astype(BF16)

    selected = {}

    def select_flux(j):
        if j not in selected:
            selected[j] = make_selection(j)
        return selected[j]

    def make_selection(j):
        arrive(FLUX_LABEL, (2 * j, 2 * j + 1))
        rows = []
        for i in range(4):
            rows.append(names_in[2 * j + i // 2, i % 2 : i % 2 + 1, :])
        return one_hot(row_of[...], joined(rows))

    def rows_of(f, slots):
        start = FLUX + f * NC * ROWS
        for c in FLUX_PIECES[NC * f : NC * (f + 1)]:
            arrive(c, slots)
        return jnp.concatenate([ring[n, start : start + NC * ROWS, :] for n in slots], axis=0)

    def place_flux(first_slot, last_slot, fields, fresh):
        sel = [select_flux(j) for j in range(first_slot // 2, last_slot // 2)]
        data = [rows_of(f, range(first_slot, last_slot)) for f in fields]
        high, low = split(jnp.concatenate(data, axis=1))
        part = mm(jnp.concatenate([*sel, *sel], axis=1), jnp.concatenate([high, low], axis=0))
        for i, f in enumerate(fields):
            one = part[:, i * COLS : (i + 1) * COLS]
            rows = slice(f * ROWS, (f + 1) * ROWS)
            main = one[:MAIN].reshape(GROUP, ROWS, COLS)
            flux_send[:, rows, :] = main if fresh else flux_send[:, rows, :] + main
            ends_acc[f] = one[MAIN:] if fresh else ends_acc[f] + one[MAIN:]

    def place_water():
        arrive(WATER, range(SLOTS))
        rows = [ring[slot, :WATER_LABEL, :] for slot in range(SLOTS)]
        high, low = split(jnp.concatenate(rows, axis=0))
        labels = [ring[slot, WATER_LABEL : WATER_LABEL + 1, :] for slot in range(SLOTS)]
        sel = [
            one_hot(row_of[:MAIN], joined(labels[4 * g : 4 * g + 4])) for g in range(SLOTS // 4)
        ]
        part = mm(jnp.concatenate([*sel, *sel], axis=1), jnp.concatenate([high, low], axis=0))
        run_send[...] = part.reshape(GROUP, ROWS, COLS)
        for copy in water_scatter:
            copy.start()

    order = [4, 5, 2, 3, 6, 7, 1]

    def scatter_copies(src, dst, c, rows):
        return [
            remote(src.at[b, rows], dst.at[b, rows], rs_ssem.at[c], rs_rsem.at[c], member(b))
            for b in order
        ]

    def whole(src, dst, c, rows):
        others = pl.ds(1, GROUP - 1)
        return remote(
            src.at[others, rows], dst.at[others, rows], rs_ssem.at[c], rs_rsem.at[c], member(1)
        )

    kinds = [
        (run_send, run_recv, 0, pl.ds(0, ROWS)),
        (flux_send, flux_recv, 1, pl.ds(0, ROWS)),
        (flux_send, flux_recv, 2, pl.ds(ROWS, BLOCK - ROWS)),
    ]
    water_scatter, *flux_scatter = [scatter_copies(*kind) for kind in kinds]
    water_whole, *flux_whole = [whole(*kind) for kind in kinds]

    for level in range(2, LEVELS + 1):
        for c in (FLUX_LABEL, *FLUX_PIECES):
            depart(c, level)
        depart(WATER, level + 2)
        if level == LEVELS:
            place_water()
    place_flux(0, 10, (0, 1), True)
    for f in range(2):
        place_flux(10, SLOTS, (f,), False)
        if f == 1:
            for b in range(GROUP):
                for e in range(2):
                    ends = 2 * ROWS + 2 * e
                    flux_send[b, ends : ends + 2, :] = ends_acc[e, 2 * b : 2 * b + 2]
        for copy in flux_scatter[f]:
            copy.start()

    for copy in halo:
        copy.wait_recv()
    st[0, :, 6:8, :] = jnp.where(first, 0.0, hr_up[...])
    st[GROUPS + 1, :, 0:2, :] = jnp.where(last, 0.0, hr_dn[...])
    step_one(1, 4)
    step_one_ends()
    step_two(1, 2)
    step_two(3, 4)
    kab_work()
    for copy in (*label_swap, *swap, *halo):
        copy.wait_send()
    every = ring.at[pl.ds(1, SLOTS - 1)]
    remote(every, every, ring_ssem, ring_rsem.at[0, 0], along(1)).wait_send()
    every = names_in.at[pl.ds(1, SLOTS - 1)]
    remote(every, every, names_ssem, ring_rsem.at[0, 0], along(1)).wait_send()

    loads[14].wait()
    water_whole.wait_recv()
    water = run_send[0]
    for b in range(1, GROUP):
        water = water + run_recv[b]
    river[...] = store[...] + water

    for copy in flux_whole:
        copy.wait_recv()

    same, other = flux_send[0], flux_recv[1]
    for b in range(2, GROUP, 2):
        same = same + flux_recv[b]
        other = other + flux_recv[b + 1]
    pair = [jnp.where(core == 0, same, other), jnp.where(core == 0, other, same)]

    g4 = jnp.stack(
        [frac[...] * pair[f // 2][(f % 2) * ROWS : (f % 2 + 1) * ROWS] for f in range(FIELDS)],
        axis=0,
    )
    ends = [pair[f // 2][2 * ROWS + 2 * (f % 2) : 2 * ROWS + 2 * (f % 2) + 2] for f in range(FIELDS)]
    frac_above = jnp.where(first, 0.0, hr_up[LEV, 1:2, :])
    frac_below = jnp.where(last, 0.0, hr_dn[LEV, 0:1, :])
    above = jnp.stack([frac_above * x[0:1] for x in ends], axis=0)
    below = jnp.stack([frac_below * x[1:2] for x in ends], axis=0)
    lap = laplacian(g4, above, below)
    for i in range(GROUPS):
        high, low = split(
            jnp.concatenate(
                [x[:, 8 * i : 8 * i + 8].reshape(8 * FIELDS, COLS) for x in (g4, lap)], axis=0
            )
        )
        forced[i] = jnp.concatenate([high, low, high], axis=0)

    for copy in (*flux_whole, water_whole):
        copy.wait_send()


def finish(base2, kab, forced, river, out_h, river_h, out, sems):
    river_copy = pltpu.make_async_copy(river, river_h.at[0], sems.at[GROUPS])
    river_copy.start()
    copies = []
    for i in range(0, GROUPS, 2):
        delta = mm(kab[...], jnp.concatenate([forced[i], forced[i + 1]], axis=1))
        for j in range(2):
            part = delta[:, COLS * j : COLS * (j + 1)].reshape(PAD, 8, COLS)
            out[i + j] = base2[i + j] + part
            copies.append(
                pltpu.make_async_copy(
                    out.at[i + j, pl.ds(0, LEV)],
                    out_h.at[0, :, pl.ds(8 * (i + j), 8)],
                    sems.at[i + j],
                )
            )
            copies[-1].start()
    for copy in (*copies, river_copy):
        copy.wait()


def shards(
    state, frac, diff, ops, weight, fo, fr, fb, ro, rr, rb, store,
):
    ops = jnp.transpose(ops, (1, 0, 2))
    fo, ro = fo.reshape(1, ROWS), ro.reshape(1, ROWS)
    args = (state, frac, diff, ops, weight, fo, fr, fb, ro, rr, rb, store)
    args = [pltpu.with_memory_space_constraint(x, pltpu.HBM) for x in args]
    vmem = pltpu.VMEM
    far = pl.BlockSpec(memory_space=pltpu.HBM)
    near = pl.BlockSpec(memory_space=vmem)
    dma = pltpu.SemaphoreType.DMA
    i32 = jnp.int32
    inner = pl.pallas_call(
        kernel,
        out_shape=(
            vmem((GROUPS, PAD, 8, COLS), F32),
            vmem((PAD * 8, 3 * 16 * FIELDS), BF16),
            vmem((GROUPS, 3 * 16 * FIELDS, COLS), BF16),
            vmem((ROWS, COLS), F32),
        ),
        in_specs=[far] * 12,
        out_specs=(near,) * 4,
        scratch_shapes=[
            vmem((GROUPS + 2, PAD, 8, COLS), F32),
            vmem((ROWS, COLS), F32),
            vmem((1, LEV), F32),
            vmem((LEV, 1, LEV), F32),
            vmem((NW, COLS, COLS), F32),
            vmem((1, ROWS), i32),
            vmem((1, ROWS), i32),
            vmem((1, ROWS), i32),
            vmem((1, ROWS), i32),
            vmem((1, ROWS), i32),
            vmem((1, ROWS), i32),
            vmem((ROWS, COLS), F32),
            dma((15,)),
            vmem((PAD, 2, COLS), F32),
            vmem((PAD, 2, COLS), F32),
            vmem((PAD, 2, COLS), F32),
            vmem((PAD, 2, COLS), F32),
            dma((2,)),
            dma((2,)),
            vmem((FIELDS, ROWS, COLS), F32),
            vmem((1, COLS), F32),
            vmem((2, 1, COLS), F32),
            dma((2 + 2 * NC,)),
            dma((2 + 2 * NC,)),
            vmem((SLOTS, SLOT, COLS), F32),
            vmem((SLOTS, 2, COLS), F32),
            dma(()),
            dma(()),
            dma((len(PIECES) + 1, SLOTS)),
            vmem((MAIN + EDGE, COLS), F32),
            vmem((2, EDGE, COLS), F32),
            vmem((GROUP, BLOCK, COLS), F32),
            vmem((GROUP, BLOCK, COLS), F32),
            vmem((GROUP, ROWS, COLS), F32),
            vmem((GROUP, ROWS, COLS), F32),
            dma((3,)),
            dma((3,)),
            vmem((PAD * 8, COLS), F32),
            vmem((PAD * 8, PAD * 8), BF16),
            vmem((PAD * 8, PAD * 8), BF16),
            vmem((GROUPS + 2, PAD, 8, COLS), F32),
        ],
        compiler_params=pltpu.CompilerParams(
            collective_id=0, has_side_effects=True, vmem_limit_bytes=32 * 1024 * 1024
        ),
        name="coupling",
    )(*args)
    inner = [pltpu.with_memory_space_constraint(x, vmem) for x in inner]
    return pl.pallas_call(
        finish,
        out_shape=(
            pltpu.HBM((1, LEV, ROWS, COLS), F32),
            pltpu.HBM((1, ROWS, COLS), F32),
        ),
        in_specs=[near] * 4,
        out_specs=(far, far),
        scratch_shapes=[vmem((GROUPS, PAD, 8, COLS), F32), dma((GROUPS + 1,))],
        compiler_params=pltpu.CompilerParams(vmem_limit_bytes=16 * 1024 * 1024),
        name="finish",
    )(*inner)


def solution(mesh):
    in_specs = (
        P("sec", None, "dom", None),
        P("sec", "dom", None),
        P("sec", None),
        P("sec", None, None),
        P("sec", "dom", None, None),
        P("sec", "dom", None),
        P("sec", "dom"),
        P("sec", "dom"),
        P("sec", "dom", None),
        P("sec", "dom"),
        P("sec", "dom"),
        P("sec", "dom", None),
    )
    out_specs = (P("sec", None, "dom", None), P("sec", "dom", None))
    return jax.shard_map(shards, mesh=mesh, in_specs=in_specs, out_specs=out_specs, check_vma=False)
```

```python
import jax
import jax.numpy as jnp
from jax import lax
from jax.experimental import pallas as pl
from jax.experimental.pallas import tpu as pltpu
from jax.sharding import PartitionSpec as P

MESH = pl.DeviceIdType.MESH
F32 = jnp.float32
BF16 = jnp.bfloat16

LEV = 30
PAD = 32
COLS = 128
ROWS = 32
FIELDS = 4
NW = 8
NY, NZ, NC = 4, 16, 2
N_DOM = NY * NZ * NC
GROUP = NY * NC
HALF = NZ // 2
SLOTS = NZ
GROUPS = ROWS // 8
MAIN = GROUP * ROWS
EDGE = GROUP * 2
WATER_LABEL = ROWS
FLUX = WATER_LABEL + 8
SLOT = FLUX + 2 * NC * ROWS
WATER, FLUX_PIECES = 0, (1, 2, 3, 4)
PIECES = (
    (0, FLUX),
    *[(FLUX + n * ROWS, ROWS) for n in range(2 * NC)],
)
FLUX_LABEL = len(PIECES)
BLOCK = 2 * ROWS + 8


def tree(jumps):
    levels, reached = {}, 0
    for level, jump in enumerate(jumps, 1):
        levels[level] = [(reached, reached + i) for i in range(jump, 0, -1)]
        reached += jump
    return levels


WATER_TREES = tree((2, 1, 2, 1, 2)), tree((1, 2, 1, 2, 1))
FLUX_TREES = tree((2, 2, 2, 2)), tree((1, 2, 2, 2))
LEVELS = len(FLUX_TREES[0])


def split(x):
    high = x.astype(BF16)
    return high, (x - high.astype(F32)).astype(BF16)


def mm(a, b):
    return jnp.dot(a, b, preferred_element_type=F32)


def mm3(a, b):
    (ah, al), (bh, bl) = a, b
    return mm(ah, bh) + (mm(ah, bl) + mm(al, bh))


def iota(shape, dim):
    return lax.broadcasted_iota(jnp.int32, shape, dim)


def neighbours_in_columns(x):
    axis = x.ndim - 1
    return pltpu.roll(x, 1, axis) + pltpu.roll(x, COLS - 1, axis)


def laplacian(x, above, below):
    row, count = iota(x.shape, 1), x.shape[1]
    down = jnp.where(row == 0, above, pltpu.roll(x, 1, 1))
    up = jnp.where(row == count - 1, below, pltpu.roll(x, count - 1, 1))
    return down + up + neighbours_in_columns(x) - 4.0 * x


def kernel(
    state_h, frac_h, diff_h, ops_h, weight_h, fo_h, fr_h, fb_h, ro_h, rr_h, rb_h, store_h,
    base2, kab, forced, river,
    st, frac, diff, ops, weight, fo, fr, fb, ro, rr, rb, store,
    local_sem,
    hs_up, hs_dn, hr_up, hr_dn, halo_ssem, halo_rsem,
    terms, label_out, label_in, part_ssem, part_rsem,
    ring, names_in, ring_ssem, names_ssem, ring_rsem, row_of, ends_acc,
    flux_send, flux_recv, run_send, run_recv, rs_ssem, rs_rsem,
    dcol, kron_h, kron_l, base1,
):
    sec = lax.axis_index("sec")
    me = lax.axis_index("dom")
    core = me & (NC - 1)
    z = (me >> 1) & (NZ - 1)
    y = me >> 5

    def dom_of(yy, zz, cc):
        return (yy * NZ + zz) * NC + cc

    def along(distance):
        return (sec, dom_of(y, (z + NZ + distance) & (NZ - 1), core))

    partners = [(sec ^ 2, me), (sec ^ 2, me ^ 1)]
    after = (sec, (me + 1) & (N_DOM - 1))
    before = (sec, (me + N_DOM - 1) & (N_DOM - 1))

    def member(b):
        return (sec, dom_of((y + b // NC) & (NY - 1), z, core ^ (b % NC)))

    barrier = pltpu.get_barrier_semaphore()
    peers = [*partners, *[along(d) for d in (1, -1, 2, -2)], after, before]
    peers += [member(b) for b in range(1, GROUP)]
    for peer in peers:
        pl.semaphore_signal(barrier, inc=1, device_id=peer, device_id_type=MESH)

    pairs = [(weight_h.at[0], weight)]
    pairs += [
        (state_h.at[0, :, pl.ds(8 * i, 8)], st.at[1 + i, pl.ds(0, LEV)]) for i in range(GROUPS)
    ]
    pairs += [
        (fb_h, fb), (rb_h, rb), (fo_h, fo), (fr_h, fr), (ro_h, ro), (rr_h, rr),
        (frac_h.at[0], frac), (ops_h, ops), (diff_h, diff), (store_h.at[0], store),
    ]
    loads = [pltpu.make_async_copy(a, b, local_sem.at[i]) for i, (a, b) in enumerate(pairs)]
    for copy in loads:
        copy.start()

    for copy in loads[5:11]:
        copy.wait()

    def label_of(owner, row):
        eye = iota((ROWS, ROWS), 0) == iota((ROWS, ROWS), 1)
        target = (owner[...] * ROWS + row[...]).astype(F32)
        rows = jnp.broadcast_to(target, (ROWS, ROWS))
        column = jnp.sum(jnp.where(eye, rows, 0.0), axis=1, keepdims=True)
        wide = jnp.broadcast_to(column, (ROWS, COLS))
        place = iota((ROWS, COLS), 0) == (iota((ROWS, COLS), 1) & (ROWS - 1))
        return jnp.sum(jnp.where(place, wide, 0.0), axis=0, keepdims=True)

    label_out[...] = label_of(fo, fr)
    ring[0, WATER_LABEL:FLUX, :] = jnp.broadcast_to(label_of(ro, rr), (8, COLS))

    tall = FIELDS * ROWS + ROWS
    spot = (iota((tall, ROWS), 0) & (ROWS - 1)) == iota((tall, ROWS), 1)
    blocks = jnp.where(
        iota((tall, ROWS), 0) < FIELDS * ROWS,
        jnp.broadcast_to(fb[...].astype(F32), (tall, ROWS)),
        jnp.broadcast_to(rb[...].astype(F32), (tall, ROWS)),
    )
    block = jnp.sum(jnp.where(spot, blocks, 0.0), axis=1, keepdims=True)
    block = jnp.broadcast_to(jnp.concatenate([block, block], axis=0), (2 * tall, COLS))
    for copy in loads[1:5]:
        copy.wait()
    surface = jnp.concatenate(
        [st[1 + i, f] for f in (*range(FIELDS), 0) for i in range(GROUPS)], axis=0
    )
    high = surface.astype(BF16).astype(F32)
    both = jnp.concatenate([high, surface - high], axis=0)
    lhs = jnp.concatenate(
        [jnp.where(block == float(w), both, 0.0).astype(BF16) for w in range(NW)], axis=1
    )
    loads[0].wait()
    rhs = jnp.concatenate(split(weight[...].reshape(NW * COLS, COLS)), axis=1)
    total = mm(lhs, rhs)
    result = total[:tall, :COLS] + (total[:tall, COLS:] + total[tall:, :COLS])
    terms[...] = result[: FIELDS * ROWS].reshape(FIELDS, ROWS, COLS)
    ring[0, :WATER_LABEL, :] = result[FIELDS * ROWS :]

    pl.semaphore_wait(barrier, len(peers))

    def remote(src, dst, ssem, rsem, device):
        return pltpu.make_async_remote_copy(
            src_ref=src, dst_ref=dst, send_sem=ssem, recv_sem=rsem,
            device_id=device, device_id_type=MESH,
        )

    def slot_of(way, distance):
        return 0 if distance == 0 else min(2 * distance - (way > 0), SLOTS - 1)

    def piece(c, slot):
        return names_in.at[slot] if c == FLUX_LABEL else ring.at[slot, pl.ds(*PIECES[c])]

    def hop(c, way, start, end):
        slot = slot_of(way, end)
        return remote(
            piece(c, slot_of(way, start)), piece(c, slot),
            names_ssem if c == FLUX_LABEL else ring_ssem, ring_rsem.at[c, slot],
            along(way * (end - start)),
        )

    arrivals, departures = {}, {}
    for c in range(len(PIECES) + 1):
        for way in (1, -1):
            trees = WATER_TREES if c == WATER else FLUX_TREES
            levels = trees[(c % 2 == 0) != (way > 0)]
            for level, edges in levels.items():
                copies = [hop(c, way, *edge) for edge in edges]
                departures[c, way, level] = (slot_of(way, edges[0][0]), copies)
                for copy, (_, end) in zip(copies, edges):
                    arrivals[c, slot_of(way, end)] = copy

    def arrive(c, slots):
        for slot in slots:
            if (c, slot) in arrivals:
                arrivals.pop((c, slot)).wait_recv()

    def depart(c, level):
        for way in (1, -1):
            if (c, way, level) in departures:
                slot, copies = departures.pop((c, way, level))
                arrive(c, [slot])
                for copy in copies:
                    copy.start()

    right_first = (z >= 2) & (z <= 9)

    def depart_by_way(pieces, level):
        steps = {1: [], -1: []}
        for way in steps:
            for c in pieces:
                if (c, way, level) in departures:
                    slot, copies = departures.pop((c, way, level))
                    steps[way].append((arrivals.pop((c, slot), None), copies))

        def run(ways):
            for way in ways:
                for arrival, copies in steps[way]:
                    if arrival is not None:
                        arrival.wait_recv()
                    for copy in copies:
                        copy.start()

        pl.when(right_first)(lambda: run((1, -1)))
        pl.when(jnp.logical_not(right_first))(lambda: run((-1, 1)))

    label_swap = [
        remote(label_out, label_in.at[i], part_ssem.at[i], part_rsem.at[i], to)
        for i, to in enumerate(partners)
    ]
    swap = []
    for f in range(2):
        for i in range(NC):
            n = NC * f + i
            swap.append(
                remote(
                    terms.at[2 * (core ^ i) + f], ring.at[0, pl.ds(FLUX + n * ROWS, ROWS)],
                    part_ssem.at[2 + n], part_rsem.at[2 + n], partners[i],
                )
            )
    for copy in (*label_swap, *swap):
        copy.start()

    depart(WATER, 1)

    loads[11].wait()
    hs_up[0:LEV] = st[1, 0:LEV, 0:2, :]
    hs_dn[0:LEV] = st[GROUPS, 0:LEV, 6:8, :]
    hs_up[LEV] = frac[0:2, :]
    hs_dn[LEV] = frac[ROWS - 2 : ROWS, :]
    hs_up[LEV + 1] = jnp.zeros((2, COLS), F32)
    hs_dn[LEV + 1] = jnp.zeros((2, COLS), F32)
    for i in range(GROUPS):
        st[1 + i, LEV:PAD] = jnp.zeros((PAD - LEV, 8, COLS), F32)
    halo = [
        remote(hs_dn, hr_up, halo_ssem.at[0], halo_rsem.at[0], after),
        remote(hs_up, hr_dn, halo_ssem.at[1], halo_rsem.at[1], before),
    ]
    for copy in halo:
        copy.start()


    tall8 = PAD * 8
    for copy in loads[12:14]:
        copy.wait()
    pick = ((iota((tall8, LEV), 0) >> 3) == iota((tall8, LEV), 1)).astype(F32)
    pick_t = ((iota((LEV, tall8), 1) >> 3) == iota((LEV, tall8), 0)).astype(BF16)
    column = jnp.sum(pick * jnp.broadcast_to(diff[...], (tall8, LEV)), axis=1, keepdims=True)
    dcol[...] = jnp.broadcast_to(column, (tall8, COLS))
    op = ops[:, 0, :]
    op_h, op_l = split(op)
    op_r = (op - op_h.astype(F32) - op_l.astype(F32)).astype(BF16)
    pick = pick.astype(BF16)
    spread = mm(mm(pick, op_h).astype(BF16), pick_t) + (
        mm(mm(pick, op_l).astype(BF16), pick_t) + mm(mm(pick, op_r).astype(BF16), pick_t)
    )
    same8 = (iota((tall8, tall8), 0) & 7) == (iota((tall8, tall8), 1) & 7)
    kh, kl = split(jnp.where(same8, spread, 0.0))
    kron_h[...] = kh
    kron_l[...] = kl

    def block_start(b):
        return dom_of((y + (b >> 1)) & (NY - 1), z, core ^ (b & 1)) * ROWS

    i = iota((MAIN, COLS), 0)
    row_of[:MAIN] = (block_start(i >> 5) + (i & (ROWS - 1))).astype(F32)
    i = iota((EDGE, COLS), 0)
    row_of[MAIN:] = (block_start(i >> 1) + jnp.where((i & 1) == 0, -1, ROWS)).astype(F32)
    flux_send[:, 2 * ROWS + 4 :, :] = jnp.zeros((GROUP, 4, COLS), F32)

    def kab_work():
        k4 = kron_h[:, : 8 * FIELDS].astype(F32) + kron_l[:, : 8 * FIELDS].astype(F32)
        eye = (iota(k4.shape, 0) == iota(k4.shape, 1)).astype(F32)
        q = jnp.concatenate([k4 + eye, dcol[:, : 8 * FIELDS] * k4], axis=1)
        kh, kl = split(mm3((kron_h[...], kron_l[...]), split(q)))
        kab[...] = jnp.concatenate([kh, kh, kl], axis=1)

    first = me == 0
    last = me == N_DOM - 1

    def apply(*groups):
        u = jnp.concatenate([u.reshape(PAD * 8, COLS) for u in groups], axis=1)
        out = mm3((kron_h[...], kron_l[...]), split(u))
        return [
            out[:, COLS * i : COLS * (i + 1)].reshape(PAD, 8, COLS) for i in range(len(groups))
        ]

    def diffused(i, source):
        x = source[i]
        lap = laplacian(x, source[i - 1, :, 7:8], source[i + 1, :, 0:1])
        return x + dcol[...].reshape(PAD, 8, COLS) * lap

    def step_one(i, j):
        base1[i], base1[j] = apply(diffused(i, st), diffused(j, st))

    def step_two(i, j):
        base2[i - 1], base2[j - 1] = apply(diffused(i, base1), diffused(j, base1))

    def step_one_ends():
        d = dcol[...].reshape(PAD, 8, COLS)
        spot = iota((PAD, 8, COLS), 1)
        above, below = st[0], st[GROUPS + 1]
        x = jnp.where(spot == 7, above[:, 7:8], below[:, 0:1])
        outer = jnp.where(spot == 7, above[:, 6:7], below[:, 1:2])
        inner = jnp.where(spot == 7, st[1, :, 0:1], st[GROUPS, :, 7:8])
        u = x + d * (outer + inner + neighbours_in_columns(x) - 4.0 * x)
        gone = ((spot == 7) & first) | ((spot < 7) & last)
        (ends,) = apply(jnp.where(gone, 0.0, u))
        base1[0] = ends
        base1[GROUPS + 1] = ends

    step_one(2, 3)
    depart(WATER, 2)
    for i, copy in enumerate(label_swap):
        copy.wait_recv()
        names_in[0, i : i + 1, :] = label_in[i]
    depart(FLUX_LABEL, 1)
    for c in FLUX_PIECES:
        swap[c - 1].wait_recv()
        depart(c, 1)
    depart(WATER, 3)

    def joined(rows):
        lane = iota((1, COLS), 1) >> 5
        names = rows[0]
        for i in range(1, 4):
            names = jnp.where(lane == i, rows[i], names)
        return names

    def one_hot(rows, names):
        return (rows == jnp.broadcast_to(names, rows.shape)).astype(F32).astype(BF16)

    selected = {}

    def select_flux(j):
        if j not in selected:
            selected[j] = make_selection(j)
        return selected[j]

    def make_selection(j):
        arrive(FLUX_LABEL, (2 * j, 2 * j + 1))
        rows = []
        for i in range(4):
            rows.append(names_in[2 * j + i // 2, i % 2 : i % 2 + 1, :])
        return one_hot(row_of[...], joined(rows))

    def rows_of(f, slots):
        start = FLUX + f * NC * ROWS
        for c in FLUX_PIECES[NC * f : NC * (f + 1)]:
            arrive(c, slots)
        return jnp.concatenate([ring[n, start : start + NC * ROWS, :] for n in slots], axis=0)

    def place_flux(first_slot, last_slot, fields, fresh):
        sel = [select_flux(j) for j in range(first_slot // 2, last_slot // 2)]
        data = [rows_of(f, range(first_slot, last_slot)) for f in fields]
        high, low = split(jnp.concatenate(data, axis=1))
        part = mm(jnp.concatenate([*sel, *sel], axis=1), jnp.concatenate([high, low], axis=0))
        for i, f in enumerate(fields):
            one = part[:, i * COLS : (i + 1) * COLS]
            rows = slice(f * ROWS, (f + 1) * ROWS)
            main = one[:MAIN].reshape(GROUP, ROWS, COLS)
            flux_send[:, rows, :] = main if fresh else flux_send[:, rows, :] + main
            ends_acc[f] = one[MAIN:] if fresh else ends_acc[f] + one[MAIN:]

    def place_water():
        arrive(WATER, range(SLOTS))
        rows = [ring[slot, :WATER_LABEL, :] for slot in range(SLOTS)]
        high, low = split(jnp.concatenate(rows, axis=0))
        labels = [ring[slot, WATER_LABEL : WATER_LABEL + 1, :] for slot in range(SLOTS)]
        sel = [
            one_hot(row_of[:MAIN], joined(labels[4 * g : 4 * g + 4])) for g in range(SLOTS // 4)
        ]
        part = mm(jnp.concatenate([*sel, *sel], axis=1), jnp.concatenate([high, low], axis=0))
        run_send[...] = part.reshape(GROUP, ROWS, COLS)
        for copy in water_scatter:
            copy.start()

    order = [4, 5, 2, 3, 6, 7, 1]

    def scatter_copies(src, dst, c, rows):
        return [
            remote(src.at[b, rows], dst.at[b, rows], rs_ssem.at[c], rs_rsem.at[c], member(b))
            for b in order
        ]

    def whole(src, dst, c, rows):
        others = pl.ds(1, GROUP - 1)
        return remote(
            src.at[others, rows], dst.at[others, rows], rs_ssem.at[c], rs_rsem.at[c], member(1)
        )

    kinds = [
        (run_send, run_recv, 0, pl.ds(0, ROWS)),
        (flux_send, flux_recv, 1, pl.ds(0, ROWS)),
        (flux_send, flux_recv, 2, pl.ds(ROWS, BLOCK - ROWS)),
    ]
    water_scatter, *flux_scatter = [scatter_copies(*kind) for kind in kinds]
    water_whole, *flux_whole = [whole(*kind) for kind in kinds]

    for level in range(2, LEVELS + 1):
        depart_by_way((FLUX_LABEL, *FLUX_PIECES), level)
        depart(WATER, level + 2)
        if level == LEVELS:
            place_water()
    place_flux(0, 10, (0, 1), True)
    for f in range(2):
        place_flux(10, SLOTS, (f,), False)
        if f == 1:
            for b in range(GROUP):
                for e in range(2):
                    ends = 2 * ROWS + 2 * e
                    flux_send[b, ends : ends + 2, :] = ends_acc[e, 2 * b : 2 * b + 2]
        for copy in flux_scatter[f]:
            copy.start()

    for copy in halo:
        copy.wait_recv()
    st[0, :, 6:8, :] = jnp.where(first, 0.0, hr_up[...])
    st[GROUPS + 1, :, 0:2, :] = jnp.where(last, 0.0, hr_dn[...])
    step_one(1, 4)
    step_one_ends()
    step_two(1, 2)
    step_two(3, 4)
    kab_work()
    for copy in (*label_swap, *swap, *halo):
        copy.wait_send()
    every = ring.at[pl.ds(1, SLOTS - 1)]
    remote(every, every, ring_ssem, ring_rsem.at[0, 0], along(1)).wait_send()
    every = names_in.at[pl.ds(1, SLOTS - 1)]
    remote(every, every, names_ssem, ring_rsem.at[0, 0], along(1)).wait_send()

    loads[14].wait()
    water_whole.wait_recv()
    water = run_send[0]
    for b in range(1, GROUP):
        water = water + run_recv[b]
    river[...] = store[...] + water

    for copy in flux_whole:
        copy.wait_recv()

    same, other = flux_send[0], flux_recv[1]
    for b in range(2, GROUP, 2):
        same = same + flux_recv[b]
        other = other + flux_recv[b + 1]
    pair = [jnp.where(core == 0, same, other), jnp.where(core == 0, other, same)]

    g4 = jnp.stack(
        [frac[...] * pair[f // 2][(f % 2) * ROWS : (f % 2 + 1) * ROWS] for f in range(FIELDS)],
        axis=0,
    )
    ends = [pair[f // 2][2 * ROWS + 2 * (f % 2) : 2 * ROWS + 2 * (f % 2) + 2] for f in range(FIELDS)]
    frac_above = jnp.where(first, 0.0, hr_up[LEV, 1:2, :])
    frac_below = jnp.where(last, 0.0, hr_dn[LEV, 0:1, :])
    above = jnp.stack([frac_above * x[0:1] for x in ends], axis=0)
    below = jnp.stack([frac_below * x[1:2] for x in ends], axis=0)
    lap = laplacian(g4, above, below)
    for i in range(GROUPS):
        high, low = split(
            jnp.concatenate(
                [x[:, 8 * i : 8 * i + 8].reshape(8 * FIELDS, COLS) for x in (g4, lap)], axis=0
            )
        )
        forced[i] = jnp.concatenate([high, low, high], axis=0)

    for copy in (*flux_whole, water_whole):
        copy.wait_send()


def finish(base2, kab, forced, river, out_h, river_h, out, sems):
    river_copy = pltpu.make_async_copy(river, river_h.at[0], sems.at[GROUPS])
    river_copy.start()
    copies = []
    for i in range(0, GROUPS, 2):
        delta = mm(kab[...], jnp.concatenate([forced[i], forced[i + 1]], axis=1))
        for j in range(2):
            part = delta[:, COLS * j : COLS * (j + 1)].reshape(PAD, 8, COLS)
            out[i + j] = base2[i + j] + part
            copies.append(
                pltpu.make_async_copy(
                    out.at[i + j, pl.ds(0, LEV)],
                    out_h.at[0, :, pl.ds(8 * (i + j), 8)],
                    sems.at[i + j],
                )
            )
            copies[-1].start()
    for copy in (*copies, river_copy):
        copy.wait()


def shards(
    state, frac, diff, ops, weight, fo, fr, fb, ro, rr, rb, store,
):
    ops = jnp.transpose(ops, (1, 0, 2))
    fo, ro = fo.reshape(1, ROWS), ro.reshape(1, ROWS)
    args = (state, frac, diff, ops, weight, fo, fr, fb, ro, rr, rb, store)
    args = [pltpu.with_memory_space_constraint(x, pltpu.HBM) for x in args]
    vmem = pltpu.VMEM
    far = pl.BlockSpec(memory_space=pltpu.HBM)
    near = pl.BlockSpec(memory_space=vmem)
    dma = pltpu.SemaphoreType.DMA
    i32 = jnp.int32
    inner = pl.pallas_call(
        kernel,
        out_shape=(
            vmem((GROUPS, PAD, 8, COLS), F32),
            vmem((PAD * 8, 3 * 16 * FIELDS), BF16),
            vmem((GROUPS, 3 * 16 * FIELDS, COLS), BF16),
            vmem((ROWS, COLS), F32),
        ),
        in_specs=[far] * 12,
        out_specs=(near,) * 4,
        scratch_shapes=[
            vmem((GROUPS + 2, PAD, 8, COLS), F32),
            vmem((ROWS, COLS), F32),
            vmem((1, LEV), F32),
            vmem((LEV, 1, LEV), F32),
            vmem((NW, COLS, COLS), F32),
            vmem((1, ROWS), i32),
            vmem((1, ROWS), i32),
            vmem((1, ROWS), i32),
            vmem((1, ROWS), i32),
            vmem((1, ROWS), i32),
            vmem((1, ROWS), i32),
            vmem((ROWS, COLS), F32),
            dma((15,)),
            vmem((PAD, 2, COLS), F32),
            vmem((PAD, 2, COLS), F32),
            vmem((PAD, 2, COLS), F32),
            vmem((PAD, 2, COLS), F32),
            dma((2,)),
            dma((2,)),
            vmem((FIELDS, ROWS, COLS), F32),
            vmem((1, COLS), F32),
            vmem((2, 1, COLS), F32),
            dma((2 + 2 * NC,)),
            dma((2 + 2 * NC,)),
            vmem((SLOTS, SLOT, COLS), F32),
            vmem((SLOTS, 2, COLS), F32),
            dma(()),
            dma(()),
            dma((len(PIECES) + 1, SLOTS)),
            vmem((MAIN + EDGE, COLS), F32),
            vmem((2, EDGE, COLS), F32),
            vmem((GROUP, BLOCK, COLS), F32),
            vmem((GROUP, BLOCK, COLS), F32),
            vmem((GROUP, ROWS, COLS), F32),
            vmem((GROUP, ROWS, COLS), F32),
            dma((3,)),
            dma((3,)),
            vmem((PAD * 8, COLS), F32),
            vmem((PAD * 8, PAD * 8), BF16),
            vmem((PAD * 8, PAD * 8), BF16),
            vmem((GROUPS + 2, PAD, 8, COLS), F32),
        ],
        compiler_params=pltpu.CompilerParams(
            collective_id=0, has_side_effects=True, vmem_limit_bytes=32 * 1024 * 1024
        ),
        name="coupling",
    )(*args)
    inner = [pltpu.with_memory_space_constraint(x, vmem) for x in inner]
    return pl.pallas_call(
        finish,
        out_shape=(
            pltpu.HBM((1, LEV, ROWS, COLS), F32),
            pltpu.HBM((1, ROWS, COLS), F32),
        ),
        in_specs=[near] * 4,
        out_specs=(far, far),
        scratch_shapes=[vmem((GROUPS, PAD, 8, COLS), F32), dma((GROUPS + 1,))],
        compiler_params=pltpu.CompilerParams(vmem_limit_bytes=16 * 1024 * 1024),
        name="finish",
    )(*inner)


def solution(mesh):
    in_specs = (
        P("sec", None, "dom", None),
        P("sec", "dom", None),
        P("sec", None),
        P("sec", None, None),
        P("sec", "dom", None, None),
        P("sec", "dom", None),
        P("sec", "dom"),
        P("sec", "dom"),
        P("sec", "dom", None),
        P("sec", "dom"),
        P("sec", "dom"),
        P("sec", "dom", None),
    )
    out_specs = (P("sec", None, "dom", None), P("sec", "dom", None))
    return jax.shard_map(shards, mesh=mesh, in_specs=in_specs, out_specs=out_specs, check_vma=False)
```

```python
import jax
import jax.numpy as jnp
from jax import lax
from jax.experimental import pallas as pl
from jax.experimental.pallas import tpu as pltpu
from jax.sharding import PartitionSpec as P

MESH = pl.DeviceIdType.MESH
F32 = jnp.float32
BF16 = jnp.bfloat16

LEV = 30
PAD = 32
COLS = 128
ROWS = 32
FIELDS = 4
NW = 8
NY, NZ, NC = 4, 16, 2
N_DOM = NY * NZ * NC
GROUP = NY * NC
HALF = NZ // 2
SLOTS = NZ
GROUPS = ROWS // 8
MAIN = GROUP * ROWS
EDGE = GROUP * 2
WATER_LABEL = ROWS
FLUX = WATER_LABEL
SLOT = FLUX + 2 * NC * ROWS
WATER, FLUX_PIECES = 0, (1, 2, 3, 4)
PIECES = (
    (0, FLUX),
    *[(FLUX + n * ROWS, ROWS) for n in range(2 * NC)],
)
FLUX_LABEL, WATER_NAMES = len(PIECES), len(PIECES) + 1
BLOCK = 2 * ROWS + 8


def tree(jumps):
    levels, reached = {}, 0
    for level, jump in enumerate(jumps, 1):
        levels[level] = [(reached, reached + i) for i in range(jump, 0, -1)]
        reached += jump
    return levels


WATER_TREES = tree((2, 1, 2, 1, 2)), tree((1, 2, 1, 2, 1))
FLUX_TREES = tree((2, 2, 2, 2)), tree((1, 2, 2, 2))
LEVELS = len(FLUX_TREES[0])


def split(x):
    high = x.astype(BF16)
    return high, (x - high.astype(F32)).astype(BF16)


def mm(a, b):
    return jnp.dot(a, b, preferred_element_type=F32)


def mm3(a, b):
    (ah, al), (bh, bl) = a, b
    return mm(ah, bh) + (mm(ah, bl) + mm(al, bh))


def iota(shape, dim):
    return lax.broadcasted_iota(jnp.int32, shape, dim)


def neighbours_in_columns(x):
    axis = x.ndim - 1
    return pltpu.roll(x, 1, axis) + pltpu.roll(x, COLS - 1, axis)


def laplacian(x, above, below):
    row, count = iota(x.shape, 1), x.shape[1]
    down = jnp.where(row == 0, above, pltpu.roll(x, 1, 1))
    up = jnp.where(row == count - 1, below, pltpu.roll(x, count - 1, 1))
    return down + up + neighbours_in_columns(x) - 4.0 * x


def kernel(
    state_h, frac_h, diff_h, ops_h, weight_h, fo_h, fr_h, fb_h, ro_h, rr_h, rb_h, store_h,
    base2, kab, forced, river,
    st, frac, diff, ops, weight, fo, fr, fb, ro, rr, rb, store,
    local_sem,
    hs_up, hs_dn, hr_up, hr_dn, halo_ssem, halo_rsem,
    terms, label_out, label_in, part_ssem, part_rsem,
    ring, names_in, water_names, ring_ssem, names_ssem, water_ssem, ring_rsem, row_of, ends_acc,
    flux_send, flux_recv, run_send, run_recv, rs_ssem, rs_rsem,
    dcol, kron_h, kron_l, base1,
):
    sec = lax.axis_index("sec")
    me = lax.axis_index("dom")
    core = me & (NC - 1)
    z = (me >> 1) & (NZ - 1)
    y = me >> 5

    def dom_of(yy, zz, cc):
        return (yy * NZ + zz) * NC + cc

    def along(distance):
        return (sec, dom_of(y, (z + NZ + distance) & (NZ - 1), core))

    partners = [(sec ^ 2, me), (sec ^ 2, me ^ 1)]
    after = (sec, (me + 1) & (N_DOM - 1))
    before = (sec, (me + N_DOM - 1) & (N_DOM - 1))

    def member(b):
        return (sec, dom_of((y + b // NC) & (NY - 1), z, core ^ (b % NC)))

    barrier = pltpu.get_barrier_semaphore()
    peers = [*partners, *[along(d) for d in (1, -1, 2, -2)], after, before]
    peers += [member(b) for b in range(1, GROUP)]
    for peer in peers:
        pl.semaphore_signal(barrier, inc=1, device_id=peer, device_id_type=MESH)

    pairs = [(weight_h.at[0], weight)]
    pairs += [
        (state_h.at[0, :, pl.ds(8 * i, 8)], st.at[1 + i, pl.ds(0, LEV)]) for i in range(GROUPS)
    ]
    pairs += [
        (fb_h, fb), (rb_h, rb), (fo_h, fo), (fr_h, fr), (ro_h, ro), (rr_h, rr),
        (frac_h.at[0], frac), (ops_h, ops), (diff_h, diff), (store_h.at[0], store),
    ]
    loads = [pltpu.make_async_copy(a, b, local_sem.at[i]) for i, (a, b) in enumerate(pairs)]
    for copy in loads:
        copy.start()

    for copy in loads[5:11]:
        copy.wait()

    def label_of(owner, row):
        eye = iota((ROWS, ROWS), 0) == iota((ROWS, ROWS), 1)
        target = (owner[...] * ROWS + row[...]).astype(F32)
        rows = jnp.broadcast_to(target, (ROWS, ROWS))
        column = jnp.sum(jnp.where(eye, rows, 0.0), axis=1, keepdims=True)
        wide = jnp.broadcast_to(column, (ROWS, COLS))
        place = iota((ROWS, COLS), 0) == (iota((ROWS, COLS), 1) & (ROWS - 1))
        return jnp.sum(jnp.where(place, wide, 0.0), axis=0, keepdims=True)

    label_out[...] = label_of(fo, fr)
    water_names[0] = label_of(ro, rr)

    tall = FIELDS * ROWS + ROWS
    spot = (iota((tall, ROWS), 0) & (ROWS - 1)) == iota((tall, ROWS), 1)
    blocks = jnp.where(
        iota((tall, ROWS), 0) < FIELDS * ROWS,
        jnp.broadcast_to(fb[...].astype(F32), (tall, ROWS)),
        jnp.broadcast_to(rb[...].astype(F32), (tall, ROWS)),
    )
    block = jnp.sum(jnp.where(spot, blocks, 0.0), axis=1, keepdims=True)
    block = jnp.broadcast_to(jnp.concatenate([block, block], axis=0), (2 * tall, COLS))
    for copy in loads[1:5]:
        copy.wait()
    surface = jnp.concatenate(
        [st[1 + i, f] for f in (*range(FIELDS), 0) for i in range(GROUPS)], axis=0
    )
    high = surface.astype(BF16).astype(F32)
    both = jnp.concatenate([high, surface - high], axis=0)
    lhs = jnp.concatenate(
        [jnp.where(block == float(w), both, 0.0).astype(BF16) for w in range(NW)], axis=1
    )
    loads[0].wait()
    rhs = jnp.concatenate(split(weight[...].reshape(NW * COLS, COLS)), axis=1)
    total = mm(lhs, rhs)
    result = total[:tall, :COLS] + (total[:tall, COLS:] + total[tall:, :COLS])
    terms[...] = result[: FIELDS * ROWS].reshape(FIELDS, ROWS, COLS)
    ring[0, :WATER_LABEL, :] = result[FIELDS * ROWS :]

    pl.semaphore_wait(barrier, len(peers))

    def remote(src, dst, ssem, rsem, device):
        return pltpu.make_async_remote_copy(
            src_ref=src, dst_ref=dst, send_sem=ssem, recv_sem=rsem,
            device_id=device, device_id_type=MESH,
        )

    def slot_of(way, distance):
        return 0 if distance == 0 else min(2 * distance - (way > 0), SLOTS - 1)

    def piece(c, slot):
        if c == WATER_NAMES:
            return water_names.at[slot]
        return names_in.at[slot] if c == FLUX_LABEL else ring.at[slot, pl.ds(*PIECES[c])]

    def hop(c, way, start, end):
        slot = slot_of(way, end)
        return remote(
            piece(c, slot_of(way, start)), piece(c, slot),
            {FLUX_LABEL: names_ssem, WATER_NAMES: water_ssem}.get(c, ring_ssem), ring_rsem.at[c, slot],
            along(way * (end - start)),
        )

    arrivals, departures = {}, {}
    for c in range(len(PIECES) + 2):
        for way in (1, -1):
            trees = WATER_TREES if c in (WATER, WATER_NAMES) else FLUX_TREES
            levels = trees[(c % 2 == 0) != (way > 0)]
            for level, edges in levels.items():
                copies = [hop(c, way, *edge) for edge in edges]
                departures[c, way, level] = (slot_of(way, edges[0][0]), copies)
                for copy, (_, end) in zip(copies, edges):
                    arrivals[c, slot_of(way, end)] = copy

    def arrive(c, slots):
        for slot in slots:
            if (c, slot) in arrivals:
                arrivals.pop((c, slot)).wait_recv()

    def depart(c, level):
        for way in (1, -1):
            if (c, way, level) in departures:
                slot, copies = departures.pop((c, way, level))
                arrive(c, [slot])
                for copy in copies:
                    copy.start()

    label_swap = [
        remote(label_out, label_in.at[i], part_ssem.at[i], part_rsem.at[i], to)
        for i, to in enumerate(partners)
    ]
    swap = []
    for f in range(2):
        for i in range(NC):
            n = NC * f + i
            swap.append(
                remote(
                    terms.at[2 * (core ^ i) + f], ring.at[0, pl.ds(FLUX + n * ROWS, ROWS)],
                    part_ssem.at[2 + n], part_rsem.at[2 + n], partners[i],
                )
            )
    for copy in (*label_swap, *swap):
        copy.start()

    depart(WATER_NAMES, 1)
    depart(WATER, 1)

    loads[11].wait()
    hs_up[0:LEV] = st[1, 0:LEV, 0:2, :]
    hs_dn[0:LEV] = st[GROUPS, 0:LEV, 6:8, :]
    hs_up[LEV] = frac[0:2, :]
    hs_dn[LEV] = frac[ROWS - 2 : ROWS, :]
    hs_up[LEV + 1] = jnp.zeros((2, COLS), F32)
    hs_dn[LEV + 1] = jnp.zeros((2, COLS), F32)
    for i in range(GROUPS):
        st[1 + i, LEV:PAD] = jnp.zeros((PAD - LEV, 8, COLS), F32)
    halo = [
        remote(hs_dn, hr_up, halo_ssem.at[0], halo_rsem.at[0], after),
        remote(hs_up, hr_dn, halo_ssem.at[1], halo_rsem.at[1], before),
    ]
    for copy in halo:
        copy.start()


    tall8 = PAD * 8
    for copy in loads[12:14]:
        copy.wait()
    pick = ((iota((tall8, LEV), 0) >> 3) == iota((tall8, LEV), 1)).astype(F32)
    pick_t = ((iota((LEV, tall8), 1) >> 3) == iota((LEV, tall8), 0)).astype(BF16)
    column = jnp.sum(pick * jnp.broadcast_to(diff[...], (tall8, LEV)), axis=1, keepdims=True)
    dcol[...] = jnp.broadcast_to(column, (tall8, COLS))
    op = ops[:, 0, :]
    op_h, op_l = split(op)
    op_r = (op - op_h.astype(F32) - op_l.astype(F32)).astype(BF16)
    pick = pick.astype(BF16)
    spread = mm(mm(pick, op_h).astype(BF16), pick_t) + (
        mm(mm(pick, op_l).astype(BF16), pick_t) + mm(mm(pick, op_r).astype(BF16), pick_t)
    )
    same8 = (iota((tall8, tall8), 0) & 7) == (iota((tall8, tall8), 1) & 7)
    kh, kl = split(jnp.where(same8, spread, 0.0))
    kron_h[...] = kh
    kron_l[...] = kl

    def block_start(b):
        return dom_of((y + (b >> 1)) & (NY - 1), z, core ^ (b & 1)) * ROWS

    i = iota((MAIN, COLS), 0)
    row_of[:MAIN] = (block_start(i >> 5) + (i & (ROWS - 1))).astype(F32)
    i = iota((EDGE, COLS), 0)
    row_of[MAIN:] = (block_start(i >> 1) + jnp.where((i & 1) == 0, -1, ROWS)).astype(F32)
    flux_send[:, 2 * ROWS + 4 :, :] = jnp.zeros((GROUP, 4, COLS), F32)

    def kab_work():
        k4 = kron_h[:, : 8 * FIELDS].astype(F32) + kron_l[:, : 8 * FIELDS].astype(F32)
        eye = (iota(k4.shape, 0) == iota(k4.shape, 1)).astype(F32)
        q = jnp.concatenate([k4 + eye, dcol[:, : 8 * FIELDS] * k4], axis=1)
        kh, kl = split(mm3((kron_h[...], kron_l[...]), split(q)))
        kab[...] = jnp.concatenate([kh, kh, kl], axis=1)

    first = me == 0
    last = me == N_DOM - 1

    def apply(*groups):
        u = jnp.concatenate([u.reshape(PAD * 8, COLS) for u in groups], axis=1)
        out = mm3((kron_h[...], kron_l[...]), split(u))
        return [
            out[:, COLS * i : COLS * (i + 1)].reshape(PAD, 8, COLS) for i in range(len(groups))
        ]

    def diffused(i, source):
        x = source[i]
        lap = laplacian(x, source[i - 1, :, 7:8], source[i + 1, :, 0:1])
        return x + dcol[...].reshape(PAD, 8, COLS) * lap

    def step_one(i, j):
        base1[i], base1[j] = apply(diffused(i, st), diffused(j, st))

    def step_two(i, j):
        base2[i - 1], base2[j - 1] = apply(diffused(i, base1), diffused(j, base1))

    def step_one_ends():
        d = dcol[...].reshape(PAD, 8, COLS)
        spot = iota((PAD, 8, COLS), 1)
        above, below = st[0], st[GROUPS + 1]
        x = jnp.where(spot == 7, above[:, 7:8], below[:, 0:1])
        outer = jnp.where(spot == 7, above[:, 6:7], below[:, 1:2])
        inner = jnp.where(spot == 7, st[1, :, 0:1], st[GROUPS, :, 7:8])
        u = x + d * (outer + inner + neighbours_in_columns(x) - 4.0 * x)
        gone = ((spot == 7) & first) | ((spot < 7) & last)
        (ends,) = apply(jnp.where(gone, 0.0, u))
        base1[0] = ends
        base1[GROUPS + 1] = ends

    depart(WATER_NAMES, 2)
    depart(WATER, 2)
    step_one(2, 3)
    for i, copy in enumerate(label_swap):
        copy.wait_recv()
        names_in[0, i : i + 1, :] = label_in[i]
    depart(FLUX_LABEL, 1)
    for c in FLUX_PIECES:
        swap[c - 1].wait_recv()
        depart(c, 1)
    depart(WATER_NAMES, 3)
    depart(WATER, 3)

    def joined(rows):
        lane = iota((1, COLS), 1) >> 5
        names = rows[0]
        for i in range(1, 4):
            names = jnp.where(lane == i, rows[i], names)
        return names

    def one_hot(rows, names):
        return (rows == jnp.broadcast_to(names, rows.shape)).astype(F32).astype(BF16)

    selected = {}

    def select_flux(j):
        if j not in selected:
            selected[j] = make_selection(j)
        return selected[j]

    def make_selection(j):
        arrive(FLUX_LABEL, (2 * j, 2 * j + 1))
        rows = []
        for i in range(4):
            rows.append(names_in[2 * j + i // 2, i % 2 : i % 2 + 1, :])
        return one_hot(row_of[...], joined(rows))

    def rows_of(f, slots):
        start = FLUX + f * NC * ROWS
        for c in FLUX_PIECES[NC * f : NC * (f + 1)]:
            arrive(c, slots)
        return jnp.concatenate([ring[n, start : start + NC * ROWS, :] for n in slots], axis=0)

    def place_flux(first_slot, last_slot, fields, fresh):
        sel = [select_flux(j) for j in range(first_slot // 2, last_slot // 2)]
        data = [rows_of(f, range(first_slot, last_slot)) for f in fields]
        high, low = split(jnp.concatenate(data, axis=1))
        part = mm(jnp.concatenate([*sel, *sel], axis=1), jnp.concatenate([high, low], axis=0))
        for i, f in enumerate(fields):
            one = part[:, i * COLS : (i + 1) * COLS]
            rows = slice(f * ROWS, (f + 1) * ROWS)
            main = one[:MAIN].reshape(GROUP, ROWS, COLS)
            flux_send[:, rows, :] = main if fresh else flux_send[:, rows, :] + main
            ends_acc[f] = one[MAIN:] if fresh else ends_acc[f] + one[MAIN:]

    def place_water():
        arrive(WATER_NAMES, range(SLOTS))
        arrive(WATER, range(SLOTS))
        rows = [ring[slot, :WATER_LABEL, :] for slot in range(SLOTS)]
        high, low = split(jnp.concatenate(rows, axis=0))
        labels = [water_names[slot] for slot in range(SLOTS)]
        sel = [
            one_hot(row_of[:MAIN], joined(labels[4 * g : 4 * g + 4])) for g in range(SLOTS // 4)
        ]
        part = mm(jnp.concatenate([*sel, *sel], axis=1), jnp.concatenate([high, low], axis=0))
        run_send[...] = part.reshape(GROUP, ROWS, COLS)
        for copy in water_scatter:
            copy.start()

    order = [4, 5, 2, 3, 6, 7, 1]

    def scatter_copies(src, dst, c, rows):
        return [
            remote(src.at[b, rows], dst.at[b, rows], rs_ssem.at[c], rs_rsem.at[c], member(b))
            for b in order
        ]

    def whole(src, dst, c, rows):
        others = pl.ds(1, GROUP - 1)
        return remote(
            src.at[others, rows], dst.at[others, rows], rs_ssem.at[c], rs_rsem.at[c], member(1)
        )

    kinds = [
        (run_send, run_recv, 0, pl.ds(0, ROWS)),
        (flux_send, flux_recv, 1, pl.ds(0, ROWS)),
        (flux_send, flux_recv, 2, pl.ds(ROWS, BLOCK - ROWS)),
    ]
    water_scatter, *flux_scatter = [scatter_copies(*kind) for kind in kinds]
    water_whole, *flux_whole = [whole(*kind) for kind in kinds]

    for level in range(2, LEVELS + 1):
        for c in (FLUX_LABEL, *FLUX_PIECES):
            depart(c, level)
        depart(WATER_NAMES, level + 2)
        depart(WATER, level + 2)
        if level == LEVELS:
            place_water()
    place_flux(0, 10, (0, 1), True)
    for f in range(2):
        place_flux(10, SLOTS, (f,), False)
        if f == 1:
            for b in range(GROUP):
                for e in range(2):
                    ends = 2 * ROWS + 2 * e
                    flux_send[b, ends : ends + 2, :] = ends_acc[e, 2 * b : 2 * b + 2]
        for copy in flux_scatter[f]:
            copy.start()

    for copy in halo:
        copy.wait_recv()
    st[0, :, 6:8, :] = jnp.where(first, 0.0, hr_up[...])
    st[GROUPS + 1, :, 0:2, :] = jnp.where(last, 0.0, hr_dn[...])
    step_one(1, 4)
    step_one_ends()
    step_two(1, 2)
    step_two(3, 4)
    kab_work()
    for copy in (*label_swap, *swap, *halo):
        copy.wait_send()
    every = ring.at[pl.ds(1, SLOTS - 1)]
    remote(every, every, ring_ssem, ring_rsem.at[0, 0], along(1)).wait_send()
    every = names_in.at[pl.ds(1, SLOTS - 1)]
    remote(every, every, names_ssem, ring_rsem.at[0, 0], along(1)).wait_send()
    every = water_names.at[pl.ds(1, SLOTS - 1)]
    remote(every, every, water_ssem, ring_rsem.at[0, 0], along(1)).wait_send()

    loads[14].wait()
    water_whole.wait_recv()
    water = run_send[0]
    for b in range(1, GROUP):
        water = water + run_recv[b]
    river[...] = store[...] + water

    for copy in flux_whole:
        copy.wait_recv()

    same, other = flux_send[0], flux_recv[1]
    for b in range(2, GROUP, 2):
        same = same + flux_recv[b]
        other = other + flux_recv[b + 1]
    pair = [jnp.where(core == 0, same, other), jnp.where(core == 0, other, same)]

    g4 = jnp.stack(
        [frac[...] * pair[f // 2][(f % 2) * ROWS : (f % 2 + 1) * ROWS] for f in range(FIELDS)],
        axis=0,
    )
    ends = [pair[f // 2][2 * ROWS + 2 * (f % 2) : 2 * ROWS + 2 * (f % 2) + 2] for f in range(FIELDS)]
    frac_above = jnp.where(first, 0.0, hr_up[LEV, 1:2, :])
    frac_below = jnp.where(last, 0.0, hr_dn[LEV, 0:1, :])
    above = jnp.stack([frac_above * x[0:1] for x in ends], axis=0)
    below = jnp.stack([frac_below * x[1:2] for x in ends], axis=0)
    lap = laplacian(g4, above, below)
    for i in range(GROUPS):
        high, low = split(
            jnp.concatenate(
                [x[:, 8 * i : 8 * i + 8].reshape(8 * FIELDS, COLS) for x in (g4, lap)], axis=0
            )
        )
        forced[i] = jnp.concatenate([high, low, high], axis=0)

    for copy in (*flux_whole, water_whole):
        copy.wait_send()


def finish(base2, kab, forced, river, out_h, river_h, out, sems):
    river_copy = pltpu.make_async_copy(river, river_h.at[0], sems.at[GROUPS])
    river_copy.start()
    copies = []
    for i in range(0, GROUPS, 2):
        delta = mm(kab[...], jnp.concatenate([forced[i], forced[i + 1]], axis=1))
        for j in range(2):
            part = delta[:, COLS * j : COLS * (j + 1)].reshape(PAD, 8, COLS)
            out[i + j] = base2[i + j] + part
            copies.append(
                pltpu.make_async_copy(
                    out.at[i + j, pl.ds(0, LEV)],
                    out_h.at[0, :, pl.ds(8 * (i + j), 8)],
                    sems.at[i + j],
                )
            )
            copies[-1].start()
    for copy in (*copies, river_copy):
        copy.wait()


def shards(
    state, frac, diff, ops, weight, fo, fr, fb, ro, rr, rb, store,
):
    ops = jnp.transpose(ops, (1, 0, 2))
    fo, ro = fo.reshape(1, ROWS), ro.reshape(1, ROWS)
    args = (state, frac, diff, ops, weight, fo, fr, fb, ro, rr, rb, store)
    args = [pltpu.with_memory_space_constraint(x, pltpu.HBM) for x in args]
    vmem = pltpu.VMEM
    far = pl.BlockSpec(memory_space=pltpu.HBM)
    near = pl.BlockSpec(memory_space=vmem)
    dma = pltpu.SemaphoreType.DMA
    i32 = jnp.int32
    inner = pl.pallas_call(
        kernel,
        out_shape=(
            vmem((GROUPS, PAD, 8, COLS), F32),
            vmem((PAD * 8, 3 * 16 * FIELDS), BF16),
            vmem((GROUPS, 3 * 16 * FIELDS, COLS), BF16),
            vmem((ROWS, COLS), F32),
        ),
        in_specs=[far] * 12,
        out_specs=(near,) * 4,
        scratch_shapes=[
            vmem((GROUPS + 2, PAD, 8, COLS), F32),
            vmem((ROWS, COLS), F32),
            vmem((1, LEV), F32),
            vmem((LEV, 1, LEV), F32),
            vmem((NW, COLS, COLS), F32),
            vmem((1, ROWS), i32),
            vmem((1, ROWS), i32),
            vmem((1, ROWS), i32),
            vmem((1, ROWS), i32),
            vmem((1, ROWS), i32),
            vmem((1, ROWS), i32),
            vmem((ROWS, COLS), F32),
            dma((15,)),
            vmem((PAD, 2, COLS), F32),
            vmem((PAD, 2, COLS), F32),
            vmem((PAD, 2, COLS), F32),
            vmem((PAD, 2, COLS), F32),
            dma((2,)),
            dma((2,)),
            vmem((FIELDS, ROWS, COLS), F32),
            vmem((1, COLS), F32),
            vmem((2, 1, COLS), F32),
            dma((2 + 2 * NC,)),
            dma((2 + 2 * NC,)),
            vmem((SLOTS, SLOT, COLS), F32),
            vmem((SLOTS, 2, COLS), F32),
            vmem((SLOTS, 1, COLS), F32),
            dma(()),
            dma(()),
            dma(()),
            dma((len(PIECES) + 2, SLOTS)),
            vmem((MAIN + EDGE, COLS), F32),
            vmem((2, EDGE, COLS), F32),
            vmem((GROUP, BLOCK, COLS), F32),
            vmem((GROUP, BLOCK, COLS), F32),
            vmem((GROUP, ROWS, COLS), F32),
            vmem((GROUP, ROWS, COLS), F32),
            dma((3,)),
            dma((3,)),
            vmem((PAD * 8, COLS), F32),
            vmem((PAD * 8, PAD * 8), BF16),
            vmem((PAD * 8, PAD * 8), BF16),
            vmem((GROUPS + 2, PAD, 8, COLS), F32),
        ],
        compiler_params=pltpu.CompilerParams(
            collective_id=0, has_side_effects=True, vmem_limit_bytes=32 * 1024 * 1024
        ),
        name="coupling",
    )(*args)
    inner = [pltpu.with_memory_space_constraint(x, vmem) for x in inner]
    return pl.pallas_call(
        finish,
        out_shape=(
            pltpu.HBM((1, LEV, ROWS, COLS), F32),
            pltpu.HBM((1, ROWS, COLS), F32),
        ),
        in_specs=[near] * 4,
        out_specs=(far, far),
        scratch_shapes=[vmem((GROUPS, PAD, 8, COLS), F32), dma((GROUPS + 1,))],
        compiler_params=pltpu.CompilerParams(vmem_limit_bytes=16 * 1024 * 1024),
        name="finish",
    )(*inner)


def solution(mesh):
    in_specs = (
        P("sec", None, "dom", None),
        P("sec", "dom", None),
        P("sec", None),
        P("sec", None, None),
        P("sec", "dom", None, None),
        P("sec", "dom", None),
        P("sec", "dom"),
        P("sec", "dom"),
        P("sec", "dom", None),
        P("sec", "dom"),
        P("sec", "dom"),
        P("sec", "dom", None),
    )
    out_specs = (P("sec", None, "dom", None), P("sec", "dom", None))
    return jax.shard_map(shards, mesh=mesh, in_specs=in_specs, out_specs=out_specs, check_vma=False)
```
